32 devices in a mesh: branch: 2 (over y), row: 4 (over z), seq: 4 (over x, core).
Axes of the slice: x: 2, y: 2, z: 4, core: 2. Of those that a mesh axis runs over, the one named last changes fastest.
Arguments:
- alignment_input: bfloat16 [256, 32, 256], P('seq', 'row'), may hold values from -6 to 6
- pairwise_input: bfloat16 [128, 32, 32], P('seq', 'row'), may hold values from -30 to 30
- alignment_gain: float32 [256], replicated, may hold values from 0.25 to 1.75
- product_gain: float32 [256], replicated, may hold values from 0.25 to 1.75
- attention_weight: bfloat16 [256, 4, 256], replicated, may hold values from -0.375 to 0.375
- mixing_weight: bfloat16 [256, 256], replicated, may hold values from -0.375 to 0.375
- outer_input_weight: bfloat16 [256, 2, 32], replicated, may hold values from -0.375 to 0.375
- outer_output_weight: bfloat16 [32, 32, 128], replicated, may hold values from -3 to 3
- bias_matrix: bfloat16 [128, 8], replicated, may hold values from -6 to 6
- pairwise_gain: float32 [128], replicated, may hold values from 0.25 to 1.75
- triangle_input_weight: bfloat16 [4, 128, 128], P(None, 'seq'), may hold values from -0.5 to 0.5
- triangle_gate_weight: bfloat16 [128, 128], P('seq'), may hold values from -0.5 to 0.5
- triangle_gain: float32 [128], P('seq'), may hold values from 0.25 to 1.75
- triangle_output_weight: bfloat16 [128, 128], P(None, 'seq'), may hold values from -0.5 to 0.5
- transition_gain: float32 [128], replicated, may hold values from 0.25 to 1.75
- transition_up_weight: bfloat16 [512, 128], P('seq'), may hold values from -0.5 to 0.5
- transition_down_weight: bfloat16 [128, 512], P(None, 'seq'), may hold values from -0.25 to 0.25
Outputs:
- alignment_output: bfloat16 [256, 32, 256], P('seq', 'row', 'branch')
- pairwise_output: bfloat16 [128, 32, 32], P('seq', 'row', 'branch')
The draws below stay inside these ranges and needn't reach their ends.
All inputs are finite; a program needn't handle non-finite values.
Results may differ from the reference program's by a relative error of at most 0.011.
Values may be sent and summed in bfloat16 or wider, within the bound.
No kernel may reach another device: no remote copies, remote signals or barrier semaphores. Data moves between devices by JAX's collectives and lax.ppermute only.
A program may use at most 128 MiB of HBM per device.

```python
import jax
import jax.numpy as jnp
from jax import lax

ALIGNMENT_WIDTH = 256
PAIR_WIDTH = 128
ATTENTION_HEADS = 8
HEAD_CHANNELS = 32
PRODUCT_WIDTH = 32
TRI_WIDTH = 128
TRANS_WIDTH = 512
SEQUENCE_COUNT = 256
RESIDUE_COUNT = 32


def bias_values(key):
    inner = jax.random.fold_in(key, 7301)
    draws = jax.random.normal(inner, (PAIR_WIDTH, ATTENTION_HEADS), jnp.float32)
    return jnp.clip(draws * PAIR_WIDTH ** (-0.5), -6.0, 6.0)


def draw_bias_matrix(key, part):
    return bias_values(key).astype(jnp.bfloat16)


def draw_pairwise_input(key, part):
    keys_all = jax.random.split(jax.random.fold_in(key, 4409), 1)
    noise = jax.random.normal(keys_all[0], (PAIR_WIDTH, RESIDUE_COUNT, RESIDUE_COUNT), jnp.float32)
    field = jnp.clip(noise, -6.0, 6.0)
    return field.astype(jnp.bfloat16)


def levels(stream_key, dims, cuts, smallest, largest):
    loudness, own = 1.0, jax.random.fold_in(stream_key, 6)
    for dim, parts in cuts:
        steps = jnp.exp(jax.random.uniform(jax.random.fold_in(own, dim), (parts,), jnp.float32, smallest / len(cuts), largest / len(cuts)))
        loudness = loudness * jnp.repeat(steps, dims[dim] // parts).reshape([-1 if axis == dim else 1 for axis in range(len(dims))])
    return loudness


def gaussian(rng, extent, width, limit, cuts=(), held_as=jnp.bfloat16):
    values = jax.random.normal(rng, extent, jnp.float32) * width
    if len(cuts) > 0:
        values = levels(rng, extent, cuts, -0.22, 0.18) * values
    return jnp.clip(values, min=-limit, max=limit).astype(held_as)


def setup_inputs(seed: int = 0) -> dict:
    seeds = jax.random.split(jax.random.key(seed), 18)
    return {
        "alignment_input": gaussian(seeds[0], (SEQUENCE_COUNT, RESIDUE_COUNT, ALIGNMENT_WIDTH), 1.0, 6.0, ((0, 4), (1, 4))),
        "pairwise_input": draw_pairwise_input(jax.random.fold_in(seeds[17], 71), 0),
        "alignment_gain": jnp.clip(1.0 + 0.15 * jax.random.normal(seeds[2], (ALIGNMENT_WIDTH,), jnp.float32), 0.25, 1.75),
        "product_gain": jnp.clip(1.0 + 0.15 * jax.random.normal(seeds[3], (ALIGNMENT_WIDTH,), jnp.float32), 0.25, 1.75),
        "attention_weight": gaussian(seeds[4], (ALIGNMENT_WIDTH, 4, ATTENTION_HEADS * HEAD_CHANNELS), ALIGNMENT_WIDTH ** -0.5, 0.375),
        "mixing_weight": gaussian(seeds[5], (ATTENTION_HEADS * HEAD_CHANNELS, ALIGNMENT_WIDTH), (ATTENTION_HEADS * HEAD_CHANNELS) ** -0.5, 0.375),
        "outer_input_weight": gaussian(seeds[6], (ALIGNMENT_WIDTH, 2, PRODUCT_WIDTH), ALIGNMENT_WIDTH ** -0.5, 0.375),
        "outer_output_weight": gaussian(seeds[7], (PRODUCT_WIDTH, PRODUCT_WIDTH, PAIR_WIDTH), (max(1, PRODUCT_WIDTH * PRODUCT_WIDTH // SEQUENCE_COUNT)) ** -0.5, 3.0),
        "bias_matrix": draw_bias_matrix(jax.random.fold_in(seeds[17], 71), 0),
        "pairwise_gain": jnp.clip(1.0 + 0.15 * jax.random.normal(seeds[9], (PAIR_WIDTH,), jnp.float32), 0.25, 1.75),
        "triangle_input_weight": gaussian(seeds[10], (4, TRI_WIDTH, PAIR_WIDTH), PAIR_WIDTH ** -0.5, 0.5, ((1, 4),)),
        "triangle_gate_weight": gaussian(seeds[11], (PAIR_WIDTH, PAIR_WIDTH), PAIR_WIDTH ** -0.5, 0.5, ((0, 4),)),
        "triangle_gain": jnp.clip(1.0 + 0.15 * jax.random.normal(seeds[12], (TRI_WIDTH,), jnp.float32), 0.25, 1.75),
        "triangle_output_weight": gaussian(seeds[13], (PAIR_WIDTH, TRI_WIDTH), TRI_WIDTH ** -0.5, 0.5, ((1, 4),)),
        "transition_gain": jnp.clip(1.0 + 0.15 * jax.random.normal(seeds[14], (PAIR_WIDTH,), jnp.float32), 0.25, 1.75),
        "transition_up_weight": gaussian(seeds[15], (TRANS_WIDTH, PAIR_WIDTH), PAIR_WIDTH ** -0.5, 0.5, ((0, 4),)),
        "transition_down_weight": gaussian(seeds[16], (PAIR_WIDTH, TRANS_WIDTH), TRANS_WIDTH ** -0.5, 0.25, ((1, 4),)),
    }


EPSILON = 1e-05

def layer_normalize(values, axis):
    average = lax.optimization_barrier(jnp.mean(values, axis=axis, keepdims=True))
    centred = values - average
    spread = lax.optimization_barrier(jnp.mean(centred * centred, axis=axis, keepdims=True))
    return centred * lax.rsqrt(spread + EPSILON)

def rounded(values):
    return lax.optimization_barrier(values.astype(jnp.bfloat16))

def reference(alignment_input, pairwise_input, alignment_gain, product_gain, attention_weight, mixing_weight, outer_input_weight, outer_output_weight, bias_matrix, pairwise_gain, triangle_input_weight, triangle_gate_weight, triangle_gain, triangle_output_weight, transition_gain, transition_up_weight, transition_down_weight):
    latent_heads = ATTENTION_HEADS * HEAD_CHANNELS
    alignment_single = alignment_input.astype(jnp.float32)
    alignment_module = layer_normalize(alignment_single, 2)
    normalized_values = (alignment_module * alignment_gain).astype(jnp.bfloat16)
    outer_normalized = (alignment_module * product_gain).astype(jnp.bfloat16)
    flattened_rows = normalized_values.reshape(-1, ALIGNMENT_WIDTH)
    outer_input_rows = outer_normalized.reshape(-1, ALIGNMENT_WIDTH)
    projected_values = jnp.dot(flattened_rows, attention_weight.reshape(ALIGNMENT_WIDTH, 4 * latent_heads), preferred_element_type=jnp.float32)
    projected_values = projected_values.reshape(SEQUENCE_COUNT, RESIDUE_COUNT, 4, ATTENTION_HEADS, HEAD_CHANNELS)
    query = rounded(projected_values[:, :, 0] * HEAD_CHANNELS ** (-0.5))
    keys = rounded(projected_values[:, :, 1])
    values = rounded(projected_values[:, :, 2])
    gate = rounded(jax.nn.sigmoid(projected_values[:, :, 3]))
    outer_products = jnp.dot(outer_input_rows, outer_input_weight.reshape(ALIGNMENT_WIDTH, 2 * PRODUCT_WIDTH), preferred_element_type=jnp.float32)
    outer_products = outer_products.astype(jnp.bfloat16).reshape(SEQUENCE_COUNT, RESIDUE_COUNT, 2, PRODUCT_WIDTH)
    left = outer_products[:, :, 0]
    right = outer_products[:, :, 1]
    pair_float = pairwise_input.astype(jnp.float32)
    unit = layer_normalize(pair_float, 0)
    plain = unit.astype(jnp.bfloat16).reshape(PAIR_WIDTH, -1)
    pair_bias = rounded(jnp.dot(bias_matrix.T, plain, preferred_element_type=jnp.float32)).astype(jnp.float32)
    pair_bias = pair_bias.reshape(ATTENTION_HEADS, RESIDUE_COUNT, RESIDUE_COUNT)

    def attend_one(operands):
        query_one, keys_one, values_one, gate_one = operands
        scores = jnp.einsum('ihd,jhd->hij', query_one.astype(jnp.float32), keys_one.astype(jnp.float32), precision=lax.Precision.HIGHEST) + pair_bias
        highest = lax.optimization_barrier(jnp.max(scores, axis=2, keepdims=True))
        weights = jnp.exp(scores - highest)
        totals = lax.optimization_barrier(jnp.sum(weights, axis=2))
        weighted = jnp.einsum('hij,jhd->ihd', rounded(weights).astype(jnp.float32), values_one.astype(jnp.float32), precision=lax.Precision.HIGHEST)
        attended = weighted / jnp.transpose(totals)[:, :, None]
        return (gate_one.astype(jnp.float32) * attended).astype(jnp.bfloat16)
    mixed_heads = lax.map(attend_one, (query, keys, values, gate))
    alignment_output = alignment_single + jnp.dot(mixed_heads.reshape(-1, latent_heads), mixing_weight, preferred_element_type=jnp.float32).reshape(SEQUENCE_COUNT, RESIDUE_COUNT, ALIGNMENT_WIDTH)
    alignment_output = alignment_output.astype(jnp.bfloat16)
    right_matrix = jnp.transpose(right, (0, 2, 1)).reshape(SEQUENCE_COUNT * PRODUCT_WIDTH, RESIDUE_COUNT)

    def outer_row(left_row):
        spread_row = jnp.einsum('sc,cdo->osd', left_row.astype(jnp.float32), outer_output_weight.astype(jnp.float32), precision=lax.Precision.HIGHEST).astype(jnp.bfloat16)
        return jnp.dot(spread_row.reshape(PAIR_WIDTH, -1), right_matrix, preferred_element_type=jnp.float32)
    outer_rows = lax.map(outer_row, jnp.transpose(left, (1, 0, 2)))
    outer_increment = rounded(jnp.transpose(outer_rows, (1, 0, 2)) * (1.0 / SEQUENCE_COUNT)).astype(jnp.float32)
    tri_input = (unit * pairwise_gain[:, None, None]).astype(jnp.bfloat16)
    tri_flat = tri_input.reshape(PAIR_WIDTH, -1)
    linear = jnp.dot(triangle_input_weight.reshape(4 * TRI_WIDTH, PAIR_WIDTH), tri_flat, preferred_element_type=jnp.float32)
    linear = linear.reshape(4, TRI_WIDTH, RESIDUE_COUNT, RESIDUE_COUNT)
    left_tri = rounded(linear[0] * jax.nn.sigmoid(linear[1])).astype(jnp.float32)
    right_tri = rounded(linear[2] * jax.nn.sigmoid(linear[3])).astype(jnp.float32)
    triangle = rounded(jnp.einsum('cik,cjk->cij', left_tri, right_tri, precision=lax.Precision.HIGHEST)).astype(jnp.float32)
    tri_norm = (layer_normalize(triangle, 0) * triangle_gain[:, None, None]).astype(jnp.bfloat16)
    tri_out = jnp.dot(triangle_output_weight, tri_norm.reshape(TRI_WIDTH, -1), preferred_element_type=jnp.float32)
    tri_gate = jax.nn.sigmoid(jnp.dot(triangle_gate_weight, tri_flat, preferred_element_type=jnp.float32))
    first_update = rounded(pair_float + (tri_gate * tri_out).reshape(PAIR_WIDTH, RESIDUE_COUNT, RESIDUE_COUNT)).astype(jnp.float32)
    trans_norm = (layer_normalize(first_update, 0) * transition_gain[:, None, None]).astype(jnp.bfloat16).reshape(PAIR_WIDTH, -1)
    hidden_units = jax.nn.relu(jnp.dot(transition_up_weight, trans_norm, preferred_element_type=jnp.float32)).astype(jnp.bfloat16)
    pair_following = first_update + jnp.dot(transition_down_weight, hidden_units, preferred_element_type=jnp.float32).reshape(PAIR_WIDTH, RESIDUE_COUNT, RESIDUE_COUNT)
    pair_following = rounded(pair_following).astype(jnp.float32)
    pairwise_output = (pair_following + outer_increment).astype(jnp.bfloat16)
    return (alignment_output, pairwise_output)
```

```python
import functools

import jax
import jax.numpy as jnp
from jax import lax
from jax.experimental import pallas as pl
from jax.experimental.pallas import tpu as pltpu
from jax.sharding import PartitionSpec as P

EPSILON = 1e-05


def shifted(value, axis, by):
    length = lax.axis_size(axis)
    pairs = [(i, i + by) for i in range(length) if 0 <= i + by < length]
    return lax.ppermute(value, axis, pairs)


def from_partner(value, axis, distance):
    return lax.ppermute(value, axis, [(i, i ^ 1 << distance) for i in range(lax.axis_size(axis))])


def layer_normalize(values, axis):
    average = jnp.mean(values, axis=axis, keepdims=True)
    centred = values - average
    spread = jnp.mean(centred * centred, axis=axis, keepdims=True)
    return centred * lax.rsqrt(spread + EPSILON)


def full_channels(values):
    return lax.all_gather(values, "seq", axis=0, tiled=True)


def channel_sum(term, kept_rows):
    return lax.psum_scatter(
        term(jnp.int32(0), kept_rows * lax.axis_size("seq")), "seq", scatter_dimension=0, tiled=True
    )


def shards(
    alignment_input,
    pairwise_input,
    alignment_gain,
    product_gain,
    attention_weight,
    mixing_weight,
    outer_input_weight,
    outer_output_weight,
    bias_matrix,
    pairwise_gain,
    triangle_input_weight,
    triangle_gate_weight,
    triangle_gain,
    triangle_output_weight,
    transition_gain,
    transition_up_weight,
    transition_down_weight,
):
    local_sequences, local_rows, alignment_channels = alignment_input.shape
    chan_local = pairwise_input.shape[0]
    residues = pairwise_input.shape[2]
    pair_width, head_total = bias_matrix.shape
    latent_heads = mixing_weight.shape[0]
    head_size = latent_heads // head_total
    outer_width = outer_input_weight.shape[2]
    tri_local = triangle_input_weight.shape[1]
    trans_local = transition_up_weight.shape[0]
    seq_total = local_sequences * lax.axis_size("seq")
    path_index = lax.axis_index("branch")
    alignment_branch = path_index == 0
    query_shape = (local_sequences, local_rows, latent_heads)
    pair_shape = (chan_local, local_rows, residues)
    full_pair_shape = (pair_width, local_rows, residues)
    key_shape = (local_sequences, 2 * latent_heads, local_rows)
    gathered = full_channels(pairwise_input)

    def alignment_early():
        alignment_module = layer_normalize(alignment_input.astype(jnp.float32), 2)
        normalized_values = (alignment_module * alignment_gain).astype(jnp.bfloat16)
        outer_normalized = (alignment_module * product_gain).astype(jnp.bfloat16)
        flattened_rows = normalized_values.reshape(-1, alignment_channels)
        outer_flattened = outer_normalized.reshape(-1, alignment_channels)
        query = (
            (
                jnp.dot(flattened_rows, attention_weight[:, 0], preferred_element_type=jnp.float32)
                * head_size ** (-0.5)
            )
            .astype(jnp.bfloat16)
            .reshape(query_shape)
        )
        gate = (
            jax.nn.sigmoid(
                jnp.dot(flattened_rows, attention_weight[:, 3], preferred_element_type=jnp.float32)
            )
            .astype(jnp.bfloat16)
            .reshape(query_shape)
        )
        key_values = (
            jnp.einsum(
                "sim,mkc->skci",
                normalized_values,
                attention_weight[:, 1:3],
                preferred_element_type=jnp.float32,
            )
            .astype(jnp.bfloat16)
            .reshape(key_shape)
        )
        left = (
            jnp.dot(outer_flattened, outer_input_weight[:, 0], preferred_element_type=jnp.float32)
            .astype(jnp.bfloat16)
            .reshape(local_sequences, local_rows, outer_width)
        )
        right_cols = jnp.einsum(
            "sim,mc->sci",
            outer_normalized,
            outer_input_weight[:, 1],
            preferred_element_type=jnp.float32,
        ).astype(jnp.bfloat16)
        empty_bias = jnp.zeros((head_total, local_rows, residues), jnp.bfloat16)
        empty_pair = jnp.zeros(full_pair_shape, jnp.bfloat16)
        return (empty_bias, empty_pair, query, key_values, gate, left, right_cols)

    def pair_early():
        unit = layer_normalize(gathered.astype(jnp.float32), 0)
        plain = unit.astype(jnp.bfloat16).reshape(pair_width, -1)
        bias_rows = (
            jnp.einsum("ch,cn->hn", bias_matrix, plain, preferred_element_type=jnp.float32)
            .astype(jnp.bfloat16)
            .reshape(head_total, local_rows, residues)
        )
        tri_input = (unit * pairwise_gain[:, None, None]).astype(jnp.bfloat16)
        empty_query = jnp.zeros(query_shape, jnp.bfloat16)
        empty_keys = jnp.zeros(key_shape, jnp.bfloat16)
        empty_left = jnp.zeros((local_sequences, local_rows, outer_width), jnp.bfloat16)
        empty_right = jnp.zeros((local_sequences, outer_width, local_rows), jnp.bfloat16)
        return (bias_rows, tri_input, empty_query, empty_keys, empty_query, empty_left, empty_right)

    bias_local, tri_input, query, key_values, gate, left, right_cols = lax.cond(
        alignment_branch, alignment_early, pair_early
    )
    bias_recv = shifted(bias_local, "branch", -1)
    query_heads = query.reshape(local_sequences, local_rows, head_total, head_size).transpose(
        0, 2, 1, 3
    )

    def fold_real(running, shard_part):
        highest, totals, weighted = running
        columns = shard_part.shape[2]
        keys_part = shard_part[:, :latent_heads].reshape(
            local_sequences, head_total, head_size, columns
        )
        values_part = shard_part[:, latent_heads:].reshape(
            local_sequences, head_total, head_size, columns
        )
        bias_part = bias_recv.astype(jnp.float32)
        scores = (
            jnp.einsum(
                "shid,shdj->shij", query_heads, keys_part, preferred_element_type=jnp.float32
            )
            + bias_part[None]
        )
        raised = jnp.maximum(highest, jnp.max(scores, axis=3))
        weights = jnp.exp(scores - raised[..., None])
        totals = jnp.sum(weights, axis=3)
        weighted = jnp.einsum(
            "shij,shdj->shid",
            weights.astype(jnp.bfloat16),
            values_part,
            preferred_element_type=jnp.float32,
        )
        return (raised, totals, weighted)

    initial = (
        jnp.full((local_sequences, head_total, local_rows), -1e30, jnp.float32),
        jnp.zeros((local_sequences, head_total, local_rows), jnp.float32),
        jnp.zeros((local_sequences, head_total, local_rows, head_size), jnp.float32),
    )
    shard_part = lax.all_gather(key_values, "row", axis=2, tiled=True)
    highest, totals, weighted = lax.cond(
        alignment_branch, lambda: fold_real(initial, shard_part), lambda: initial
    )
    safe_totals = jnp.where(totals > 0, totals, 1.0)
    attended = (weighted / safe_totals[..., None]).transpose(0, 2, 1, 3).reshape(query_shape)
    mixed_heads = (gate.astype(jnp.float32) * attended).astype(jnp.bfloat16)
    right_full = lax.all_gather(right_cols, "row", axis=2, tiled=True)
    right_matrix = right_full.reshape(local_sequences * outer_width, residues)
    spread = lax.cond(
        alignment_branch,
        lambda: jnp.einsum(
            "sic,cdo->oisd", left, outer_output_weight, preferred_element_type=jnp.float32
        ).astype(jnp.bfloat16),
        lambda: jnp.zeros((pair_width, local_rows, local_sequences, outer_width), jnp.bfloat16),
    )

    def outer_term(amount):
        spread_part = spread.reshape(amount * local_rows, local_sequences * outer_width)
        return jnp.dot(spread_part, right_matrix, preferred_element_type=jnp.float32).reshape(
            amount, local_rows, residues
        )

    tri_flat = tri_input.reshape(pair_width, -1)

    def pair_operands():
        linear = jnp.dot(
            triangle_input_weight.reshape(4 * tri_local, pair_width),
            tri_flat,
            preferred_element_type=jnp.float32,
        )
        linear = linear.reshape(4, tri_local, local_rows, residues)
        left_part = (linear[0] * jax.nn.sigmoid(linear[1])).astype(jnp.bfloat16)
        right_part = (linear[2] * jax.nn.sigmoid(linear[3])).astype(jnp.bfloat16)
        return (left_part, right_part)

    def empty_operands():
        empty = jnp.zeros((tri_local, local_rows, residues), jnp.bfloat16)
        return (empty, empty)

    left_tri, right_tri = lax.cond(alignment_branch, empty_operands, pair_operands)
    tri_shard_part = lax.all_gather(right_tri, "row", axis=1, tiled=True)
    triangle = lax.optimization_barrier(
        lax.cond(
            alignment_branch,
            lambda: jnp.zeros((tri_local, local_rows, tri_shard_part.shape[1]), jnp.float32),
            lambda: jnp.einsum(
                "cik,cjk->cij", left_tri, tri_shard_part, preferred_element_type=jnp.float32
            ),
        ).astype(jnp.bfloat16)
    )
    tri_float = triangle.astype(jnp.float32)
    summed, squared = lax.psum(
        (jnp.sum(tri_float, axis=0), jnp.sum(tri_float * tri_float, axis=0)), "seq"
    )
    tri_total = tri_local * lax.axis_size("seq")
    average = summed / tri_total
    variance = jnp.maximum(squared / tri_total - average * average, 0.0)
    tri_norm = (
        (tri_float - average) * lax.rsqrt(variance + EPSILON) * triangle_gain[:, None, None]
    ).astype(jnp.bfloat16)
    norm_flat = tri_norm.reshape(tri_local, -1)

    def tri_term(amount):
        return jnp.dot(
            triangle_output_weight, norm_flat, preferred_element_type=jnp.float32
        ).reshape(amount, local_rows, residues)

    def first_term(offset, amount):
        return lax.cond(alignment_branch, lambda: outer_term(amount), lambda: tri_term(amount))

    summed_first = channel_sum(first_term, chan_local)
    outer_increment = (summed_first * (1.0 / seq_total)).astype(jnp.bfloat16)
    gate_values = jax.nn.sigmoid(
        jnp.dot(triangle_gate_weight, tri_flat, preferred_element_type=jnp.float32)
    ).reshape(pair_shape)
    first_update = lax.optimization_barrier(
        (pairwise_input.astype(jnp.float32) + gate_values * summed_first).astype(jnp.bfloat16)
    )
    gathered_next = full_channels(first_update)

    def pair_hidden():
        trans_norm = (
            (layer_normalize(gathered_next.astype(jnp.float32), 0) * transition_gain[:, None, None])
            .astype(jnp.bfloat16)
            .reshape(pair_width, -1)
        )
        return jax.nn.relu(
            jnp.dot(transition_up_weight, trans_norm, preferred_element_type=jnp.float32)
        ).astype(jnp.bfloat16)

    hidden_units = lax.cond(
        alignment_branch,
        lambda: jnp.zeros((trans_local, local_rows * residues), jnp.bfloat16),
        pair_hidden,
    )

    def trans_real(amount):
        return jnp.dot(
            transition_down_weight, hidden_units, preferred_element_type=jnp.float32
        ).reshape(amount, local_rows, residues)

    def trans_term(offset, amount):
        return lax.cond(
            alignment_branch,
            lambda: jnp.zeros((amount, local_rows, residues), jnp.float32),
            lambda: trans_real(amount),
        )

    pair_following = (
        first_update.astype(jnp.float32) + channel_sum(trans_term, chan_local)
    ).astype(jnp.bfloat16)
    half_residues = residues // 2
    halved_width = alignment_channels // 2
    outgoing_product = jnp.where(
        alignment_branch,
        outer_increment[:, :, half_residues:],
        pair_following[:, :, :half_residues],
    )
    incoming = from_partner(outgoing_product, "branch", 0)
    local_half = jnp.where(
        alignment_branch,
        outer_increment[:, :, :half_residues],
        pair_following[:, :, half_residues:],
    )
    pairwise_output = (local_half.astype(jnp.float32) + incoming.astype(jnp.float32)).astype(
        jnp.bfloat16
    )
    mixed_received = shifted(mixed_heads, "branch", 1)
    mixed_applied = jnp.where(alignment_branch, mixed_heads, mixed_received)
    mix_columns = lax.dynamic_slice_in_dim(
        mixing_weight, path_index * halved_width, halved_width, 1
    )
    residual_stream = lax.dynamic_slice_in_dim(
        alignment_input, path_index * halved_width, halved_width, 2
    )
    projected_values = jnp.dot(
        mixed_applied.reshape(-1, latent_heads), mix_columns, preferred_element_type=jnp.float32
    )
    alignment_output = (
        residual_stream.astype(jnp.float32)
        + projected_values.reshape(local_sequences, local_rows, halved_width)
    ).astype(jnp.bfloat16)
    return (alignment_output, pairwise_output)


def rounded(values):
    return values.astype(jnp.bfloat16)


def widened(values):
    return values.astype(jnp.float32)


def product(left, right, contract_left=1, contract_right=0):
    return lax.dot_general(
        left,
        right,
        (((contract_left,), (contract_right,)), ((), ())),
        preferred_element_type=jnp.float32,
    )


def group_maximum(values, group):
    tiles = []
    for start in range(0, values.shape[1], 128):
        tile = values[:, start : start + 128]
        lane = lax.broadcasted_iota(jnp.int32, tile.shape, 1)
        step = 1
        while step < group:
            ahead = pltpu.roll(tile, 128 - step, 1)
            behind = pltpu.roll(tile, step, 1)
            tile = jnp.maximum(tile, jnp.where((lane & step) == 0, ahead, behind))
            step *= 2
        tiles.append(tile)
    return jnp.concatenate(tiles, axis=1)


def same_group(rows, columns, group):
    row = lax.broadcasted_iota(jnp.int32, (rows, columns), 0) // group
    column = lax.broadcasted_iota(jnp.int32, (rows, columns), 1) // group
    return row == column


def kernel_call(body, outputs, operands, scratch=(), flops=0):
    vmem = pl.BlockSpec(memory_space=pltpu.VMEM)
    size = sum(a.size * a.dtype.itemsize for a in operands)
    size += sum(o.size * o.dtype.itemsize for o in outputs)
    return pl.pallas_call(
        body,
        out_shape=outputs,
        in_specs=[vmem] * len(operands),
        out_specs=[vmem] * len(outputs),
        scratch_shapes=list(scratch),
        cost_estimate=pl.CostEstimate(flops=flops, bytes_accessed=size, transcendentals=0),
        compiler_params=pltpu.CompilerParams(vmem_limit_bytes=32 * 2**20),
    )(*operands)


def exchange(value, axes, distance):
    members = lax.axis_size(axes)
    return lax.ppermute(value, axes, [(i, i ^ distance) for i in range(members)])


def send_kernel(sizes, rows_ref, pair_ref, gain_ref, weight_ref, same_ref, other_ref, left_ref, wide):
    sequences, local_rows, residues, chan_local, outer_width = sizes
    part = sequences // 4
    part_rows = part * local_rows
    unit_here = 2 * lax.axis_index("branch") + lax.rem(lax.axis_index("row"), 2)
    unit_other = 2 * lax.axis_index("branch") + 1 - lax.rem(lax.axis_index("row"), 2)
    same_ref[0:part_rows, :] = rows_ref[pl.ds(unit_here * part_rows, part_rows), :]
    other_ref[0:part_rows, :] = rows_ref[pl.ds(unit_other * part_rows, part_rows), :]
    pair = widened(pair_ref[...])
    flat_pair = rounded(jnp.concatenate([pair[:, i, :] for i in range(local_rows)], axis=1))
    same_ref[part_rows : part_rows + chan_local, :] = flat_pair
    other_ref[part_rows : part_rows + chan_local, :] = flat_pair
    normed = rounded(layer_normalize(widened(rows_ref[...]), 1) * gain_ref[...])
    wide[:, 0 : 2 * outer_width] = product(normed, weight_ref[...])
    base = part_rows + chan_local
    for i in range(local_rows):
        both = rounded(wide[pl.ds(i, sequences, stride=local_rows), :])
        lanes = slice(i * outer_width, (i + 1) * outer_width)
        left_ref[:, lanes] = both[:, :outer_width]
        same_ref[base : base + sequences, lanes] = both[:, outer_width : 2 * outer_width]
    other_ref[base : base + sequences, :] = same_ref[base : base + sequences, :]


def weight_kernel(left_ref, input_ref, gate_ref, gain_ref, output_ref, up_ref, down_ref, packed_ref):
    at = 0
    kinds, tri_local, _ = input_ref.shape
    for kind in range(kinds):
        packed_ref[at : at + tri_local, :] = input_ref[kind]
        at += tri_local
    packed_ref[at : at + gate_ref.shape[0], :] = gate_ref[...]
    at += gate_ref.shape[0]
    scaled = widened(output_ref[...]) * gain_ref[...]
    packed_ref[at : at + tri_local, :] = rounded(scaled.T)
    at += tri_local
    for ref in (up_ref, down_ref):
        packed_ref[at : at + ref.shape[0], :] = ref[...]
        at += ref.shape[0]
    sequences = left_ref.shape[0]
    for start in (0, 128):
        packed_ref[at : at + sequences, :] = left_ref[:, start : start + 128]
        at += sequences


def relay_kernel(sizes, own_ref, one_ref, two_ref, three_ref, relay_ref):
    sequences, local_rows, residues, chan_local, outer_width = sizes
    part_rows = sequences // 4 * local_rows
    row = lax.axis_index("row")
    branch = lax.axis_index("branch")
    base = part_rows + chan_local
    shard_total = 4
    for distance, ref in enumerate((own_ref, one_ref, two_ref, three_ref)):
        shard = row ^ distance
        relay_ref[pl.ds(pl.multiple_of(shard * chan_local, chan_local), chan_local), :] = ref[
            part_rows:base, :
        ]

        @pl.when(shard // 2 == branch)
        def _():
            start = shard_total * chan_local + lax.rem(shard, 2) * sequences
            relay_ref[pl.ds(pl.multiple_of(start, sequences), sequences), :] = ref[
                base : base + sequences, :
            ]


def score_kernel(
    sizes, own_ref, one_ref, two_ref, three_ref, gain_ref, weight_ref,
    score_ref, values_ref, gate_ref, module,
):
    sequences, local_rows, residues, chan_local, outer_width = sizes
    part = sequences // 4
    part_rows = part * local_rows
    width = gain_ref.shape[1]
    head_size = 32
    row = lax.axis_index("row")
    for distance, ref in enumerate((own_ref, one_ref, two_ref, three_ref)):
        shard = row ^ distance
        block = widened(ref[0:part_rows, :])
        unit = layer_normalize(block, 1) * gain_ref[...]
        module[:, pl.ds(pl.multiple_of(shard * local_rows, local_rows), local_rows), :] = unit.reshape(
            part, local_rows, width
        )
    normed = rounded(module[...].reshape(part * residues, width))
    half = residues // 2
    here = module[:, pl.ds(pl.multiple_of(row // 2 * half, half), half), :]
    query_rows = rounded(here.reshape(part * half, width))
    heads = values_ref.shape[1]
    query = rounded(product(query_rows, weight_ref[:, 0:heads]) * head_size ** (-0.5))
    keys = rounded(product(normed, weight_ref[:, heads : 2 * heads]))
    values_ref[...] = rounded(product(normed, weight_ref[:, 2 * heads : 3 * heads]))
    gate_ref[...] = rounded(jax.nn.sigmoid(product(query_rows, weight_ref[:, 3 * heads :])))
    groups = heads // head_size
    mask = same_group(groups * residues, heads, head_size)
    for s in range(part):
        one = keys[s * residues : (s + 1) * residues]
        spread = jnp.where(mask, jnp.concatenate([one] * groups, axis=0), jnp.bfloat16(0))
        score_ref[s * half : (s + 1) * half, :] = product(
            query[s * half : (s + 1) * half], spread, 1, 1
        )


def mix_kernel(
    sizes, pair_refs, score_ref, values_ref, gate_ref, bias_ref, mixing_ref, own_ref, one_ref,
    near_here_ref, near_there_ref, far_here_ref, far_there_ref, full, flat, module,
):
    sequences, local_rows, residues, chan_local, outer_width = sizes
    part = sequences // 4
    part_rows = part * local_rows
    half = residues // 2
    heads = values_ref.shape[1]
    head_size = 32
    groups = heads // head_size
    row = lax.axis_index("row")
    branch = lax.axis_index("branch")
    seq = lax.axis_index("seq")
    pair_width = 4 * chan_local
    for distance, ref in zip((0, 2, 1, 3), pair_refs):
        source = pl.multiple_of((seq ^ distance) * chan_local, chan_local)
        for k in range(2):
            shard = row // 2 * 2 + k
            start = pl.multiple_of(shard * chan_local, chan_local)
            full[k, pl.ds(source, chan_local), :] = ref[pl.ds(start, chan_local), :]
    for k in range(2):
        plain = rounded(layer_normalize(widened(full[k]), 0))
        bias = widened(rounded(product(bias_ref[...], plain)))
        for i in range(local_rows):
            for h in range(groups):
                flat[k * local_rows + i : k * local_rows + i + 1, h * residues : (h + 1) * residues] = bias[
                    h : h + 1, i * residues : (i + 1) * residues
                ]
    bias_rows = flat[...]
    scores = (
        score_ref[...].reshape(part, half, groups * residues) + bias_rows[None]
    ).reshape(part * half, groups * residues)
    weights = rounded(jnp.exp(scores - group_maximum(scores, residues)))
    mask = same_group(groups * residues, heads, head_size)
    ones = jnp.where(mask, jnp.bfloat16(1), jnp.bfloat16(0))
    totals = product(weights, ones)
    attended = []
    for s in range(part):
        one = values_ref[s * residues : (s + 1) * residues, :]
        spread = jnp.where(mask, jnp.concatenate([one] * groups, axis=0), jnp.bfloat16(0))
        attended.append(product(weights[s * half : (s + 1) * half], spread))
    mixed = rounded(widened(gate_ref[...]) * (jnp.concatenate(attended, axis=0) / totals))
    projected = product(mixed, mixing_ref[...])
    width = projected.shape[1]
    module[...] = projected.reshape(part, half, width)
    halved = width // 2
    for distance, ref, here, there in (
        (0, own_ref, near_here_ref, near_there_ref),
        (1, one_ref, far_here_ref, far_there_ref),
    ):
        place = lax.rem(row, 2) ^ distance
        update = module[:, pl.ds(pl.multiple_of(place * local_rows, local_rows), local_rows), :]
        result = rounded(widened(ref[0:part_rows, :]) + update.reshape(part_rows, width))
        low, high = result[:, :halved], result[:, halved:]
        here[...] = jnp.where(branch == 0, low, high)
        there[...] = jnp.where(branch == 0, high, low)


def place_kernel(own_ref, branch_ref, row_ref, both_ref, output_ref):
    rows = own_ref.shape[0]
    branch = lax.axis_index("branch")
    parity = lax.rem(lax.axis_index("row"), 2)
    for flip_branch, flip_row, ref in (
        (0, 0, own_ref),
        (1, 0, branch_ref),
        (0, 1, row_ref),
        (1, 1, both_ref),
    ):
        unit = 2 * (branch ^ flip_branch) + (parity ^ flip_row)
        output_ref[pl.ds(pl.multiple_of(unit * rows, rows), rows), :] = ref[...]


def pair_kernel(
    sizes, pair_refs, weight_refs, gain_ref, transition_gain_ref, outer_weight_ref, seq_total,
    output_ref, rows, columns, gates, outer, outer_flat, ordered, final,
):
    sequences, local_rows, residues, chan_local, outer_width = sizes
    half = residues // 2
    row = lax.axis_index("row")
    branch = lax.axis_index("branch")
    seq = lax.axis_index("seq")
    width = 4 * chan_local
    chan = chan_local
    for distance, pair_ref, weight_ref in zip((0, 2, 1, 3), pair_refs, weight_refs):
        place = pl.ds(pl.multiple_of((seq ^ distance) * chan, chan), chan)
        rows[place, :] = pair_ref[pl.ds(pl.multiple_of(row * chan, chan), chan), :]
        for k in range(2):
            start = pl.multiple_of((2 * branch + k) * chan, chan)
            columns[k, place, :] = pair_ref[pl.ds(start, chan), :]
        gates[place, :] = weight_ref[4 * chan : 5 * chan, :]

    def projection(values, kind):
        weights = jnp.concatenate([w[kind * chan : (kind + 1) * chan, :] for w in weight_refs], axis=0)
        return product(values, weights, 1, 1)

    raw = widened(rows[...])
    row_input = rounded((layer_normalize(raw, 0) * gain_ref[...]).T)
    left = widened(
        rounded(projection(row_input, 0) * jax.nn.sigmoid(projection(row_input, 1)))
    ).reshape(local_rows, residues, width)
    right = []
    for k in range(2):
        column_input = rounded((layer_normalize(widened(columns[k]), 0) * gain_ref[...]).T)
        right.append(
            widened(
                rounded(projection(column_input, 2) * jax.nn.sigmoid(projection(column_input, 3)))
            ).reshape(local_rows, residues, width)
        )
    right = jnp.concatenate(right, axis=0)
    triangle = jnp.concatenate(
        [jnp.sum(left[i][None] * right, axis=1) for i in range(local_rows)], axis=0
    )
    triangle = widened(rounded(triangle))
    tri_norm = rounded(layer_normalize(triangle, 1))
    output_weight = jnp.concatenate([w[5 * chan : 6 * chan, :] for w in weight_refs], axis=0)
    tri_out = product(tri_norm, output_weight)
    ordered[...] = raw.T.reshape(local_rows, residues, width)
    place = pl.ds(pl.multiple_of(branch * half, half), half)
    raw_here = ordered[:, place, :].reshape(local_rows * half, width)
    ordered[...] = widened(row_input).reshape(local_rows, residues, width)
    input_here = rounded(ordered[:, place, :].reshape(local_rows * half, width))
    gate = jax.nn.sigmoid(product(input_here, gates[...], 1, 1))
    first_update = widened(rounded(raw_here + gate * tri_out))
    trans_norm = rounded(layer_normalize(first_update, 1) * transition_gain_ref[...])
    down = jnp.zeros((local_rows * half, width), jnp.float32)
    at = 6 * chan
    hidden_local = (weight_refs[0].shape[0] - at - 2 * sequences) // 2
    for w in weight_refs:
        hidden = rounded(jax.nn.relu(product(trans_norm, w[at : at + hidden_local, :], 1, 1)))
        down += product(hidden, w[at + hidden_local : at + hidden_local + width, :], 1, 1)
    pair_next = widened(rounded(first_update + down))

    at = at + 2 * hidden_local
    lefts = jnp.concatenate(
        [
            jnp.concatenate([w[at : at + sequences, :], w[at + sequences : at + 2 * sequences, :]], axis=1)
            for w in weight_refs
        ],
        axis=0,
    )
    base = 4 * chan
    rights = jnp.concatenate(
        [
            jnp.concatenate([p[base : base + sequences, :], p[base + sequences :, :]], axis=1)
            for p in pair_refs
        ],
        axis=0,
    )
    outer_all = product(rounded(widened(lefts).T), rights)
    each = 128 // outer_width
    for tile in range(half // each):
        outer[tile] = outer_all[:, tile * 128 : (tile + 1) * 128]
        for c in range(outer_width):
            strip = outer[tile, pl.ds(c, local_rows, stride=outer_width), :]
            for k in range(each):
                j = tile * each + k
                outer_flat[
                    j * local_rows : (j + 1) * local_rows, c * outer_width : (c + 1) * outer_width
                ] = strip[:, k * outer_width : (k + 1) * outer_width]
    final[...] = product(rounded(outer_flat[...]), outer_weight_ref[...]) * (1.0 / seq_total)
    outer_update = jnp.concatenate(
        [final[pl.ds(i, half, stride=local_rows), :] for i in range(local_rows)], axis=0
    )
    outer_update = widened(rounded(outer_update))
    final[...] = (pair_next + outer_update).T
    output_ref[...] = rounded(final[pl.ds(pl.multiple_of(seq * chan, chan), chan), :])


def compact_shards(
    alignment_input, pairwise_input, alignment_gain, product_gain, attention_weight, mixing_weight,
    outer_input_weight, outer_output_weight, bias_matrix, pairwise_gain, triangle_input_weight,
    triangle_gate_weight, triangle_gain, triangle_output_weight, transition_gain,
    transition_up_weight, transition_down_weight,
):
    sequences, local_rows, width = alignment_input.shape
    chan_local, _, residues = pairwise_input.shape
    pair_width, groups = bias_matrix.shape
    heads = mixing_weight.shape[0]
    outer_width = outer_input_weight.shape[2]
    part = sequences // 4
    part_rows = part * local_rows
    half = residues // 2
    sizes = (sequences, local_rows, residues, chan_local, outer_width)
    half_type, full_type = jnp.bfloat16, jnp.float32

    def shape(*dims, dtype=half_type):
        return jax.ShapeDtypeStruct(dims, dtype)

    rows_flat = alignment_input.reshape(sequences * local_rows, width)
    message_rows = part_rows + chan_local + sequences
    same, other, left = kernel_call(
        functools.partial(send_kernel, sizes),
        [shape(message_rows, width), shape(message_rows, width), shape(sequences, local_rows * outer_width)],
        [rows_flat, pairwise_input, product_gain[None], outer_input_weight.reshape(width, 2 * outer_width)],
        [pltpu.VMEM((sequences * local_rows, 128), full_type)],
    )
    from_three = exchange(other, "row", 3)
    from_two = exchange(same, "row", 2)
    from_one = exchange(other, "row", 1)
    received = (same, from_one, from_two, from_three)

    packed_rows = 6 * chan_local + transition_up_weight.shape[0] + transition_down_weight.shape[0] + 2 * sequences
    (packed,) = kernel_call(
        weight_kernel,
        [shape(packed_rows, pair_width)],
        [left, triangle_input_weight, triangle_gate_weight, triangle_gain[None],
         triangle_output_weight, transition_up_weight, transition_down_weight],
    )
    packed_x = exchange(packed, "seq", 2)
    packed_core = exchange(packed, "seq", 1)
    packed_both = exchange(packed_x, "seq", 1)
    weights = (packed, packed_x, packed_core, packed_both)

    (relay,) = kernel_call(
        functools.partial(relay_kernel, sizes),
        [shape(4 * chan_local + 2 * sequences, width)],
        list(received),
    )
    relay_x = exchange(relay, "seq", 2)
    relay_core = exchange(relay, "seq", 1)
    relay_both = exchange(relay_x, "seq", 1)
    relays = (relay, relay_x, relay_core, relay_both)

    scores, values, gate = kernel_call(
        functools.partial(score_kernel, sizes),
        [shape(part * half, groups * residues, dtype=full_type), shape(part * residues, heads), shape(part * half, heads)],
        [*received, alignment_gain[None], attention_weight.reshape(width, 4 * heads)],
        [pltpu.VMEM((part, residues, width), full_type)],
    )

    def mix_body(*refs):
        mix_kernel(sizes, refs[:4], *refs[4:])

    near_here, near_there, far_here, far_there = kernel_call(
        mix_body,
        [shape(part_rows, width // 2)] * 4,
        [*relays, scores, values, gate, bias_matrix.T, mixing_weight, same, from_one],
        [
            pltpu.VMEM((2, pair_width, local_rows * residues), half_type),
            pltpu.VMEM((half, groups * residues), full_type),
            pltpu.VMEM((part, half, width), full_type),
        ],
    )
    axes = ("branch", "row")
    across = lax.axis_size("row")
    from_branch = exchange(near_there, axes, across)
    from_both = exchange(far_there, axes, across + 1)
    from_row = exchange(far_here, axes, 1)

    def pair_body(*refs):
        pair_kernel(sizes, refs[:4], refs[4:8], *refs[8:11], sequences * 4, *refs[11:])

    (pair_flat,) = kernel_call(
        pair_body,
        [shape(chan_local, local_rows * half)],
        [*relays, *weights, pairwise_gain[:, None], transition_gain[None],
         outer_output_weight.reshape(outer_width * outer_width, pair_width)],
        [
            pltpu.VMEM((pair_width, local_rows * residues), half_type),
            pltpu.VMEM((2, pair_width, local_rows * residues), half_type),
            pltpu.VMEM((pair_width, pair_width), half_type),
            pltpu.VMEM((half * outer_width // 128, local_rows * outer_width, 128), full_type),
            pltpu.VMEM((local_rows * half, outer_width * outer_width), full_type),
            pltpu.VMEM((local_rows, residues, pair_width), full_type),
            pltpu.VMEM((local_rows * half, pair_width), full_type),
        ],
    )
    (alignment_flat,) = kernel_call(
        place_kernel,
        [shape(sequences * local_rows, width // 2)],
        [near_here, from_branch, from_row, from_both],
    )
    return (
        alignment_flat.reshape(sequences, local_rows, width // 2),
        pair_flat.reshape(chan_local, local_rows, half),
    )


def is_compact(mesh, residues):
    return mesh.shape["row"] == 4 and mesh.shape["seq"] == 4 and mesh.shape["branch"] == 2


def solution(mesh):
    return jax.shard_map(
        compact_shards if is_compact(mesh, None) else shards,
        mesh=mesh,
        in_specs=(
            P("seq", "row", None),
            P("seq", "row", None),
            P(),
            P(),
            P(),
            P(),
            P(),
            P(),
            P(),
            P(),
            P(None, "seq", None),
            P("seq", None),
            P("seq"),
            P(None, "seq"),
            P(),
            P("seq", None),
            P(None, "seq"),
        ),
        out_specs=(P("seq", "row", "branch"), P("seq", "row", "branch")),
        check_vma=False,
    )
```

```python
import functools

import jax
import jax.numpy as jnp
from jax import lax
from jax.experimental import pallas as pl
from jax.experimental.pallas import tpu as pltpu
from jax.sharding import PartitionSpec as P

EPSILON = 1e-05


def shifted(value, axis, by):
    length = lax.axis_size(axis)
    pairs = [(i, i + by) for i in range(length) if 0 <= i + by < length]
    return lax.ppermute(value, axis, pairs)


def from_partner(value, axis, distance):
    return lax.ppermute(value, axis, [(i, i ^ 1 << distance) for i in range(lax.axis_size(axis))])


def layer_normalize(values, axis):
    average = jnp.mean(values, axis=axis, keepdims=True)
    centred = values - average
    spread = jnp.mean(centred * centred, axis=axis, keepdims=True)
    return centred * lax.rsqrt(spread + EPSILON)


def full_channels(values):
    return lax.all_gather(values, "seq", axis=0, tiled=True)


def channel_sum(term, kept_rows):
    return lax.psum_scatter(
        term(jnp.int32(0), kept_rows * lax.axis_size("seq")), "seq", scatter_dimension=0, tiled=True
    )


def shards(
    alignment_input,
    pairwise_input,
    alignment_gain,
    product_gain,
    attention_weight,
    mixing_weight,
    outer_input_weight,
    outer_output_weight,
    bias_matrix,
    pairwise_gain,
    triangle_input_weight,
    triangle_gate_weight,
    triangle_gain,
    triangle_output_weight,
    transition_gain,
    transition_up_weight,
    transition_down_weight,
):
    local_sequences, local_rows, alignment_channels = alignment_input.shape
    chan_local = pairwise_input.shape[0]
    residues = pairwise_input.shape[2]
    pair_width, head_total = bias_matrix.shape
    latent_heads = mixing_weight.shape[0]
    head_size = latent_heads // head_total
    outer_width = outer_input_weight.shape[2]
    tri_local = triangle_input_weight.shape[1]
    trans_local = transition_up_weight.shape[0]
    seq_total = local_sequences * lax.axis_size("seq")
    path_index = lax.axis_index("branch")
    alignment_branch = path_index == 0
    query_shape = (local_sequences, local_rows, latent_heads)
    pair_shape = (chan_local, local_rows, residues)
    full_pair_shape = (pair_width, local_rows, residues)
    key_shape = (local_sequences, 2 * latent_heads, local_rows)
    gathered = full_channels(pairwise_input)

    def alignment_early():
        alignment_module = layer_normalize(alignment_input.astype(jnp.float32), 2)
        normalized_values = (alignment_module * alignment_gain).astype(jnp.bfloat16)
        outer_normalized = (alignment_module * product_gain).astype(jnp.bfloat16)
        flattened_rows = normalized_values.reshape(-1, alignment_channels)
        outer_flattened = outer_normalized.reshape(-1, alignment_channels)
        query = (
            (
                jnp.dot(flattened_rows, attention_weight[:, 0], preferred_element_type=jnp.float32)
                * head_size ** (-0.5)
            )
            .astype(jnp.bfloat16)
            .reshape(query_shape)
        )
        gate = (
            jax.nn.sigmoid(
                jnp.dot(flattened_rows, attention_weight[:, 3], preferred_element_type=jnp.float32)
            )
            .astype(jnp.bfloat16)
            .reshape(query_shape)
        )
        key_values = (
            jnp.einsum(
                "sim,mkc->skci",
                normalized_values,
                attention_weight[:, 1:3],
                preferred_element_type=jnp.float32,
            )
            .astype(jnp.bfloat16)
            .reshape(key_shape)
        )
        left = (
            jnp.dot(outer_flattened, outer_input_weight[:, 0], preferred_element_type=jnp.float32)
            .astype(jnp.bfloat16)
            .reshape(local_sequences, local_rows, outer_width)
        )
        right_cols = jnp.einsum(
            "sim,mc->sci",
            outer_normalized,
            outer_input_weight[:, 1],
            preferred_element_type=jnp.float32,
        ).astype(jnp.bfloat16)
        empty_bias = jnp.zeros((head_total, local_rows, residues), jnp.bfloat16)
        empty_pair = jnp.zeros(full_pair_shape, jnp.bfloat16)
        return (empty_bias, empty_pair, query, key_values, gate, left, right_cols)

    def pair_early():
        unit = layer_normalize(gathered.astype(jnp.float32), 0)
        plain = unit.astype(jnp.bfloat16).reshape(pair_width, -1)
        bias_rows = (
            jnp.einsum("ch,cn->hn", bias_matrix, plain, preferred_element_type=jnp.float32)
            .astype(jnp.bfloat16)
            .reshape(head_total, local_rows, residues)
        )
        tri_input = (unit * pairwise_gain[:, None, None]).astype(jnp.bfloat16)
        empty_query = jnp.zeros(query_shape, jnp.bfloat16)
        empty_keys = jnp.zeros(key_shape, jnp.bfloat16)
        empty_left = jnp.zeros((local_sequences, local_rows, outer_width), jnp.bfloat16)
        empty_right = jnp.zeros((local_sequences, outer_width, local_rows), jnp.bfloat16)
        return (bias_rows, tri_input, empty_query, empty_keys, empty_query, empty_left, empty_right)

    bias_local, tri_input, query, key_values, gate, left, right_cols = lax.cond(
        alignment_branch, alignment_early, pair_early
    )
    bias_recv = shifted(bias_local, "branch", -1)
    query_heads = query.reshape(local_sequences, local_rows, head_total, head_size).transpose(
        0, 2, 1, 3
    )

    def fold_real(running, shard_part):
        highest, totals, weighted = running
        columns = shard_part.shape[2]
        keys_part = shard_part[:, :latent_heads].reshape(
            local_sequences, head_total, head_size, columns
        )
        values_part = shard_part[:, latent_heads:].reshape(
            local_sequences, head_total, head_size, columns
        )
        bias_part = bias_recv.astype(jnp.float32)
        scores = (
            jnp.einsum(
                "shid,shdj->shij", query_heads, keys_part, preferred_element_type=jnp.float32
            )
            + bias_part[None]
        )
        raised = jnp.maximum(highest, jnp.max(scores, axis=3))
        weights = jnp.exp(scores - raised[..., None])
        totals = jnp.sum(weights, axis=3)
        weighted = jnp.einsum(
            "shij,shdj->shid",
            weights.astype(jnp.bfloat16),
            values_part,
            preferred_element_type=jnp.float32,
        )
        return (raised, totals, weighted)

    initial = (
        jnp.full((local_sequences, head_total, local_rows), -1e30, jnp.float32),
        jnp.zeros((local_sequences, head_total, local_rows), jnp.float32),
        jnp.zeros((local_sequences, head_total, local_rows, head_size), jnp.float32),
    )
    shard_part = lax.all_gather(key_values, "row", axis=2, tiled=True)
    highest, totals, weighted = lax.cond(
        alignment_branch, lambda: fold_real(initial, shard_part), lambda: initial
    )
    safe_totals = jnp.where(totals > 0, totals, 1.0)
    attended = (weighted / safe_totals[..., None]).transpose(0, 2, 1, 3).reshape(query_shape)
    mixed_heads = (gate.astype(jnp.float32) * attended).astype(jnp.bfloat16)
    right_full = lax.all_gather(right_cols, "row", axis=2, tiled=True)
    right_matrix = right_full.reshape(local_sequences * outer_width, residues)
    spread = lax.cond(
        alignment_branch,
        lambda: jnp.einsum(
            "sic,cdo->oisd", left, outer_output_weight, preferred_element_type=jnp.float32
        ).astype(jnp.bfloat16),
        lambda: jnp.zeros((pair_width, local_rows, local_sequences, outer_width), jnp.bfloat16),
    )

    def outer_term(amount):
        spread_part = spread.reshape(amount * local_rows, local_sequences * outer_width)
        return jnp.dot(spread_part, right_matrix, preferred_element_type=jnp.float32).reshape(
            amount, local_rows, residues
        )

    tri_flat = tri_input.reshape(pair_width, -1)

    def pair_operands():
        linear = jnp.dot(
            triangle_input_weight.reshape(4 * tri_local, pair_width),
            tri_flat,
            preferred_element_type=jnp.float32,
        )
        linear = linear.reshape(4, tri_local, local_rows, residues)
        left_part = (linear[0] * jax.nn.sigmoid(linear[1])).astype(jnp.bfloat16)
        right_part = (linear[2] * jax.nn.sigmoid(linear[3])).astype(jnp.bfloat16)
        return (left_part, right_part)

    def empty_operands():
        empty = jnp.zeros((tri_local, local_rows, residues), jnp.bfloat16)
        return (empty, empty)

    left_tri, right_tri = lax.cond(alignment_branch, empty_operands, pair_operands)
    tri_shard_part = lax.all_gather(right_tri, "row", axis=1, tiled=True)
    triangle = lax.optimization_barrier(
        lax.cond(
            alignment_branch,
            lambda: jnp.zeros((tri_local, local_rows, tri_shard_part.shape[1]), jnp.float32),
            lambda: jnp.einsum(
                "cik,cjk->cij", left_tri, tri_shard_part, preferred_element_type=jnp.float32
            ),
        ).astype(jnp.bfloat16)
    )
    tri_float = triangle.astype(jnp.float32)
    summed, squared = lax.psum(
        (jnp.sum(tri_float, axis=0), jnp.sum(tri_float * tri_float, axis=0)), "seq"
    )
    tri_total = tri_local * lax.axis_size("seq")
    average = summed / tri_total
    variance = jnp.maximum(squared / tri_total - average * average, 0.0)
    tri_norm = (
        (tri_float - average) * lax.rsqrt(variance + EPSILON) * triangle_gain[:, None, None]
    ).astype(jnp.bfloat16)
    norm_flat = tri_norm.reshape(tri_local, -1)

    def tri_term(amount):
        return jnp.dot(
            triangle_output_weight, norm_flat, preferred_element_type=jnp.float32
        ).reshape(amount, local_rows, residues)

    def first_term(offset, amount):
        return lax.cond(alignment_branch, lambda: outer_term(amount), lambda: tri_term(amount))

    summed_first = channel_sum(first_term, chan_local)
    outer_increment = (summed_first * (1.0 / seq_total)).astype(jnp.bfloat16)
    gate_values = jax.nn.sigmoid(
        jnp.dot(triangle_gate_weight, tri_flat, preferred_element_type=jnp.float32)
    ).reshape(pair_shape)
    first_update = lax.optimization_barrier(
        (pairwise_input.astype(jnp.float32) + gate_values * summed_first).astype(jnp.bfloat16)
    )
    gathered_next = full_channels(first_update)

    def pair_hidden():
        trans_norm = (
            (layer_normalize(gathered_next.astype(jnp.float32), 0) * transition_gain[:, None, None])
            .astype(jnp.bfloat16)
            .reshape(pair_width, -1)
        )
        return jax.nn.relu(
            jnp.dot(transition_up_weight, trans_norm, preferred_element_type=jnp.float32)
        ).astype(jnp.bfloat16)

    hidden_units = lax.cond(
        alignment_branch,
        lambda: jnp.zeros((trans_local, local_rows * residues), jnp.bfloat16),
        pair_hidden,
    )

    def trans_real(amount):
        return jnp.dot(
            transition_down_weight, hidden_units, preferred_element_type=jnp.float32
        ).reshape(amount, local_rows, residues)

    def trans_term(offset, amount):
        return lax.cond(
            alignment_branch,
            lambda: jnp.zeros((amount, local_rows, residues), jnp.float32),
            lambda: trans_real(amount),
        )

    pair_following = (
        first_update.astype(jnp.float32) + channel_sum(trans_term, chan_local)
    ).astype(jnp.bfloat16)
    half_residues = residues // 2
    halved_width = alignment_channels // 2
    outgoing_product = jnp.where(
        alignment_branch,
        outer_increment[:, :, half_residues:],
        pair_following[:, :, :half_residues],
    )
    incoming = from_partner(outgoing_product, "branch", 0)
    local_half = jnp.where(
        alignment_branch,
        outer_increment[:, :, :half_residues],
        pair_following[:, :, half_residues:],
    )
    pairwise_output = (local_half.astype(jnp.float32) + incoming.astype(jnp.float32)).astype(
        jnp.bfloat16
    )
    mixed_received = shifted(mixed_heads, "branch", 1)
    mixed_applied = jnp.where(alignment_branch, mixed_heads, mixed_received)
    mix_columns = lax.dynamic_slice_in_dim(
        mixing_weight, path_index * halved_width, halved_width, 1
    )
    residual_stream = lax.dynamic_slice_in_dim(
        alignment_input, path_index * halved_width, halved_width, 2
    )
    projected_values = jnp.dot(
        mixed_applied.reshape(-1, latent_heads), mix_columns, preferred_element_type=jnp.float32
    )
    alignment_output = (
        residual_stream.astype(jnp.float32)
        + projected_values.reshape(local_sequences, local_rows, halved_width)
    ).astype(jnp.bfloat16)
    return (alignment_output, pairwise_output)


BIAS_COST = 175 * 10**6


def rounded(values):
    return values.astype(jnp.bfloat16)


def widened(values):
    return values.astype(jnp.float32)


def product(left, right, contract_left=1, contract_right=0):
    return lax.dot_general(
        left,
        right,
        (((contract_left,), (contract_right,)), ((), ())),
        preferred_element_type=jnp.float32,
    )


def group_maximum(values, group):
    tiles = []
    for start in range(0, values.shape[1], 128):
        tile = values[:, start : start + 128]
        lane = lax.broadcasted_iota(jnp.int32, tile.shape, 1)
        step = 1
        while step < group:
            ahead = pltpu.roll(tile, 128 - step, 1)
            behind = pltpu.roll(tile, step, 1)
            tile = jnp.maximum(tile, jnp.where((lane & step) == 0, ahead, behind))
            step *= 2
        tiles.append(tile)
    return jnp.concatenate(tiles, axis=1)


def same_group(rows, columns, group):
    row = lax.broadcasted_iota(jnp.int32, (rows, columns), 0) // group
    column = lax.broadcasted_iota(jnp.int32, (rows, columns), 1) // group
    return row == column


def as_column(row):
    size = row.shape[1]
    return jnp.sum(jnp.where(same_group(size, size, 1), row, 0.0), axis=1, keepdims=True)


def kernel_call(body, outputs, operands, scratch=(), flops=0, in_hbm=(), room=32 * 2**20):
    vmem = pl.BlockSpec(memory_space=pltpu.VMEM)
    hbm = pl.BlockSpec(memory_space=pltpu.HBM)
    size = sum(a.size * a.dtype.itemsize for a in operands)
    size += sum(o.size * o.dtype.itemsize for o in outputs)
    return pl.pallas_call(
        body,
        out_shape=outputs,
        in_specs=[hbm if i in in_hbm else vmem for i in range(len(operands))],
        out_specs=[vmem] * len(outputs),
        scratch_shapes=list(scratch),
        cost_estimate=pl.CostEstimate(flops=flops, bytes_accessed=size, transcendentals=0),
        compiler_params=pltpu.CompilerParams(vmem_limit_bytes=room),
    )(*operands)


def exchange(value, axes, distance):
    members = lax.axis_size(axes)
    return lax.ppermute(value, axes, [(i, i ^ distance) for i in range(members)])


def start_kernel(token_ref):
    token_ref[...] = jnp.zeros_like(token_ref)


def send_kernel(
    sizes, rows_ref, pair_ref, gain_ref, weight_ref, input_ref, gate_ref, tri_gain_ref, output_ref, up_ref,
    down_ref, token_ref, same_ref, other_ref, shared_ref, flat_ref, wide,
):
    sequences, local_rows, residues, chan_local, outer_width = sizes
    part = sequences // 4
    part_rows = part * local_rows
    pair = widened(pair_ref[...])
    flat_pair = rounded(jnp.concatenate([pair[:, i, :] for i in range(local_rows)], axis=1))
    flat_ref[...] = flat_pair
    shared_ref[0:chan_local, :] = flat_pair
    at = chan_local + sequences
    narrow = gate_ref.shape[1]
    scaled = rounded(widened(output_ref[...]) * as_column(tri_gain_ref[...]))
    kinds = [input_ref[kind] for kind in range(input_ref.shape[0])]
    down = down_ref[...]
    for block in (*kinds, gate_ref[...], scaled, down[:chan_local]):
        shared_ref[at : at + chan_local, :narrow] = block
        at += chan_local
    at = chan_local + sequences
    for block in (up_ref[...], down[chan_local:]):
        shared_ref[at : at + block.shape[0], narrow:] = block
        at += block.shape[0]
    same_ref[part_rows : part_rows + chan_local, :] = flat_pair
    other_ref[part_rows : part_rows + chan_local, :] = flat_pair
    unit_here = 2 * lax.axis_index("branch") + lax.rem(lax.axis_index("row"), 2)
    unit_other = 2 * lax.axis_index("branch") + 1 - lax.rem(lax.axis_index("row"), 2)
    same_ref[0:part_rows, :] = rows_ref[pl.ds(unit_here * part_rows, part_rows), :]
    other_ref[0:part_rows, :] = rows_ref[pl.ds(unit_other * part_rows, part_rows), :]
    normed = rounded(layer_normalize(widened(rows_ref[...]), 1) * gain_ref[...])
    wide[:, 0 : 2 * outer_width] = product(normed, weight_ref[...], 1, 1)
    base = part_rows + chan_local
    for i in range(local_rows):
        both = rounded(wide[pl.ds(i, sequences, stride=local_rows), :])
        lanes = slice(i * outer_width, (i + 1) * outer_width)
        shared_ref[chan_local : chan_local + sequences, lanes] = both[:, :outer_width]
        same_ref[base : base + sequences, lanes] = both[:, outer_width : 2 * outer_width]
    other_ref[base : base + sequences, :] = same_ref[base : base + sequences, :]


def keep_kernel(*refs):
    count = len(refs) // 2
    for source, target in zip(refs[:count], refs[count:]):
        target[...] = source[...]


def relay_kernel(sizes, own_ref, one_ref, two_ref, three_ref, after_bias_ref, after_keep_ref, relay_ref):
    sequences, local_rows, residues, chan_local, outer_width = sizes
    part_rows = sequences // 4 * local_rows
    row = lax.axis_index("row")
    branch = lax.axis_index("branch")
    base = part_rows + chan_local
    for distance, ref in enumerate((own_ref, one_ref, two_ref, three_ref)):
        shard = row ^ distance

        @pl.when(shard // 2 == branch)
        def _():
            place = lax.rem(shard, 2)
            relay_ref[pl.ds(pl.multiple_of(place * chan_local, chan_local), chan_local), :] = ref[
                part_rows:base, :
            ]
            start = 2 * chan_local + place * sequences
            relay_ref[pl.ds(pl.multiple_of(start, chan_local), sequences), :] = ref[
                base : base + sequences, :
            ]


def score_kernel(
    sizes, own_ref, one_ref, two_ref, three_ref, gain_ref, weight_ref,
    score_ref, values_ref, gate_ref, module,
):
    sequences, local_rows, residues, chan_local, outer_width = sizes
    part = sequences // 4
    part_rows = part * local_rows
    width = gain_ref.shape[1]
    head_size = 32
    row = lax.axis_index("row")
    for distance, ref in enumerate((own_ref, one_ref, two_ref, three_ref)):
        shard = row ^ distance
        block = widened(ref[0:part_rows, :])
        unit = layer_normalize(block, 1) * gain_ref[...]
        module[:, pl.ds(pl.multiple_of(shard * local_rows, local_rows), local_rows), :] = unit.reshape(
            part, local_rows, width
        )
    normed = rounded(module[...].reshape(part * residues, width))
    half = residues // 2
    here = module[:, pl.ds(pl.multiple_of(row // 2 * half, half), half), :]
    query_rows = rounded(here.reshape(part * half, width))
    heads = values_ref.shape[1]
    query = rounded(product(query_rows, weight_ref[:, 0:heads]) * head_size ** (-0.5))
    keys = rounded(product(normed, weight_ref[:, heads : 2 * heads]))
    values_ref[...] = rounded(product(normed, weight_ref[:, 2 * heads : 3 * heads]))
    gate_ref[...] = rounded(jax.nn.sigmoid(product(query_rows, weight_ref[:, 3 * heads :])))
    groups = heads // head_size
    mask = same_group(groups * residues, heads, head_size)
    for s in range(part):
        one = keys[s * residues : (s + 1) * residues]
        spread = jnp.where(mask, jnp.concatenate([one] * groups, axis=0), jnp.bfloat16(0))
        score_ref[s * half : (s + 1) * half, :] = product(
            query[s * half : (s + 1) * half], spread, 1, 1
        )


def bias_kernel(chan_local, pair_refs, matrix_ref, bias_ref, full, flat):
    groups = matrix_ref.shape[0]
    residues = flat.shape[1] // groups
    local_rows = flat.shape[0]
    seq = lax.axis_index("seq")
    for distance, ref in zip((0, 2, 1, 3), pair_refs):
        place = pl.ds(pl.multiple_of((seq ^ distance) * chan_local, chan_local), chan_local)
        full[place, :] = widened(ref[0:chan_local, :])
    plain = rounded(layer_normalize(full[...], 0))
    bias = product(matrix_ref[...], plain)
    for i in range(local_rows):
        for h in range(groups):
            flat[i : i + 1, h * residues : (h + 1) * residues] = bias[
                h : h + 1, i * residues : (i + 1) * residues
            ]
    rows = rounded(flat[...])
    bias_ref[...] = jnp.concatenate([rows, rows], axis=0)


def mix_kernel(
    sizes, near_bias_ref, far_bias_ref, score_ref, values_ref, gate_ref, mixing_ref, own_ref, one_ref,
    near_here_ref, near_there_ref, far_here_ref, far_there_ref, module,
):
    sequences, local_rows, residues, chan_local, outer_width = sizes
    part = sequences // 4
    part_rows = part * local_rows
    half = residues // 2
    heads = values_ref.shape[1]
    head_size = 32
    groups = heads // head_size
    row = lax.axis_index("row")
    branch = lax.axis_index("branch")
    first = lax.broadcasted_iota(jnp.int32, near_bias_ref.shape, 0) // local_rows == lax.rem(row, 2)
    bias_rows = jnp.where(first, widened(near_bias_ref[...]), widened(far_bias_ref[...]))
    scores = (
        score_ref[...].reshape(part, half, groups * residues) + bias_rows[None]
    ).reshape(part * half, groups * residues)
    weights = rounded(jnp.exp(scores - group_maximum(scores, residues)))
    mask = same_group(groups * residues, heads, head_size)
    ones = jnp.where(mask, jnp.bfloat16(1), jnp.bfloat16(0))
    totals = product(weights, ones)
    attended = []
    for s in range(part):
        one = values_ref[s * residues : (s + 1) * residues, :]
        spread = jnp.where(mask, jnp.concatenate([one] * groups, axis=0), jnp.bfloat16(0))
        attended.append(product(weights[s * half : (s + 1) * half], spread))
    mixed = rounded(widened(gate_ref[...]) * (jnp.concatenate(attended, axis=0) / totals))
    projected = product(mixed, mixing_ref[...])
    width = projected.shape[1]
    module[...] = projected.reshape(part, half, width)
    halved = width // 2
    for distance, ref, here, there in (
        (0, own_ref, near_here_ref, near_there_ref),
        (1, one_ref, far_here_ref, far_there_ref),
    ):
        place = lax.rem(row, 2) ^ distance
        update = module[:, pl.ds(pl.multiple_of(place * local_rows, local_rows), local_rows), :]
        result = rounded(widened(ref[0:part_rows, :]) + update.reshape(part_rows, width))
        low, high = result[:, :halved], result[:, halved:]
        here[...] = jnp.where(branch == 0, low, high)
        there[...] = jnp.where(branch == 0, high, low)


def place_kernel(own_ref, branch_ref, row_ref, both_ref, pair_ref, output_ref, pair_output_ref):
    pair_output_ref[...] = pair_ref[...]
    rows = own_ref.shape[0]
    branch = lax.axis_index("branch")
    parity = lax.rem(lax.axis_index("row"), 2)
    for flip_branch, flip_row, ref in (
        (0, 0, own_ref),
        (1, 0, branch_ref),
        (0, 1, row_ref),
        (1, 1, both_ref),
    ):
        unit = 2 * (branch ^ flip_branch) + (parity ^ flip_row)
        output_ref[pl.ds(pl.multiple_of(unit * rows, rows), rows), :] = ref[...]


def pair_kernel(
    sizes, shared_refs, pair_refs, gain_ref, transition_gain_ref, outer_weight_ref, seq_total, hidden_local,
    output_ref, rows, columns, gates, outer, outer_flat, ordered, final,
):
    sequences, local_rows, residues, chan_local, outer_width = sizes
    half = residues // 2
    branch = lax.axis_index("branch")
    seq = lax.axis_index("seq")
    width = 4 * chan_local
    chan = chan_local
    gain = as_column(gain_ref[...])
    at = chan + sequences
    weight_refs = [ref.at[at:, 0:width] for ref in shared_refs]
    hidden_refs = [ref.at[at:, width:] for ref in shared_refs]
    for distance, row_ref, pair_ref, weight_ref in zip((0, 2, 1, 3), shared_refs, pair_refs, weight_refs):
        place = pl.ds(pl.multiple_of((seq ^ distance) * chan, chan), chan)
        rows[place, :] = row_ref[0:chan, :]
        for k in range(2):
            columns[k, place, :] = pair_ref[k * chan : (k + 1) * chan, :]
        gates[place, :] = weight_ref[4 * chan : 5 * chan, :]

    def projection(values, kind):
        weights = jnp.concatenate([w[kind * chan : (kind + 1) * chan, :] for w in weight_refs], axis=0)
        return product(values, weights, 1, 1)

    raw = widened(rows[...])
    row_input = rounded((layer_normalize(raw, 0) * gain).T)
    left = widened(
        rounded(projection(row_input, 0) * jax.nn.sigmoid(projection(row_input, 1)))
    ).reshape(local_rows, residues, width)
    right = []
    for k in range(2):
        column_input = rounded((layer_normalize(widened(columns[k]), 0) * gain).T)
        right.append(
            widened(
                rounded(projection(column_input, 2) * jax.nn.sigmoid(projection(column_input, 3)))
            ).reshape(local_rows, residues, width)
        )
    right = jnp.concatenate(right, axis=0)
    triangle = jnp.concatenate(
        [jnp.sum(left[i][None] * right, axis=1) for i in range(local_rows)], axis=0
    )
    triangle = widened(rounded(triangle))
    tri_norm = rounded(layer_normalize(triangle, 1))
    output_weight = jnp.concatenate([w[5 * chan : 6 * chan, :] for w in weight_refs], axis=0)
    tri_out = product(tri_norm, output_weight)
    ordered[...] = raw.T.reshape(local_rows, residues, width)
    place = pl.ds(pl.multiple_of(branch * half, half), half)
    raw_here = ordered[:, place, :].reshape(local_rows * half, width)
    ordered[...] = widened(row_input).reshape(local_rows, residues, width)
    input_here = rounded(ordered[:, place, :].reshape(local_rows * half, width))
    gate = jax.nn.sigmoid(product(input_here, gates[...], 1, 1))
    first_update = widened(rounded(raw_here + gate * tri_out))
    trans_norm = rounded(layer_normalize(first_update, 1) * transition_gain_ref[...])
    down = jnp.zeros((local_rows * half, width), jnp.float32)
    for w, h in zip(weight_refs, hidden_refs):
        hidden = rounded(jax.nn.relu(product(trans_norm, h[0:hidden_local, :], 1, 1)))
        down_weight = jnp.concatenate([w[6 * chan : 7 * chan, :], h[hidden_local : hidden_local + 3 * chan, :]], axis=0)
        down += product(hidden, down_weight, 1, 1)
    pair_next = widened(rounded(first_update + down))

    lefts = jnp.concatenate([ref[chan : chan + sequences, :] for ref in shared_refs], axis=0)
    base = 2 * chan
    rights = jnp.concatenate(
        [
            jnp.concatenate([p[base : base + sequences, :], p[base + sequences :, :]], axis=1)
            for p in pair_refs
        ],
        axis=0,
    )
    outer_all = product(rounded(widened(lefts).T), rights)
    each = 128 // outer_width
    for tile in range(half // each):
        outer[tile] = outer_all[:, tile * 128 : (tile + 1) * 128]
        for c in range(outer_width):
            strip = outer[tile, pl.ds(c, local_rows, stride=outer_width), :]
            for k in range(each):
                j = tile * each + k
                outer_flat[
                    j * local_rows : (j + 1) * local_rows, c * outer_width : (c + 1) * outer_width
                ] = strip[:, k * outer_width : (k + 1) * outer_width]
    final[...] = product(rounded(outer_flat[...]), outer_weight_ref[...]) * (1.0 / seq_total)
    outer_update = jnp.concatenate(
        [final[pl.ds(i, half, stride=local_rows), :] for i in range(local_rows)], axis=0
    )
    outer_update = widened(rounded(outer_update))
    result = pair_next + outer_update
    own = result[:, 0:chan]
    for k in range(1, 4):
        own = jnp.where(seq == k, result[:, k * chan : (k + 1) * chan], own)
    output_ref[...] = rounded(own)


def compact_shards(
    alignment_input, pairwise_input, alignment_gain, product_gain, attention_weight, mixing_weight,
    outer_input_weight, outer_output_weight, bias_matrix, pairwise_gain, triangle_input_weight,
    triangle_gate_weight, triangle_gain, triangle_output_weight, transition_gain,
    transition_up_weight, transition_down_weight,
):
    sequences, local_rows, width = alignment_input.shape
    chan_local, _, residues = pairwise_input.shape
    pair_width, groups = bias_matrix.shape
    heads = mixing_weight.shape[0]
    outer_width = outer_input_weight.shape[2]
    part = sequences // 4
    part_rows = part * local_rows
    half = residues // 2
    sizes = (sequences, local_rows, residues, chan_local, outer_width)
    half_type, full_type = jnp.bfloat16, jnp.float32

    def shape(*dims, dtype=half_type):
        return jax.ShapeDtypeStruct(dims, dtype)

    rows_flat = alignment_input.reshape(sequences * local_rows, width)
    message_rows = part_rows + chan_local + sequences
    outer_weight_flat = outer_input_weight.transpose(1, 2, 0).reshape(2 * outer_width, width)
    (token,) = kernel_call(start_kernel, [shape(8, 128, dtype=full_type)], [], flops=5 * 10**9)
    hidden_local = transition_up_weight.shape[0]
    shared_rows = chan_local + sequences + 7 * chan_local
    same, other, shared, pair_flat = kernel_call(
        functools.partial(send_kernel, sizes),
        [shape(message_rows, width), shape(message_rows, width),
         shape(shared_rows, width), shape(chan_local, local_rows * residues)],
        [rows_flat, pairwise_input, product_gain[None], outer_weight_flat, triangle_input_weight,
         triangle_gate_weight, triangle_gain[None], triangle_output_weight.T, transition_up_weight,
         transition_down_weight, token],
        [pltpu.VMEM((sequences * local_rows, 128), full_type)],
    )
    shared_x = exchange(shared, "seq", 2)
    shared_core = exchange(shared, "seq", 1)
    shared_both = exchange(shared_x, "seq", 1)
    shareds = (shared, shared_x, shared_core, shared_both)
    from_three = exchange(other, "row", 3)
    from_two = exchange(same, "row", 2)
    from_one = exchange(other, "row", 1)
    received = (same, from_one, from_two, from_three)

    pair_core = exchange(pair_flat, "seq", 1)
    pair_both = exchange(shared_x[0:chan_local], "seq", 1)
    pairs = (shared, shared_x, pair_core, pair_both)

    late_weight = lax.optimization_barrier((attention_weight, pair_flat))[0]
    kept = [late_weight.reshape(width, 4 * heads), mixing_weight,
            outer_output_weight.reshape(outer_width * outer_width, pair_width),
            alignment_gain[None], pairwise_gain[None], transition_gain[None]]
    attention_kept, mixing_kept, outer_kept, row_gain, pair_gain, last_gain = kernel_call(
        keep_kernel, [shape(*a.shape, dtype=a.dtype) for a in kept], kept
    )

    def bias_body(*refs):
        bias_kernel(chan_local, refs[:4], *refs[4:])

    (near_bias,) = kernel_call(
        bias_body,
        [shape(half, groups * residues)],
        [*pairs, bias_matrix.T],
        [
            pltpu.VMEM((pair_width, local_rows * residues), full_type),
            pltpu.VMEM((local_rows, groups * residues), full_type),
        ],
        flops=BIAS_COST,
    )
    far_bias = exchange(near_bias, "row", 1)

    (relay,) = kernel_call(
        functools.partial(relay_kernel, sizes),
        [shape(2 * chan_local + 2 * sequences, width)],
        [*received, far_bias, row_gain],
    )
    relay_x = exchange(relay, "seq", 2)
    relay_core = exchange(relay, "seq", 1)
    relay_both = exchange(relay, "seq", 3)
    relays = (relay, relay_x, relay_core, relay_both)

    scores, values, gate = kernel_call(
        functools.partial(score_kernel, sizes),
        [shape(part * half, groups * residues, dtype=full_type), shape(part * residues, heads), shape(part * half, heads)],
        [*received, row_gain, attention_kept],
        [pltpu.VMEM((part, residues, width), full_type)],
        flops=3 * 10**9,
    )

    near_here, near_there, far_here, far_there = kernel_call(
        functools.partial(mix_kernel, sizes),
        [shape(part_rows, width // 2)] * 4,
        [near_bias, far_bias, scores, values, gate, mixing_kept, same, from_one],
        [pltpu.VMEM((part, half, width), full_type)],
        flops=3 * 10**9,
    )
    axes = ("branch", "row")
    across = lax.axis_size("row")
    from_branch = exchange(near_there, axes, across)
    from_both = exchange(far_there, axes, across + 1)
    from_row = exchange(far_here, axes, 1)

    def pair_body(*refs):
        pair_kernel(sizes, refs[:4], refs[4:8], *refs[8:11], sequences * 4, hidden_local, *refs[11:])

    (pair_done,) = kernel_call(
        pair_body,
        [shape(local_rows * half, chan_local)],
        [*shareds, *relays, pair_gain, last_gain, outer_kept],
        [
            pltpu.VMEM((pair_width, local_rows * residues), half_type),
            pltpu.VMEM((2, pair_width, local_rows * residues), half_type),
            pltpu.VMEM((pair_width, pair_width), half_type),
            pltpu.VMEM((half * outer_width // 128, local_rows * outer_width, 128), full_type),
            pltpu.VMEM((local_rows * half, outer_width * outer_width), full_type),
            pltpu.VMEM((local_rows, residues, pair_width), full_type),
            pltpu.VMEM((local_rows * half, pair_width), full_type),
        ],
    )
    alignment_flat, pairwise_output = kernel_call(
        place_kernel,
        [shape(sequences * local_rows, width // 2), shape(local_rows * half, chan_local)],
        [near_here, from_branch, from_row, from_both, pair_done],
    )
    return (
        alignment_flat.reshape(sequences, local_rows, width // 2),
        pairwise_output.reshape(local_rows, half, chan_local).transpose(2, 0, 1),
    )


def is_compact(mesh, residues):
    return mesh.shape["row"] == 4 and mesh.shape["seq"] == 4 and mesh.shape["branch"] == 2


def solution(mesh):
    return jax.shard_map(
        compact_shards if is_compact(mesh, None) else shards,
        mesh=mesh,
        in_specs=(
            P("seq", "row", None),
            P("seq", "row", None),
            P(),
            P(),
            P(),
            P(),
            P(),
            P(),
            P(),
            P(),
            P(None, "seq", None),
            P("seq", None),
            P("seq"),
            P(None, "seq"),
            P(),
            P("seq", None),
            P(None, "seq"),
        ),
        out_specs=(P("seq", "row", "branch"), P("seq", "row", "branch")),
        check_vma=False,
    )
```

```python
import functools

import jax
import jax.numpy as jnp
from jax import lax
from jax.experimental import pallas as pl
from jax.experimental.pallas import tpu as pltpu
from jax.sharding import PartitionSpec as P

EPSILON = 1e-05


def shifted(value, axis, by):
    length = lax.axis_size(axis)
    pairs = [(i, i + by) for i in range(length) if 0 <= i + by < length]
    return lax.ppermute(value, axis, pairs)


def from_partner(value, axis, distance):
    return lax.ppermute(value, axis, [(i, i ^ 1 << distance) for i in range(lax.axis_size(axis))])


def layer_normalize(values, axis):
    average = jnp.mean(values, axis=axis, keepdims=True)
    centred = values - average
    spread = jnp.mean(centred * centred, axis=axis, keepdims=True)
    return centred * lax.rsqrt(spread + EPSILON)


def full_channels(values):
    return lax.all_gather(values, "seq", axis=0, tiled=True)


def channel_sum(term, kept_rows):
    return lax.psum_scatter(
        term(jnp.int32(0), kept_rows * lax.axis_size("seq")), "seq", scatter_dimension=0, tiled=True
    )


def shards(
    alignment_input,
    pairwise_input,
    alignment_gain,
    product_gain,
    attention_weight,
    mixing_weight,
    outer_input_weight,
    outer_output_weight,
    bias_matrix,
    pairwise_gain,
    triangle_input_weight,
    triangle_gate_weight,
    triangle_gain,
    triangle_output_weight,
    transition_gain,
    transition_up_weight,
    transition_down_weight,
):
    local_sequences, local_rows, alignment_channels = alignment_input.shape
    chan_local = pairwise_input.shape[0]
    residues = pairwise_input.shape[2]
    pair_width, head_total = bias_matrix.shape
    latent_heads = mixing_weight.shape[0]
    head_size = latent_heads // head_total
    outer_width = outer_input_weight.shape[2]
    tri_local = triangle_input_weight.shape[1]
    trans_local = transition_up_weight.shape[0]
    seq_total = local_sequences * lax.axis_size("seq")
    path_index = lax.axis_index("branch")
    alignment_branch = path_index == 0
    query_shape = (local_sequences, local_rows, latent_heads)
    pair_shape = (chan_local, local_rows, residues)
    full_pair_shape = (pair_width, local_rows, residues)
    key_shape = (local_sequences, 2 * latent_heads, local_rows)
    gathered = full_channels(pairwise_input)

    def alignment_early():
        alignment_module = layer_normalize(alignment_input.astype(jnp.float32), 2)
        normalized_values = (alignment_module * alignment_gain).astype(jnp.bfloat16)
        outer_normalized = (alignment_module * product_gain).astype(jnp.bfloat16)
        flattened_rows = normalized_values.reshape(-1, alignment_channels)
        outer_flattened = outer_normalized.reshape(-1, alignment_channels)
        query = (
            (
                jnp.dot(flattened_rows, attention_weight[:, 0], preferred_element_type=jnp.float32)
                * head_size ** (-0.5)
            )
            .astype(jnp.bfloat16)
            .reshape(query_shape)
        )
        gate = (
            jax.nn.sigmoid(
                jnp.dot(flattened_rows, attention_weight[:, 3], preferred_element_type=jnp.float32)
            )
            .astype(jnp.bfloat16)
            .reshape(query_shape)
        )
        key_values = (
            jnp.einsum(
                "sim,mkc->skci",
                normalized_values,
                attention_weight[:, 1:3],
                preferred_element_type=jnp.float32,
            )
            .astype(jnp.bfloat16)
            .reshape(key_shape)
        )
        left = (
            jnp.dot(outer_flattened, outer_input_weight[:, 0], preferred_element_type=jnp.float32)
            .astype(jnp.bfloat16)
            .reshape(local_sequences, local_rows, outer_width)
        )
        right_cols = jnp.einsum(
            "sim,mc->sci",
            outer_normalized,
            outer_input_weight[:, 1],
            preferred_element_type=jnp.float32,
        ).astype(jnp.bfloat16)
        empty_bias = jnp.zeros((head_total, local_rows, residues), jnp.bfloat16)
        empty_pair = jnp.zeros(full_pair_shape, jnp.bfloat16)
        return (empty_bias, empty_pair, query, key_values, gate, left, right_cols)

    def pair_early():
        unit = layer_normalize(gathered.astype(jnp.float32), 0)
        plain = unit.astype(jnp.bfloat16).reshape(pair_width, -1)
        bias_rows = (
            jnp.einsum("ch,cn->hn", bias_matrix, plain, preferred_element_type=jnp.float32)
            .astype(jnp.bfloat16)
            .reshape(head_total, local_rows, residues)
        )
        tri_input = (unit * pairwise_gain[:, None, None]).astype(jnp.bfloat16)
        empty_query = jnp.zeros(query_shape, jnp.bfloat16)
        empty_keys = jnp.zeros(key_shape, jnp.bfloat16)
        empty_left = jnp.zeros((local_sequences, local_rows, outer_width), jnp.bfloat16)
        empty_right = jnp.zeros((local_sequences, outer_width, local_rows), jnp.bfloat16)
        return (bias_rows, tri_input, empty_query, empty_keys, empty_query, empty_left, empty_right)

    bias_local, tri_input, query, key_values, gate, left, right_cols = lax.cond(
        alignment_branch, alignment_early, pair_early
    )
    bias_recv = shifted(bias_local, "branch", -1)
    query_heads = query.reshape(local_sequences, local_rows, head_total, head_size).transpose(
        0, 2, 1, 3
    )

    def fold_real(running, shard_part):
        highest, totals, weighted = running
        columns = shard_part.shape[2]
        keys_part = shard_part[:, :latent_heads].reshape(
            local_sequences, head_total, head_size, columns
        )
        values_part = shard_part[:, latent_heads:].reshape(
            local_sequences, head_total, head_size, columns
        )
        bias_part = bias_recv.astype(jnp.float32)
        scores = (
            jnp.einsum(
                "shid,shdj->shij", query_heads, keys_part, preferred_element_type=jnp.float32
            )
            + bias_part[None]
        )
        raised = jnp.maximum(highest, jnp.max(scores, axis=3))
        weights = jnp.exp(scores - raised[..., None])
        totals = jnp.sum(weights, axis=3)
        weighted = jnp.einsum(
            "shij,shdj->shid",
            weights.astype(jnp.bfloat16),
            values_part,
            preferred_element_type=jnp.float32,
        )
        return (raised, totals, weighted)

    initial = (
        jnp.full((local_sequences, head_total, local_rows), -1e30, jnp.float32),
        jnp.zeros((local_sequences, head_total, local_rows), jnp.float32),
        jnp.zeros((local_sequences, head_total, local_rows, head_size), jnp.float32),
    )
    shard_part = lax.all_gather(key_values, "row", axis=2, tiled=True)
    highest, totals, weighted = lax.cond(
        alignment_branch, lambda: fold_real(initial, shard_part), lambda: initial
    )
    safe_totals = jnp.where(totals > 0, totals, 1.0)
    attended = (weighted / safe_totals[..., None]).transpose(0, 2, 1, 3).reshape(query_shape)
    mixed_heads = (gate.astype(jnp.float32) * attended).astype(jnp.bfloat16)
    right_full = lax.all_gather(right_cols, "row", axis=2, tiled=True)
    right_matrix = right_full.reshape(local_sequences * outer_width, residues)
    spread = lax.cond(
        alignment_branch,
        lambda: jnp.einsum(
            "sic,cdo->oisd", left, outer_output_weight, preferred_element_type=jnp.float32
        ).astype(jnp.bfloat16),
        lambda: jnp.zeros((pair_width, local_rows, local_sequences, outer_width), jnp.bfloat16),
    )

    def outer_term(amount):
        spread_part = spread.reshape(amount * local_rows, local_sequences * outer_width)
        return jnp.dot(spread_part, right_matrix, preferred_element_type=jnp.float32).reshape(
            amount, local_rows, residues
        )

    tri_flat = tri_input.reshape(pair_width, -1)

    def pair_operands():
        linear = jnp.dot(
            triangle_input_weight.reshape(4 * tri_local, pair_width),
            tri_flat,
            preferred_element_type=jnp.float32,
        )
        linear = linear.reshape(4, tri_local, local_rows, residues)
        left_part = (linear[0] * jax.nn.sigmoid(linear[1])).astype(jnp.bfloat16)
        right_part = (linear[2] * jax.nn.sigmoid(linear[3])).astype(jnp.bfloat16)
        return (left_part, right_part)

    def empty_operands():
        empty = jnp.zeros((tri_local, local_rows, residues), jnp.bfloat16)
        return (empty, empty)

    left_tri, right_tri = lax.cond(alignment_branch, empty_operands, pair_operands)
    tri_shard_part = lax.all_gather(right_tri, "row", axis=1, tiled=True)
    triangle = lax.optimization_barrier(
        lax.cond(
            alignment_branch,
            lambda: jnp.zeros((tri_local, local_rows, tri_shard_part.shape[1]), jnp.float32),
            lambda: jnp.einsum(
                "cik,cjk->cij", left_tri, tri_shard_part, preferred_element_type=jnp.float32
            ),
        ).astype(jnp.bfloat16)
    )
    tri_float = triangle.astype(jnp.float32)
    summed, squared = lax.psum(
        (jnp.sum(tri_float, axis=0), jnp.sum(tri_float * tri_float, axis=0)), "seq"
    )
    tri_total = tri_local * lax.axis_size("seq")
    average = summed / tri_total
    variance = jnp.maximum(squared / tri_total - average * average, 0.0)
    tri_norm = (
        (tri_float - average) * lax.rsqrt(variance + EPSILON) * triangle_gain[:, None, None]
    ).astype(jnp.bfloat16)
    norm_flat = tri_norm.reshape(tri_local, -1)

    def tri_term(amount):
        return jnp.dot(
            triangle_output_weight, norm_flat, preferred_element_type=jnp.float32
        ).reshape(amount, local_rows, residues)

    def first_term(offset, amount):
        return lax.cond(alignment_branch, lambda: outer_term(amount), lambda: tri_term(amount))

    summed_first = channel_sum(first_term, chan_local)
    outer_increment = (summed_first * (1.0 / seq_total)).astype(jnp.bfloat16)
    gate_values = jax.nn.sigmoid(
        jnp.dot(triangle_gate_weight, tri_flat, preferred_element_type=jnp.float32)
    ).reshape(pair_shape)
    first_update = lax.optimization_barrier(
        (pairwise_input.astype(jnp.float32) + gate_values * summed_first).astype(jnp.bfloat16)
    )
    gathered_next = full_channels(first_update)

    def pair_hidden():
        trans_norm = (
            (layer_normalize(gathered_next.astype(jnp.float32), 0) * transition_gain[:, None, None])
            .astype(jnp.bfloat16)
            .reshape(pair_width, -1)
        )
        return jax.nn.relu(
            jnp.dot(transition_up_weight, trans_norm, preferred_element_type=jnp.float32)
        ).astype(jnp.bfloat16)

    hidden_units = lax.cond(
        alignment_branch,
        lambda: jnp.zeros((trans_local, local_rows * residues), jnp.bfloat16),
        pair_hidden,
    )

    def trans_real(amount):
        return jnp.dot(
            transition_down_weight, hidden_units, preferred_element_type=jnp.float32
        ).reshape(amount, local_rows, residues)

    def trans_term(offset, amount):
        return lax.cond(
            alignment_branch,
            lambda: jnp.zeros((amount, local_rows, residues), jnp.float32),
            lambda: trans_real(amount),
        )

    pair_following = (
        first_update.astype(jnp.float32) + channel_sum(trans_term, chan_local)
    ).astype(jnp.bfloat16)
    half_residues = residues // 2
    halved_width = alignment_channels // 2
    outgoing_product = jnp.where(
        alignment_branch,
        outer_increment[:, :, half_residues:],
        pair_following[:, :, :half_residues],
    )
    incoming = from_partner(outgoing_product, "branch", 0)
    local_half = jnp.where(
        alignment_branch,
        outer_increment[:, :, :half_residues],
        pair_following[:, :, half_residues:],
    )
    pairwise_output = (local_half.astype(jnp.float32) + incoming.astype(jnp.float32)).astype(
        jnp.bfloat16
    )
    mixed_received = shifted(mixed_heads, "branch", 1)
    mixed_applied = jnp.where(alignment_branch, mixed_heads, mixed_received)
    mix_columns = lax.dynamic_slice_in_dim(
        mixing_weight, path_index * halved_width, halved_width, 1
    )
    residual_stream = lax.dynamic_slice_in_dim(
        alignment_input, path_index * halved_width, halved_width, 2
    )
    projected_values = jnp.dot(
        mixed_applied.reshape(-1, latent_heads), mix_columns, preferred_element_type=jnp.float32
    )
    alignment_output = (
        residual_stream.astype(jnp.float32)
        + projected_values.reshape(local_sequences, local_rows, halved_width)
    ).astype(jnp.bfloat16)
    return (alignment_output, pairwise_output)


BIAS_COST = 175 * 10**6


def rounded(values):
    return values.astype(jnp.bfloat16)


def widened(values):
    return values.astype(jnp.float32)


def product(left, right, contract_left=1, contract_right=0):
    return lax.dot_general(
        left,
        right,
        (((contract_left,), (contract_right,)), ((), ())),
        preferred_element_type=jnp.float32,
    )


def group_maximum(values, group):
    tiles = []
    for start in range(0, values.shape[1], 128):
        tile = values[:, start : start + 128]
        lane = lax.broadcasted_iota(jnp.int32, tile.shape, 1)
        step = 1
        while step < group:
            ahead = pltpu.roll(tile, 128 - step, 1)
            behind = pltpu.roll(tile, step, 1)
            tile = jnp.maximum(tile, jnp.where((lane & step) == 0, ahead, behind))
            step *= 2
        tiles.append(tile)
    return jnp.concatenate(tiles, axis=1)


def same_group(rows, columns, group):
    row = lax.broadcasted_iota(jnp.int32, (rows, columns), 0) // group
    column = lax.broadcasted_iota(jnp.int32, (rows, columns), 1) // group
    return row == column


def as_column(row):
    size = row.shape[1]
    return jnp.sum(jnp.where(same_group(size, size, 1), row, 0.0), axis=1, keepdims=True)


def kernel_call(body, outputs, operands, scratch=(), flops=0, in_hbm=(), room=32 * 2**20):
    vmem = pl.BlockSpec(memory_space=pltpu.VMEM)
    hbm = pl.BlockSpec(memory_space=pltpu.HBM)
    size = sum(a.size * a.dtype.itemsize for a in operands)
    size += sum(o.size * o.dtype.itemsize for o in outputs)
    return pl.pallas_call(
        body,
        out_shape=outputs,
        in_specs=[hbm if i in in_hbm else vmem for i in range(len(operands))],
        out_specs=[vmem] * len(outputs),
        scratch_shapes=list(scratch),
        cost_estimate=pl.CostEstimate(flops=flops, bytes_accessed=size, transcendentals=0),
        compiler_params=pltpu.CompilerParams(vmem_limit_bytes=room),
    )(*operands)


def exchange(value, axes, distance):
    members = lax.axis_size(axes)
    return lax.ppermute(value, axes, [(i, i ^ distance) for i in range(members)])


def start_kernel(token_ref):
    token_ref[...] = jnp.zeros_like(token_ref)


def send_kernel(
    sizes, rows_ref, pair_ref, gain_ref, weight_ref, input_ref, gate_ref, tri_gain_ref, output_ref, up_ref,
    down_ref, token_ref, same_ref, other_ref, shared_ref, flat_ref, wide,
):
    sequences, local_rows, residues, chan_local, outer_width = sizes
    part = sequences // 4
    part_rows = part * local_rows
    pair = widened(pair_ref[...])
    flat_pair = rounded(jnp.concatenate([pair[:, i, :] for i in range(local_rows)], axis=1))
    flat_ref[...] = flat_pair
    shared_ref[0:chan_local, :] = flat_pair
    at = chan_local + sequences
    narrow = gate_ref.shape[1]
    scaled = rounded(widened(output_ref[...]) * as_column(tri_gain_ref[...]))
    kinds = [input_ref[kind] for kind in range(input_ref.shape[0])]
    down = down_ref[...]
    for block in (*kinds, gate_ref[...], scaled, down[:chan_local]):
        shared_ref[at : at + chan_local, :narrow] = block
        at += chan_local
    at = chan_local + sequences
    for block in (up_ref[...], down[chan_local:]):
        shared_ref[at : at + block.shape[0], narrow:] = block
        at += block.shape[0]
    same_ref[part_rows : part_rows + chan_local, :] = flat_pair
    other_ref[part_rows : part_rows + chan_local, :] = flat_pair
    unit_here = 2 * lax.axis_index("branch") + lax.rem(lax.axis_index("row"), 2)
    unit_other = 2 * lax.axis_index("branch") + 1 - lax.rem(lax.axis_index("row"), 2)
    same_ref[0:part_rows, :] = rows_ref[pl.ds(unit_here * part_rows, part_rows), :]
    other_ref[0:part_rows, :] = rows_ref[pl.ds(unit_other * part_rows, part_rows), :]
    normed = rounded(layer_normalize(widened(rows_ref[...]), 1) * gain_ref[...])
    wide[:, 0 : 2 * outer_width] = product(normed, weight_ref[...], 1, 1)
    base = part_rows + chan_local
    for i in range(local_rows):
        both = rounded(wide[pl.ds(i, sequences, stride=local_rows), :])
        lanes = slice(i * outer_width, (i + 1) * outer_width)
        shared_ref[chan_local : chan_local + sequences, lanes] = both[:, :outer_width]
        same_ref[base : base + sequences, lanes] = both[:, outer_width : 2 * outer_width]
    other_ref[base : base + sequences, :] = same_ref[base : base + sequences, :]


def keep_kernel(*refs):
    count = len(refs) // 2
    for source, target in zip(refs[:count], refs[count:]):
        target[...] = source[...]


def relay_kernel(sizes, own_ref, one_ref, two_ref, three_ref, after_bias_ref, after_keep_ref, relay_ref):
    sequences, local_rows, residues, chan_local, outer_width = sizes
    part_rows = sequences // 4 * local_rows
    row = lax.axis_index("row")
    branch = lax.axis_index("branch")
    base = part_rows + chan_local
    for distance, ref in enumerate((own_ref, one_ref, two_ref, three_ref)):
        shard = row ^ distance

        @pl.when(shard // 2 == branch)
        def _():
            place = lax.rem(shard, 2)
            relay_ref[pl.ds(pl.multiple_of(place * chan_local, chan_local), chan_local), :] = ref[
                part_rows:base, :
            ]
            start = 2 * chan_local + place * sequences
            relay_ref[pl.ds(pl.multiple_of(start, chan_local), sequences), :] = ref[
                base : base + sequences, :
            ]


def score_kernel(
    sizes, own_ref, one_ref, two_ref, three_ref, gain_ref, weight_ref, *refs,
):
    score_ref, values_ref, gate_ref, module = refs[-4:]
    sequences, local_rows, residues, chan_local, outer_width = sizes
    part = sequences // 4
    part_rows = part * local_rows
    width = gain_ref.shape[1]
    head_size = 32
    row = lax.axis_index("row")
    for distance, ref in enumerate((own_ref, one_ref, two_ref, three_ref)):
        shard = row ^ distance
        block = widened(ref[0:part_rows, :])
        unit = layer_normalize(block, 1) * gain_ref[...]
        module[:, pl.ds(pl.multiple_of(shard * local_rows, local_rows), local_rows), :] = unit.reshape(
            part, local_rows, width
        )
    normed = rounded(module[...].reshape(part * residues, width))
    half = residues // 2
    here = module[:, pl.ds(pl.multiple_of(row // 2 * half, half), half), :]
    query_rows = rounded(here.reshape(part * half, width))
    heads = values_ref.shape[1]
    query = rounded(product(query_rows, weight_ref[:, 0:heads]) * head_size ** (-0.5))
    keys = rounded(product(normed, weight_ref[:, heads : 2 * heads]))
    values_ref[...] = rounded(product(normed, weight_ref[:, 2 * heads : 3 * heads]))
    gate_ref[...] = rounded(jax.nn.sigmoid(product(query_rows, weight_ref[:, 3 * heads :])))
    groups = heads // head_size
    mask = same_group(groups * residues, heads, head_size)
    for s in range(part):
        one = keys[s * residues : (s + 1) * residues]
        spread = jnp.where(mask, jnp.concatenate([one] * groups, axis=0), jnp.bfloat16(0))
        score_ref[s * half : (s + 1) * half, :] = product(
            query[s * half : (s + 1) * half], spread, 1, 1
        )


def bias_kernel(chan_local, pair_refs, matrix_ref, bias_ref, full, flat):
    groups = matrix_ref.shape[0]
    residues = flat.shape[1] // groups
    local_rows = flat.shape[0]
    seq = lax.axis_index("seq")
    for distance, ref in zip((0, 2, 1, 3), pair_refs):
        place = pl.ds(pl.multiple_of((seq ^ distance) * chan_local, chan_local), chan_local)
        full[place, :] = widened(ref[0:chan_local, :])
    plain = rounded(layer_normalize(full[...], 0))
    bias = product(matrix_ref[...], plain)
    for i in range(local_rows):
        for h in range(groups):
            flat[i : i + 1, h * residues : (h + 1) * residues] = bias[
                h : h + 1, i * residues : (i + 1) * residues
            ]
    rows = rounded(flat[...])
    bias_ref[...] = jnp.concatenate([rows, rows], axis=0)


def mix_kernel(
    sizes, near_bias_ref, far_bias_ref, score_ref, values_ref, gate_ref, mixing_ref, own_ref, one_ref, *refs,
):
    near_here_ref, near_there_ref, far_here_ref, far_there_ref, module = refs[-5:]
    sequences, local_rows, residues, chan_local, outer_width = sizes
    part = sequences // 4
    part_rows = part * local_rows
    half = residues // 2
    heads = values_ref.shape[1]
    head_size = 32
    groups = heads // head_size
    row = lax.axis_index("row")
    branch = lax.axis_index("branch")
    first = lax.broadcasted_iota(jnp.int32, near_bias_ref.shape, 0) // local_rows == lax.rem(row, 2)
    bias_rows = jnp.where(first, widened(near_bias_ref[...]), widened(far_bias_ref[...]))
    scores = (
        score_ref[...].reshape(part, half, groups * residues) + bias_rows[None]
    ).reshape(part * half, groups * residues)
    weights = rounded(jnp.exp(scores - group_maximum(scores, residues)))
    mask = same_group(groups * residues, heads, head_size)
    ones = jnp.where(mask, jnp.bfloat16(1), jnp.bfloat16(0))
    totals = product(weights, ones)
    attended = []
    for s in range(part):
        one = values_ref[s * residues : (s + 1) * residues, :]
        spread = jnp.where(mask, jnp.concatenate([one] * groups, axis=0), jnp.bfloat16(0))
        attended.append(product(weights[s * half : (s + 1) * half], spread))
    mixed = rounded(widened(gate_ref[...]) * (jnp.concatenate(attended, axis=0) / totals))
    projected = product(mixed, mixing_ref[...])
    width = projected.shape[1]
    module[...] = projected.reshape(part, half, width)
    halved = width // 2
    for distance, ref, here, there in (
        (0, own_ref, near_here_ref, near_there_ref),
        (1, one_ref, far_here_ref, far_there_ref),
    ):
        place = lax.rem(row, 2) ^ distance
        update = module[:, pl.ds(pl.multiple_of(place * local_rows, local_rows), local_rows), :]
        result = rounded(widened(ref[0:part_rows, :]) + update.reshape(part_rows, width))
        low, high = result[:, :halved], result[:, halved:]
        here[...] = jnp.where(branch == 0, low, high)
        there[...] = jnp.where(branch == 0, high, low)


def place_kernel(own_ref, branch_ref, row_ref, both_ref, pair_ref, output_ref, pair_output_ref):
    pair_output_ref[...] = pair_ref[...]
    rows = own_ref.shape[0]
    branch = lax.axis_index("branch")
    parity = lax.rem(lax.axis_index("row"), 2)
    for flip_branch, flip_row, ref in (
        (0, 0, own_ref),
        (1, 0, branch_ref),
        (0, 1, row_ref),
        (1, 1, both_ref),
    ):
        unit = 2 * (branch ^ flip_branch) + (parity ^ flip_row)
        output_ref[pl.ds(pl.multiple_of(unit * rows, rows), rows), :] = ref[...]


def pair_kernel(
    sizes, shared_refs, pair_refs, gain_ref, transition_gain_ref, outer_weight_ref, seq_total, hidden_local,
    output_ref, rows, columns, gates, outer, outer_flat, ordered, final,
):
    sequences, local_rows, residues, chan_local, outer_width = sizes
    half = residues // 2
    branch = lax.axis_index("branch")
    seq = lax.axis_index("seq")
    width = 4 * chan_local
    chan = chan_local
    gain = as_column(gain_ref[...])
    at = chan + sequences
    weight_refs = [ref.at[at:, 0:width] for ref in shared_refs]
    hidden_refs = [ref.at[at:, width:] for ref in shared_refs]
    for distance, row_ref, pair_ref, weight_ref in zip((0, 2, 1, 3), shared_refs, pair_refs, weight_refs):
        place = pl.ds(pl.multiple_of((seq ^ distance) * chan, chan), chan)
        rows[place, :] = row_ref[0:chan, :]
        for k in range(2):
            columns[k, place, :] = pair_ref[k * chan : (k + 1) * chan, :]
        gates[place, :] = weight_ref[4 * chan : 5 * chan, :]

    def projection(values, kind):
        weights = jnp.concatenate([w[kind * chan : (kind + 1) * chan, :] for w in weight_refs], axis=0)
        return product(values, weights, 1, 1)

    raw = widened(rows[...])
    row_input = rounded((layer_normalize(raw, 0) * gain).T)
    left = widened(
        rounded(projection(row_input, 0) * jax.nn.sigmoid(projection(row_input, 1)))
    ).reshape(local_rows, residues, width)
    right = []
    for k in range(2):
        column_input = rounded((layer_normalize(widened(columns[k]), 0) * gain).T)
        right.append(
            widened(
                rounded(projection(column_input, 2) * jax.nn.sigmoid(projection(column_input, 3)))
            ).reshape(local_rows, residues, width)
        )
    right = jnp.concatenate(right, axis=0)
    triangle = jnp.concatenate(
        [jnp.sum(left[i][None] * right, axis=1) for i in range(local_rows)], axis=0
    )
    triangle = widened(rounded(triangle))
    tri_norm = rounded(layer_normalize(triangle, 1))
    output_weight = jnp.concatenate([w[5 * chan : 6 * chan, :] for w in weight_refs], axis=0)
    tri_out = product(tri_norm, output_weight)
    ordered[...] = raw.T.reshape(local_rows, residues, width)
    place = pl.ds(pl.multiple_of(branch * half, half), half)
    raw_here = ordered[:, place, :].reshape(local_rows * half, width)
    ordered[...] = widened(row_input).reshape(local_rows, residues, width)
    input_here = rounded(ordered[:, place, :].reshape(local_rows * half, width))
    gate = jax.nn.sigmoid(product(input_here, gates[...], 1, 1))
    first_update = widened(rounded(raw_here + gate * tri_out))
    trans_norm = rounded(layer_normalize(first_update, 1) * transition_gain_ref[...])
    down = jnp.zeros((local_rows * half, width), jnp.float32)
    for w, h in zip(weight_refs, hidden_refs):
        hidden = rounded(jax.nn.relu(product(trans_norm, h[0:hidden_local, :], 1, 1)))
        down_weight = jnp.concatenate([w[6 * chan : 7 * chan, :], h[hidden_local : hidden_local + 3 * chan, :]], axis=0)
        down += product(hidden, down_weight, 1, 1)
    pair_next = widened(rounded(first_update + down))

    lefts = jnp.concatenate([ref[chan : chan + sequences, :] for ref in shared_refs], axis=0)
    base = 2 * chan
    rights = jnp.concatenate(
        [
            jnp.concatenate([p[base : base + sequences, :], p[base + sequences :, :]], axis=1)
            for p in pair_refs
        ],
        axis=0,
    )
    outer_all = product(rounded(widened(lefts).T), rights)
    each = 128 // outer_width
    for tile in range(half // each):
        outer[tile] = outer_all[:, tile * 128 : (tile + 1) * 128]
        for c in range(outer_width):
            strip = outer[tile, pl.ds(c, local_rows, stride=outer_width), :]
            for k in range(each):
                j = tile * each + k
                outer_flat[
                    j * local_rows : (j + 1) * local_rows, c * outer_width : (c + 1) * outer_width
                ] = strip[:, k * outer_width : (k + 1) * outer_width]
    final[...] = product(rounded(outer_flat[...]), outer_weight_ref[...]) * (1.0 / seq_total)
    outer_update = jnp.concatenate(
        [final[pl.ds(i, half, stride=local_rows), :] for i in range(local_rows)], axis=0
    )
    outer_update = widened(rounded(outer_update))
    result = pair_next + outer_update
    own = result[:, 0:chan]
    for k in range(1, 4):
        own = jnp.where(seq == k, result[:, k * chan : (k + 1) * chan], own)
    output_ref[...] = rounded(own)


def compact_shards(
    alignment_input, pairwise_input, alignment_gain, product_gain, attention_weight, mixing_weight,
    outer_input_weight, outer_output_weight, bias_matrix, pairwise_gain, triangle_input_weight,
    triangle_gate_weight, triangle_gain, triangle_output_weight, transition_gain,
    transition_up_weight, transition_down_weight,
):
    sequences, local_rows, width = alignment_input.shape
    chan_local, _, residues = pairwise_input.shape
    pair_width, groups = bias_matrix.shape
    heads = mixing_weight.shape[0]
    outer_width = outer_input_weight.shape[2]
    part = sequences // 4
    part_rows = part * local_rows
    half = residues // 2
    sizes = (sequences, local_rows, residues, chan_local, outer_width)
    half_type, full_type = jnp.bfloat16, jnp.float32

    def shape(*dims, dtype=half_type):
        return jax.ShapeDtypeStruct(dims, dtype)

    rows_flat = alignment_input.reshape(sequences * local_rows, width)
    message_rows = part_rows + chan_local + sequences
    outer_weight_flat = outer_input_weight.transpose(1, 2, 0).reshape(2 * outer_width, width)
    (token,) = kernel_call(start_kernel, [shape(8, 128, dtype=full_type)], [], flops=5 * 10**9)
    hidden_local = transition_up_weight.shape[0]
    shared_rows = chan_local + sequences + 7 * chan_local
    same, other, shared, pair_flat = kernel_call(
        functools.partial(send_kernel, sizes),
        [shape(message_rows, width), shape(message_rows, width),
         shape(shared_rows, width), shape(chan_local, local_rows * residues)],
        [rows_flat, pairwise_input, product_gain[None], outer_weight_flat, triangle_input_weight,
         triangle_gate_weight, triangle_gain[None], triangle_output_weight.T, transition_up_weight,
         transition_down_weight, token],
        [pltpu.VMEM((sequences * local_rows, 128), full_type)],
    )
    shared_x = exchange(shared, "seq", 2)
    shared_core = exchange(shared, "seq", 1)
    shared_both = exchange(shared_x, "seq", 1)
    shareds = (shared, shared_x, shared_core, shared_both)
    from_three = exchange(other, "row", 3)
    from_two = exchange(same, "row", 2)
    from_one = exchange(other, "row", 1)
    received = (same, from_one, from_two, from_three)

    pair_core = exchange(pair_flat, "seq", 1)
    pair_both = exchange(shared_x[0:chan_local], "seq", 1)
    pairs = (shared, shared_x, pair_core, pair_both)


    late_weight = lax.optimization_barrier((attention_weight, pair_flat))[0]
    kept = [late_weight.reshape(width, 4 * heads), mixing_weight,
            outer_output_weight.reshape(outer_width * outer_width, pair_width),
            alignment_gain[None], pairwise_gain[None], transition_gain[None]]
    attention_kept, mixing_kept, outer_kept, row_gain, pair_gain, last_gain = kernel_call(
        keep_kernel, [shape(*a.shape, dtype=a.dtype) for a in kept], kept
    )

    def bias_body(*refs):
        bias_kernel(chan_local, refs[:4], *refs[4:])

    (near_bias,) = kernel_call(
        bias_body,
        [shape(half, groups * residues)],
        [*pairs, bias_matrix.T],
        [
            pltpu.VMEM((pair_width, local_rows * residues), full_type),
            pltpu.VMEM((local_rows, groups * residues), full_type),
        ],
        flops=BIAS_COST,
    )
    far_bias = exchange(near_bias, "row", 1)

    (relay,) = kernel_call(
        functools.partial(relay_kernel, sizes),
        [shape(2 * chan_local + 2 * sequences, width)],
        [*received, far_bias, row_gain],
    )
    relay_x = exchange(relay, "seq", 2)
    relay_core = exchange(relay, "seq", 1)
    relay_both = exchange(relay, "seq", 3)
    relays = (relay, relay_x, relay_core, relay_both)

    scores, values, gate = kernel_call(
        functools.partial(score_kernel, sizes),
        [shape(part * half, groups * residues, dtype=full_type), shape(part * residues, heads), shape(part * half, heads)],
        [*received, row_gain, attention_kept, relay],
        [pltpu.VMEM((part, residues, width), full_type)],
        flops=3 * 10**9,
    )

    near_here, near_there, far_here, far_there = kernel_call(
        functools.partial(mix_kernel, sizes),
        [shape(part_rows, width // 2)] * 4,
        [near_bias, far_bias, scores, values, gate, mixing_kept, same, from_one, shared_core, shared_both],
        [pltpu.VMEM((part, half, width), full_type)],
        flops=3 * 10**9,
    )
    axes = ("branch", "row")
    across = lax.axis_size("row")
    from_branch = exchange(near_there, axes, across)
    from_both = exchange(far_there, axes, across + 1)
    from_row = exchange(far_here, axes, 1)

    def pair_body(*refs):
        pair_kernel(sizes, refs[:4], refs[4:8], *refs[8:11], sequences * 4, hidden_local, *refs[11:])

    (pair_done,) = kernel_call(
        pair_body,
        [shape(local_rows * half, chan_local)],
        [*shareds, *relays, pair_gain, last_gain, outer_kept],
        [
            pltpu.VMEM((pair_width, local_rows * residues), half_type),
            pltpu.VMEM((2, pair_width, local_rows * residues), half_type),
            pltpu.VMEM((pair_width, pair_width), half_type),
            pltpu.VMEM((half * outer_width // 128, local_rows * outer_width, 128), full_type),
            pltpu.VMEM((local_rows * half, outer_width * outer_width), full_type),
            pltpu.VMEM((local_rows, residues, pair_width), full_type),
            pltpu.VMEM((local_rows * half, pair_width), full_type),
        ],
    )
    alignment_flat, pairwise_output = kernel_call(
        place_kernel,
        [shape(sequences * local_rows, width // 2), shape(local_rows * half, chan_local)],
        [near_here, from_branch, from_row, from_both, pair_done],
    )
    return (
        alignment_flat.reshape(sequences, local_rows, width // 2),
        pairwise_output.reshape(local_rows, half, chan_local).transpose(2, 0, 1),
    )


def is_compact(mesh, residues):
    return mesh.shape["row"] == 4 and mesh.shape["seq"] == 4 and mesh.shape["branch"] == 2


def solution(mesh):
    return jax.shard_map(
        compact_shards if is_compact(mesh, None) else shards,
        mesh=mesh,
        in_specs=(
            P("seq", "row", None),
            P("seq", "row", None),
            P(),
            P(),
            P(),
            P(),
            P(),
            P(),
            P(),
            P(),
            P(None, "seq", None),
            P("seq", None),
            P("seq"),
            P(None, "seq"),
            P(),
            P("seq", None),
            P(None, "seq"),
        ),
        out_specs=(P("seq", "row", "branch"), P("seq", "row", "branch")),
        check_vma=False,
    )
```

```python
import functools

import jax
import jax.numpy as jnp
from jax import lax
from jax.experimental import pallas as pl
from jax.experimental.pallas import tpu as pltpu
from jax.sharding import PartitionSpec as P

EPSILON = 1e-05


def shifted(value, axis, by):
    length = lax.axis_size(axis)
    pairs = [(i, i + by) for i in range(length) if 0 <= i + by < length]
    return lax.ppermute(value, axis, pairs)


def from_partner(value, axis, distance):
    return lax.ppermute(value, axis, [(i, i ^ 1 << distance) for i in range(lax.axis_size(axis))])


def layer_normalize(values, axis):
    average = jnp.mean(values, axis=axis, keepdims=True)
    centred = values - average
    spread = jnp.mean(centred * centred, axis=axis, keepdims=True)
    return centred * lax.rsqrt(spread + EPSILON)


def full_channels(values):
    return lax.all_gather(values, "seq", axis=0, tiled=True)


def channel_sum(term, kept_rows):
    return lax.psum_scatter(
        term(jnp.int32(0), kept_rows * lax.axis_size("seq")), "seq", scatter_dimension=0, tiled=True
    )


def shards(
    alignment_input,
    pairwise_input,
    alignment_gain,
    product_gain,
    attention_weight,
    mixing_weight,
    outer_input_weight,
    outer_output_weight,
    bias_matrix,
    pairwise_gain,
    triangle_input_weight,
    triangle_gate_weight,
    triangle_gain,
    triangle_output_weight,
    transition_gain,
    transition_up_weight,
    transition_down_weight,
):
    local_sequences, local_rows, alignment_channels = alignment_input.shape
    chan_local = pairwise_input.shape[0]
    residues = pairwise_input.shape[2]
    pair_width, head_total = bias_matrix.shape
    latent_heads = mixing_weight.shape[0]
    head_size = latent_heads // head_total
    outer_width = outer_input_weight.shape[2]
    tri_local = triangle_input_weight.shape[1]
    trans_local = transition_up_weight.shape[0]
    seq_total = local_sequences * lax.axis_size("seq")
    path_index = lax.axis_index("branch")
    alignment_branch = path_index == 0
    query_shape = (local_sequences, local_rows, latent_heads)
    pair_shape = (chan_local, local_rows, residues)
    full_pair_shape = (pair_width, local_rows, residues)
    key_shape = (local_sequences, 2 * latent_heads, local_rows)
    gathered = full_channels(pairwise_input)

    def alignment_early():
        alignment_module = layer_normalize(alignment_input.astype(jnp.float32), 2)
        normalized_values = (alignment_module * alignment_gain).astype(jnp.bfloat16)
        outer_normalized = (alignment_module * product_gain).astype(jnp.bfloat16)
        flattened_rows = normalized_values.reshape(-1, alignment_channels)
        outer_flattened = outer_normalized.reshape(-1, alignment_channels)
        query = (
            (
                jnp.dot(flattened_rows, attention_weight[:, 0], preferred_element_type=jnp.float32)
                * head_size ** (-0.5)
            )
            .astype(jnp.bfloat16)
            .reshape(query_shape)
        )
        gate = (
            jax.nn.sigmoid(
                jnp.dot(flattened_rows, attention_weight[:, 3], preferred_element_type=jnp.float32)
            )
            .astype(jnp.bfloat16)
            .reshape(query_shape)
        )
        key_values = (
            jnp.einsum(
                "sim,mkc->skci",
                normalized_values,
                attention_weight[:, 1:3],
                preferred_element_type=jnp.float32,
            )
            .astype(jnp.bfloat16)
            .reshape(key_shape)
        )
        left = (
            jnp.dot(outer_flattened, outer_input_weight[:, 0], preferred_element_type=jnp.float32)
            .astype(jnp.bfloat16)
            .reshape(local_sequences, local_rows, outer_width)
        )
        right_cols = jnp.einsum(
            "sim,mc->sci",
            outer_normalized,
            outer_input_weight[:, 1],
            preferred_element_type=jnp.float32,
        ).astype(jnp.bfloat16)
        empty_bias = jnp.zeros((head_total, local_rows, residues), jnp.bfloat16)
        empty_pair = jnp.zeros(full_pair_shape, jnp.bfloat16)
        return (empty_bias, empty_pair, query, key_values, gate, left, right_cols)

    def pair_early():
        unit = layer_normalize(gathered.astype(jnp.float32), 0)
        plain = unit.astype(jnp.bfloat16).reshape(pair_width, -1)
        bias_rows = (
            jnp.einsum("ch,cn->hn", bias_matrix, plain, preferred_element_type=jnp.float32)
            .astype(jnp.bfloat16)
            .reshape(head_total, local_rows, residues)
        )
        tri_input = (unit * pairwise_gain[:, None, None]).astype(jnp.bfloat16)
        empty_query = jnp.zeros(query_shape, jnp.bfloat16)
        empty_keys = jnp.zeros(key_shape, jnp.bfloat16)
        empty_left = jnp.zeros((local_sequences, local_rows, outer_width), jnp.bfloat16)
        empty_right = jnp.zeros((local_sequences, outer_width, local_rows), jnp.bfloat16)
        return (bias_rows, tri_input, empty_query, empty_keys, empty_query, empty_left, empty_right)

    bias_local, tri_input, query, key_values, gate, left, right_cols = lax.cond(
        alignment_branch, alignment_early, pair_early
    )
    bias_recv = shifted(bias_local, "branch", -1)
    query_heads = query.reshape(local_sequences, local_rows, head_total, head_size).transpose(
        0, 2, 1, 3
    )

    def fold_real(running, shard_part):
        highest, totals, weighted = running
        columns = shard_part.shape[2]
        keys_part = shard_part[:, :latent_heads].reshape(
            local_sequences, head_total, head_size, columns
        )
        values_part = shard_part[:, latent_heads:].reshape(
            local_sequences, head_total, head_size, columns
        )
        bias_part = bias_recv.astype(jnp.float32)
        scores = (
            jnp.einsum(
                "shid,shdj->shij", query_heads, keys_part, preferred_element_type=jnp.float32
            )
            + bias_part[None]
        )
        raised = jnp.maximum(highest, jnp.max(scores, axis=3))
        weights = jnp.exp(scores - raised[..., None])
        totals = jnp.sum(weights, axis=3)
        weighted = jnp.einsum(
            "shij,shdj->shid",
            weights.astype(jnp.bfloat16),
            values_part,
            preferred_element_type=jnp.float32,
        )
        return (raised, totals, weighted)

    initial = (
        jnp.full((local_sequences, head_total, local_rows), -1e30, jnp.float32),
        jnp.zeros((local_sequences, head_total, local_rows), jnp.float32),
        jnp.zeros((local_sequences, head_total, local_rows, head_size), jnp.float32),
    )
    shard_part = lax.all_gather(key_values, "row", axis=2, tiled=True)
    highest, totals, weighted = lax.cond(
        alignment_branch, lambda: fold_real(initial, shard_part), lambda: initial
    )
    safe_totals = jnp.where(totals > 0, totals, 1.0)
    attended = (weighted / safe_totals[..., None]).transpose(0, 2, 1, 3).reshape(query_shape)
    mixed_heads = (gate.astype(jnp.float32) * attended).astype(jnp.bfloat16)
    right_full = lax.all_gather(right_cols, "row", axis=2, tiled=True)
    right_matrix = right_full.reshape(local_sequences * outer_width, residues)
    spread = lax.cond(
        alignment_branch,
        lambda: jnp.einsum(
            "sic,cdo->oisd", left, outer_output_weight, preferred_element_type=jnp.float32
        ).astype(jnp.bfloat16),
        lambda: jnp.zeros((pair_width, local_rows, local_sequences, outer_width), jnp.bfloat16),
    )

    def outer_term(amount):
        spread_part = spread.reshape(amount * local_rows, local_sequences * outer_width)
        return jnp.dot(spread_part, right_matrix, preferred_element_type=jnp.float32).reshape(
            amount, local_rows, residues
        )

    tri_flat = tri_input.reshape(pair_width, -1)

    def pair_operands():
        linear = jnp.dot(
            triangle_input_weight.reshape(4 * tri_local, pair_width),
            tri_flat,
            preferred_element_type=jnp.float32,
        )
        linear = linear.reshape(4, tri_local, local_rows, residues)
        left_part = (linear[0] * jax.nn.sigmoid(linear[1])).astype(jnp.bfloat16)
        right_part = (linear[2] * jax.nn.sigmoid(linear[3])).astype(jnp.bfloat16)
        return (left_part, right_part)

    def empty_operands():
        empty = jnp.zeros((tri_local, local_rows, residues), jnp.bfloat16)
        return (empty, empty)

    left_tri, right_tri = lax.cond(alignment_branch, empty_operands, pair_operands)
    tri_shard_part = lax.all_gather(right_tri, "row", axis=1, tiled=True)
    triangle = lax.optimization_barrier(
        lax.cond(
            alignment_branch,
            lambda: jnp.zeros((tri_local, local_rows, tri_shard_part.shape[1]), jnp.float32),
            lambda: jnp.einsum(
                "cik,cjk->cij", left_tri, tri_shard_part, preferred_element_type=jnp.float32
            ),
        ).astype(jnp.bfloat16)
    )
    tri_float = triangle.astype(jnp.float32)
    summed, squared = lax.psum(
        (jnp.sum(tri_float, axis=0), jnp.sum(tri_float * tri_float, axis=0)), "seq"
    )
    tri_total = tri_local * lax.axis_size("seq")
    average = summed / tri_total
    variance = jnp.maximum(squared / tri_total - average * average, 0.0)
    tri_norm = (
        (tri_float - average) * lax.rsqrt(variance + EPSILON) * triangle_gain[:, None, None]
    ).astype(jnp.bfloat16)
    norm_flat = tri_norm.reshape(tri_local, -1)

    def tri_term(amount):
        return jnp.dot(
            triangle_output_weight, norm_flat, preferred_element_type=jnp.float32
        ).reshape(amount, local_rows, residues)

    def first_term(offset, amount):
        return lax.cond(alignment_branch, lambda: outer_term(amount), lambda: tri_term(amount))

    summed_first = channel_sum(first_term, chan_local)
    outer_increment = (summed_first * (1.0 / seq_total)).astype(jnp.bfloat16)
    gate_values = jax.nn.sigmoid(
        jnp.dot(triangle_gate_weight, tri_flat, preferred_element_type=jnp.float32)
    ).reshape(pair_shape)
    first_update = lax.optimization_barrier(
        (pairwise_input.astype(jnp.float32) + gate_values * summed_first).astype(jnp.bfloat16)
    )
    gathered_next = full_channels(first_update)

    def pair_hidden():
        trans_norm = (
            (layer_normalize(gathered_next.astype(jnp.float32), 0) * transition_gain[:, None, None])
            .astype(jnp.bfloat16)
            .reshape(pair_width, -1)
        )
        return jax.nn.relu(
            jnp.dot(transition_up_weight, trans_norm, preferred_element_type=jnp.float32)
        ).astype(jnp.bfloat16)

    hidden_units = lax.cond(
        alignment_branch,
        lambda: jnp.zeros((trans_local, local_rows * residues), jnp.bfloat16),
        pair_hidden,
    )

    def trans_real(amount):
        return jnp.dot(
            transition_down_weight, hidden_units, preferred_element_type=jnp.float32
        ).reshape(amount, local_rows, residues)

    def trans_term(offset, amount):
        return lax.cond(
            alignment_branch,
            lambda: jnp.zeros((amount, local_rows, residues), jnp.float32),
            lambda: trans_real(amount),
        )

    pair_following = (
        first_update.astype(jnp.float32) + channel_sum(trans_term, chan_local)
    ).astype(jnp.bfloat16)
    half_residues = residues // 2
    halved_width = alignment_channels // 2
    outgoing_product = jnp.where(
        alignment_branch,
        outer_increment[:, :, half_residues:],
        pair_following[:, :, :half_residues],
    )
    incoming = from_partner(outgoing_product, "branch", 0)
    local_half = jnp.where(
        alignment_branch,
        outer_increment[:, :, :half_residues],
        pair_following[:, :, half_residues:],
    )
    pairwise_output = (local_half.astype(jnp.float32) + incoming.astype(jnp.float32)).astype(
        jnp.bfloat16
    )
    mixed_received = shifted(mixed_heads, "branch", 1)
    mixed_applied = jnp.where(alignment_branch, mixed_heads, mixed_received)
    mix_columns = lax.dynamic_slice_in_dim(
        mixing_weight, path_index * halved_width, halved_width, 1
    )
    residual_stream = lax.dynamic_slice_in_dim(
        alignment_input, path_index * halved_width, halved_width, 2
    )
    projected_values = jnp.dot(
        mixed_applied.reshape(-1, latent_heads), mix_columns, preferred_element_type=jnp.float32
    )
    alignment_output = (
        residual_stream.astype(jnp.float32)
        + projected_values.reshape(local_sequences, local_rows, halved_width)
    ).astype(jnp.bfloat16)
    return (alignment_output, pairwise_output)


BIAS_COST = 175 * 10**6


def rounded(values):
    return values.astype(jnp.bfloat16)


def widened(values):
    return values.astype(jnp.float32)


def product(left, right, contract_left=1, contract_right=0):
    return lax.dot_general(
        left,
        right,
        (((contract_left,), (contract_right,)), ((), ())),
        preferred_element_type=jnp.float32,
    )


def head_mask(groups, rows, head_size):
    shape = (groups * rows, groups * head_size)
    row = lax.broadcasted_iota(jnp.int32, shape, 0) // rows
    return row == lax.broadcasted_iota(jnp.int32, shape, 1) // head_size


def same_group(rows, columns, group):
    row = lax.broadcasted_iota(jnp.int32, (rows, columns), 0) // group
    column = lax.broadcasted_iota(jnp.int32, (rows, columns), 1) // group
    return row == column


def as_column(row):
    size = row.shape[1]
    return jnp.sum(jnp.where(same_group(size, size, 1), row, 0.0), axis=1, keepdims=True)


def kernel_call(body, outputs, operands, scratch=(), flops=0, in_hbm=(), room=32 * 2**20):
    vmem = pl.BlockSpec(memory_space=pltpu.VMEM)
    hbm = pl.BlockSpec(memory_space=pltpu.HBM)
    size = sum(a.size * a.dtype.itemsize for a in operands)
    size += sum(o.size * o.dtype.itemsize for o in outputs)
    return pl.pallas_call(
        body,
        out_shape=outputs,
        in_specs=[hbm if i in in_hbm else vmem for i in range(len(operands))],
        out_specs=[vmem] * len(outputs),
        scratch_shapes=list(scratch),
        cost_estimate=pl.CostEstimate(flops=flops, bytes_accessed=size, transcendentals=0),
        compiler_params=pltpu.CompilerParams(vmem_limit_bytes=room),
    )(*operands)


def exchange(value, axes, distance):
    members = lax.axis_size(axes)
    return lax.ppermute(value, axes, [(i, i ^ distance) for i in range(members)])


def start_kernel(token_ref):
    token_ref[...] = jnp.zeros_like(token_ref)


def send_kernel(
    sizes, rows_ref, pair_ref, gain_ref, weight_ref, input_ref, gate_ref, tri_gain_ref, output_ref, up_ref,
    down_ref, token_ref, same_ref, other_ref, shared_ref, wide,
):
    sequences, local_rows, residues, chan_local, outer_width = sizes
    part = sequences // 4
    part_rows = part * local_rows
    pair = widened(pair_ref[...])
    flat_pair = rounded(jnp.concatenate([pair[:, i, :] for i in range(local_rows)], axis=1))
    shared_ref[0:chan_local, :] = flat_pair
    at = chan_local + sequences
    narrow = gate_ref.shape[1]
    scaled = rounded(widened(output_ref[...]) * as_column(tri_gain_ref[...]))
    kinds = [input_ref[kind] for kind in range(input_ref.shape[0])]
    down = down_ref[...]
    for block in (*kinds, gate_ref[...], scaled, down[:chan_local]):
        shared_ref[at : at + chan_local, :narrow] = block
        at += chan_local
    at = chan_local + sequences
    for block in (up_ref[...], down[chan_local:]):
        shared_ref[at : at + block.shape[0], narrow:] = block
        at += block.shape[0]
    same_ref[part_rows : part_rows + chan_local, :] = flat_pair
    other_ref[part_rows : part_rows + chan_local, :] = flat_pair
    unit_here = 2 * lax.axis_index("branch") + lax.rem(lax.axis_index("row"), 2)
    unit_other = 2 * lax.axis_index("branch") + 1 - lax.rem(lax.axis_index("row"), 2)
    same_ref[0:part_rows, :] = rows_ref[pl.ds(unit_here * part_rows, part_rows), :]
    other_ref[0:part_rows, :] = rows_ref[pl.ds(unit_other * part_rows, part_rows), :]
    normed = rounded(layer_normalize(widened(rows_ref[...]), 1) * gain_ref[...])
    wide[:, 0 : 2 * outer_width] = product(normed, weight_ref[...], 1, 1)
    base = part_rows + chan_local
    for i in range(local_rows):
        both = rounded(wide[pl.ds(i, sequences, stride=local_rows), :])
        lanes = slice(i * outer_width, (i + 1) * outer_width)
        shared_ref[chan_local : chan_local + sequences, lanes] = both[:, :outer_width]
        same_ref[base : base + sequences, lanes] = both[:, outer_width : 2 * outer_width]
    other_ref[base : base + sequences, :] = same_ref[base : base + sequences, :]


def pack_kernel(chan_local, own_ref, other_ref, pair_ref, rest_ref):
    rest = own_ref.shape[0] - chan_local
    for k, ref in enumerate((own_ref, other_ref)):
        pair_ref[k * chan_local : (k + 1) * chan_local, :] = ref[:chan_local, :]
        rest_ref[k * rest : (k + 1) * rest, :] = ref[chan_local:, :]


def keep_kernel(*refs):
    count = len(refs) // 2
    for source, target in zip(refs[:count], refs[count:]):
        target[...] = source[...]


def relay_kernel(sizes, own_ref, one_ref, two_ref, three_ref, after_bias_ref, after_keep_ref, relay_ref):
    sequences, local_rows, residues, chan_local, outer_width = sizes
    part_rows = sequences // 4 * local_rows
    row = lax.axis_index("row")
    branch = lax.axis_index("branch")
    base = part_rows + chan_local
    for distance, ref in enumerate((own_ref, one_ref, two_ref, three_ref)):
        shard = row ^ distance

        @pl.when(shard // 2 == branch)
        def _():
            place = lax.rem(shard, 2)
            relay_ref[pl.ds(pl.multiple_of(place * chan_local, chan_local), chan_local), :] = ref[
                part_rows:base, :
            ]
            start = 2 * chan_local + place * sequences
            relay_ref[pl.ds(pl.multiple_of(start, chan_local), sequences), :] = ref[
                base : base + sequences, :
            ]


def score_kernel(
    sizes, own_ref, one_ref, two_ref, three_ref, gain_ref, weight_ref, *refs,
):
    score_ref, values_ref, gate_ref, module = refs[-4:]
    sequences, local_rows, residues, chan_local, outer_width = sizes
    part = sequences // 4
    part_rows = part * local_rows
    width = gain_ref.shape[1]
    head_size = 32
    row = lax.axis_index("row")
    for distance, ref in enumerate((own_ref, one_ref, two_ref, three_ref)):
        shard = row ^ distance
        block = widened(ref[0:part_rows, :])
        unit = layer_normalize(block, 1) * gain_ref[...]
        module[:, pl.ds(pl.multiple_of(shard * local_rows, local_rows), local_rows), :] = unit.reshape(
            part, local_rows, width
        )
    normed = rounded(module[...].reshape(part * residues, width))
    half = residues // 2
    here = module[:, pl.ds(pl.multiple_of(row // 2 * half, half), half), :]
    query_rows = rounded(here.reshape(part * half, width))
    heads = values_ref.shape[1]
    query = rounded(product(query_rows, weight_ref[:, 0:heads]) * head_size ** (-0.5))
    keys = rounded(product(normed, weight_ref[:, heads : 2 * heads]))
    values_ref[...] = rounded(product(normed, weight_ref[:, 2 * heads : 3 * heads]))
    gate_ref[...] = rounded(jax.nn.sigmoid(product(query_rows, weight_ref[:, 3 * heads :])))
    groups = heads // head_size
    mask = head_mask(groups, half, head_size)
    for s in range(part):
        one = query[s * half : (s + 1) * half]
        spread = jnp.where(mask, jnp.concatenate([one] * groups, axis=0), jnp.bfloat16(0))
        score_ref[s * residues : (s + 1) * residues, :] = product(
            keys[s * residues : (s + 1) * residues], spread, 1, 1
        )


def bias_kernel(chan_local, local_rows, pair_refs, matrix_ref, bias_ref, full):
    groups = matrix_ref.shape[0]
    residues = bias_ref.shape[0]
    seq = lax.axis_index("seq")
    for distance, ref in zip((0, 2, 1, 3), pair_refs):
        place = pl.ds(pl.multiple_of((seq ^ distance) * chan_local, chan_local), chan_local)
        full[place, :] = widened(ref[0:chan_local, :])
    plain = rounded(layer_normalize(full[...], 0))
    bias = rounded(product(matrix_ref[...], plain).T)
    lanes = bias_ref.shape[1]
    half = lanes // groups
    head = lax.broadcasted_iota(jnp.int32, (groups, lanes), 0)
    lane = lax.broadcasted_iota(jnp.int32, (groups, lanes), 1)
    first = lax.rem(lax.axis_index("row"), 2) * local_rows
    total = jnp.zeros(bias_ref.shape, jnp.float32)
    for i in range(local_rows):
        pick = jnp.where(lane == head * half + first + i, jnp.bfloat16(1), jnp.bfloat16(0))
        total += product(bias[i * residues : (i + 1) * residues, :], pick)
    bias_ref[...] = rounded(total)


def mix_kernel(
    sizes, near_bias_ref, far_bias_ref, score_ref, values_ref, gate_ref, mixing_ref, own_ref, one_ref, *refs,
):
    near_here_ref, near_there_ref, far_here_ref, far_there_ref, module = refs[-5:]
    sequences, local_rows, residues, chan_local, outer_width = sizes
    part = sequences // 4
    part_rows = part * local_rows
    half = residues // 2
    heads = values_ref.shape[1]
    head_size = 32
    groups = heads // head_size
    row = lax.axis_index("row")
    branch = lax.axis_index("branch")
    bias = widened(near_bias_ref[...]) + widened(far_bias_ref[...])
    scores = score_ref[...].reshape(part, residues, groups * half) + bias[None]
    weights = jnp.exp(scores - jnp.max(scores, axis=1, keepdims=True))
    weights = rounded(weights / jnp.sum(weights, axis=1, keepdims=True))
    mask = head_mask(groups, half, head_size)
    attended = []
    for s in range(part):
        every = product(weights[s], values_ref[s * residues : (s + 1) * residues, :], 0, 0)
        every = jnp.where(mask, every, 0.0).reshape(groups, half, heads)
        attended.append(jnp.sum(every, axis=0))
    mixed = rounded(widened(gate_ref[...]) * jnp.concatenate(attended, axis=0))
    projected = product(mixed, mixing_ref[...])
    width = projected.shape[1]
    module[...] = projected.reshape(part, half, width)
    halved = width // 2
    for distance, ref, here, there in (
        (0, own_ref, near_here_ref, near_there_ref),
        (1, one_ref, far_here_ref, far_there_ref),
    ):
        place = lax.rem(row, 2) ^ distance
        update = module[:, pl.ds(pl.multiple_of(place * local_rows, local_rows), local_rows), :]
        result = rounded(widened(ref[0:part_rows, :]) + update.reshape(part_rows, width))
        low, high = result[:, :halved], result[:, halved:]
        here[...] = jnp.where(branch == 0, low, high)
        there[...] = jnp.where(branch == 0, high, low)


def place_kernel(own_ref, branch_ref, row_ref, both_ref, pair_ref, output_ref, pair_output_ref):
    pair_output_ref[...] = pair_ref[...]
    rows = own_ref.shape[0]
    branch = lax.axis_index("branch")
    parity = lax.rem(lax.axis_index("row"), 2)
    for flip_branch, flip_row, ref in (
        (0, 0, own_ref),
        (1, 0, branch_ref),
        (0, 1, row_ref),
        (1, 1, both_ref),
    ):
        unit = 2 * (branch ^ flip_branch) + (parity ^ flip_row)
        output_ref[pl.ds(pl.multiple_of(unit * rows, rows), rows), :] = ref[...]


def pair_kernel(
    sizes, row_refs, rest_refs, pair_refs, gain_ref, transition_gain_ref, outer_weight_ref, seq_total, hidden_local,
    output_ref, rows, columns, gates, outer, outer_flat, ordered, final,
):
    sequences, local_rows, residues, chan_local, outer_width = sizes
    half = residues // 2
    branch = lax.axis_index("branch")
    seq = lax.axis_index("seq")
    width = 4 * chan_local
    chan = chan_local
    gain = as_column(gain_ref[...])
    weight_refs = [ref.at[sequences:, 0:width] for ref in rest_refs]
    hidden_refs = [ref.at[sequences:, width:] for ref in rest_refs]
    for distance, row_ref, pair_ref, weight_ref in zip((0, 2, 1, 3), row_refs, pair_refs, weight_refs):
        place = pl.ds(pl.multiple_of((seq ^ distance) * chan, chan), chan)
        rows[place, :] = row_ref[0:chan, :]
        for k in range(2):
            columns[k, place, :] = pair_ref[k * chan : (k + 1) * chan, :]
        gates[place, :] = weight_ref[4 * chan : 5 * chan, :]

    def projection(values, kind):
        weights = jnp.concatenate([w[kind * chan : (kind + 1) * chan, :] for w in weight_refs], axis=0)
        return product(values, weights, 1, 1)

    raw = widened(rows[...])
    row_input = rounded((layer_normalize(raw, 0) * gain).T)
    left = widened(
        rounded(projection(row_input, 0) * jax.nn.sigmoid(projection(row_input, 1)))
    ).reshape(local_rows, residues, width)
    right = []
    for k in range(2):
        column_input = rounded((layer_normalize(widened(columns[k]), 0) * gain).T)
        right.append(
            widened(
                rounded(projection(column_input, 2) * jax.nn.sigmoid(projection(column_input, 3)))
            ).reshape(local_rows, residues, width)
        )
    right = jnp.concatenate(right, axis=0)
    triangle = jnp.concatenate(
        [jnp.sum(left[i][None] * right, axis=1) for i in range(local_rows)], axis=0
    )
    triangle = widened(rounded(triangle))
    tri_norm = rounded(layer_normalize(triangle, 1))
    output_weight = jnp.concatenate([w[5 * chan : 6 * chan, :] for w in weight_refs], axis=0)
    tri_out = product(tri_norm, output_weight)
    ordered[...] = raw.T.reshape(local_rows, residues, width)
    place = pl.ds(pl.multiple_of(branch * half, half), half)
    raw_here = ordered[:, place, :].reshape(local_rows * half, width)
    ordered[...] = widened(row_input).reshape(local_rows, residues, width)
    input_here = rounded(ordered[:, place, :].reshape(local_rows * half, width))
    gate = jax.nn.sigmoid(product(input_here, gates[...], 1, 1))
    first_update = widened(rounded(raw_here + gate * tri_out))
    trans_norm = rounded(layer_normalize(first_update, 1) * transition_gain_ref[...])
    down = jnp.zeros((local_rows * half, width), jnp.float32)
    for w, h in zip(weight_refs, hidden_refs):
        hidden = rounded(jax.nn.relu(product(trans_norm, h[0:hidden_local, :], 1, 1)))
        down_weight = jnp.concatenate([w[6 * chan : 7 * chan, :], h[hidden_local : hidden_local + 3 * chan, :]], axis=0)
        down += product(hidden, down_weight, 1, 1)
    pair_next = widened(rounded(first_update + down))

    lefts = jnp.concatenate([ref[:sequences, :] for ref in rest_refs], axis=0)
    base = 2 * chan
    rights = jnp.concatenate(
        [
            jnp.concatenate([p[base : base + sequences, :], p[base + sequences :, :]], axis=1)
            for p in pair_refs
        ],
        axis=0,
    )
    outer_all = product(rounded(widened(lefts).T), rights)
    each = 128 // outer_width
    for tile in range(half // each):
        outer[tile] = outer_all[:, tile * 128 : (tile + 1) * 128]
        for c in range(outer_width):
            strip = outer[tile, pl.ds(c, local_rows, stride=outer_width), :]
            for k in range(each):
                j = tile * each + k
                outer_flat[
                    j * local_rows : (j + 1) * local_rows, c * outer_width : (c + 1) * outer_width
                ] = strip[:, k * outer_width : (k + 1) * outer_width]
    final[...] = product(rounded(outer_flat[...]), outer_weight_ref[...]) * (1.0 / seq_total)
    outer_update = jnp.concatenate(
        [final[pl.ds(i, half, stride=local_rows), :] for i in range(local_rows)], axis=0
    )
    outer_update = widened(rounded(outer_update))
    result = pair_next + outer_update
    own = result[:, 0:chan]
    for k in range(1, 4):
        own = jnp.where(seq == k, result[:, k * chan : (k + 1) * chan], own)
    output_ref[...] = rounded(own)


def compact_shards(
    alignment_input, pairwise_input, alignment_gain, product_gain, attention_weight, mixing_weight,
    outer_input_weight, outer_output_weight, bias_matrix, pairwise_gain, triangle_input_weight,
    triangle_gate_weight, triangle_gain, triangle_output_weight, transition_gain,
    transition_up_weight, transition_down_weight,
):
    sequences, local_rows, width = alignment_input.shape
    chan_local, _, residues = pairwise_input.shape
    pair_width, groups = bias_matrix.shape
    heads = mixing_weight.shape[0]
    outer_width = outer_input_weight.shape[2]
    part = sequences // 4
    part_rows = part * local_rows
    half = residues // 2
    sizes = (sequences, local_rows, residues, chan_local, outer_width)
    half_type, full_type = jnp.bfloat16, jnp.float32

    def shape(*dims, dtype=half_type):
        return jax.ShapeDtypeStruct(dims, dtype)

    rows_flat = alignment_input.reshape(sequences * local_rows, width)
    message_rows = part_rows + chan_local + sequences
    outer_weight_flat = outer_input_weight.transpose(1, 2, 0).reshape(2 * outer_width, width)
    (token,) = kernel_call(start_kernel, [shape(8, 128, dtype=full_type)], [], flops=5 * 10**9)
    hidden_local = transition_up_weight.shape[0]
    shared_rows = chan_local + sequences + 7 * chan_local
    same, other, shared = kernel_call(
        functools.partial(send_kernel, sizes),
        [shape(message_rows, width), shape(message_rows, width),
         shape(shared_rows, width)],
        [rows_flat, pairwise_input, product_gain[None], outer_weight_flat, triangle_input_weight,
         triangle_gate_weight, triangle_gain[None], triangle_output_weight.T, transition_up_weight,
         transition_down_weight, token],
        [pltpu.VMEM((sequences * local_rows, 128), full_type)],
    )
    shared_x = exchange(shared, "seq", 2)
    pair_two, rest_two = kernel_call(
        functools.partial(pack_kernel, chan_local),
        [shape(2 * chan_local, width), shape(2 * (shared_rows - chan_local), width)],
        [shared, shared_x],
    )
    pair_core = exchange(pair_two, "seq", 1)
    rest_core = exchange(rest_two, "seq", 1)
    from_three = exchange(other, "row", 3)
    from_two = exchange(same, "row", 2)
    from_one = exchange(other, "row", 1)
    received = (same, from_one, from_two, from_three)

    late_weight = lax.optimization_barrier((attention_weight, shared))[0]
    kept = [late_weight.reshape(width, 4 * heads), mixing_weight,
            outer_output_weight.reshape(outer_width * outer_width, pair_width),
            alignment_gain[None], pairwise_gain[None], transition_gain[None]]
    attention_kept, mixing_kept, outer_kept, row_gain, pair_gain, last_gain = kernel_call(
        keep_kernel, [shape(*a.shape, dtype=a.dtype) for a in kept], kept
    )

    def bias_body(*refs):
        bias_kernel(chan_local, local_rows, (refs[0], refs[1], refs[2].at[:chan_local], refs[2].at[chan_local:]), *refs[3:])

    (near_bias,) = kernel_call(
        bias_body,
        [shape(residues, groups * half)],
        [shared, shared_x, pair_core, bias_matrix.T],
        [
            pltpu.VMEM((pair_width, local_rows * residues), full_type),
        ],
        flops=BIAS_COST,
    )
    far_bias = exchange(near_bias, "row", 1)

    (relay,) = kernel_call(
        functools.partial(relay_kernel, sizes),
        [shape(2 * chan_local + 2 * sequences, width)],
        [*received, far_bias, row_gain],
    )
    relay_x = exchange(relay, "seq", 2)
    relay_core = exchange(relay, "seq", 1)
    relay_both = exchange(relay, "seq", 3)
    relays = (relay, relay_x, relay_core, relay_both)

    scores, values, gate = kernel_call(
        functools.partial(score_kernel, sizes),
        [shape(part * residues, groups * half, dtype=full_type), shape(part * residues, heads), shape(part * half, heads)],
        [*received, row_gain, attention_kept, relay],
        [pltpu.VMEM((part, residues, width), full_type)],
        flops=3 * 10**9,
    )

    near_here, near_there, far_here, far_there = kernel_call(
        functools.partial(mix_kernel, sizes),
        [shape(part_rows, width // 2)] * 4,
        [near_bias, far_bias, scores, values, gate, mixing_kept, same, from_one, rest_core, relay_core],
        [pltpu.VMEM((part, half, width), full_type)],
        flops=3 * 10**9,
    )
    axes = ("branch", "row")
    across = lax.axis_size("row")
    from_branch = exchange(near_there, axes, across)
    from_both = exchange(far_there, axes, across + 1)
    from_row = exchange(far_here, axes, 1)

    def pair_body(*refs):
        own, other, pair, rest = refs[:4]
        count = rest.shape[0] // 2
        row_refs = (own, other, pair.at[:chan_local], pair.at[chan_local:])
        rest_refs = (own.at[chan_local:], other.at[chan_local:], rest.at[:count], rest.at[count:])
        pair_kernel(sizes, row_refs, rest_refs, refs[4:8], *refs[8:11], sequences * 4, hidden_local, *refs[11:])

    (pair_done,) = kernel_call(
        pair_body,
        [shape(local_rows * half, chan_local)],
        [shared, shared_x, pair_core, rest_core, *relays, pair_gain, last_gain, outer_kept],
        [
            pltpu.VMEM((pair_width, local_rows * residues), half_type),
            pltpu.VMEM((2, pair_width, local_rows * residues), half_type),
            pltpu.VMEM((pair_width, pair_width), half_type),
            pltpu.VMEM((half * outer_width // 128, local_rows * outer_width, 128), full_type),
            pltpu.VMEM((local_rows * half, outer_width * outer_width), full_type),
            pltpu.VMEM((local_rows, residues, pair_width), full_type),
            pltpu.VMEM((local_rows * half, pair_width), full_type),
        ],
    )
    alignment_flat, pairwise_output = kernel_call(
        place_kernel,
        [shape(sequences * local_rows, width // 2), shape(local_rows * half, chan_local)],
        [near_here, from_branch, from_row, from_both, pair_done],
    )
    return (
        alignment_flat.reshape(sequences, local_rows, width // 2),
        pairwise_output.reshape(local_rows, half, chan_local).transpose(2, 0, 1),
    )


def is_compact(mesh, residues):
    return mesh.shape["row"] == 4 and mesh.shape["seq"] == 4 and mesh.shape["branch"] == 2


def solution(mesh):
    return jax.shard_map(
        compact_shards if is_compact(mesh, None) else shards,
        mesh=mesh,
        in_specs=(
            P("seq", "row", None),
            P("seq", "row", None),
            P(),
            P(),
            P(),
            P(),
            P(),
            P(),
            P(),
            P(),
            P(None, "seq", None),
            P("seq", None),
            P("seq"),
            P(None, "seq"),
            P(),
            P("seq", None),
            P(None, "seq"),
        ),
        out_specs=(P("seq", "row", "branch"), P("seq", "row", "branch")),
        check_vma=False,
    )
```

```python
import functools

import jax
import jax.numpy as jnp
from jax import lax
from jax.experimental import pallas as pl
from jax.experimental.pallas import tpu as pltpu
from jax.sharding import PartitionSpec as P

EPSILON = 1e-05


def shifted(value, axis, by):
    length = lax.axis_size(axis)
    pairs = [(i, i + by) for i in range(length) if 0 <= i + by < length]
    return lax.ppermute(value, axis, pairs)


def from_partner(value, axis, distance):
    return lax.ppermute(value, axis, [(i, i ^ 1 << distance) for i in range(lax.axis_size(axis))])


def layer_normalize(values, axis):
    average = jnp.mean(values, axis=axis, keepdims=True)
    centred = values - average
    spread = jnp.mean(centred * centred, axis=axis, keepdims=True)
    return centred * lax.rsqrt(spread + EPSILON)


def full_channels(values):
    return lax.all_gather(values, "seq", axis=0, tiled=True)


def channel_sum(term, kept_rows):
    return lax.psum_scatter(
        term(jnp.int32(0), kept_rows * lax.axis_size("seq")), "seq", scatter_dimension=0, tiled=True
    )


def shards(
    alignment_input,
    pairwise_input,
    alignment_gain,
    product_gain,
    attention_weight,
    mixing_weight,
    outer_input_weight,
    outer_output_weight,
    bias_matrix,
    pairwise_gain,
    triangle_input_weight,
    triangle_gate_weight,
    triangle_gain,
    triangle_output_weight,
    transition_gain,
    transition_up_weight,
    transition_down_weight,
):
    local_sequences, local_rows, alignment_channels = alignment_input.shape
    chan_local = pairwise_input.shape[0]
    residues = pairwise_input.shape[2]
    pair_width, head_total = bias_matrix.shape
    latent_heads = mixing_weight.shape[0]
    head_size = latent_heads // head_total
    outer_width = outer_input_weight.shape[2]
    tri_local = triangle_input_weight.shape[1]
    trans_local = transition_up_weight.shape[0]
    seq_total = local_sequences * lax.axis_size("seq")
    path_index = lax.axis_index("branch")
    alignment_branch = path_index == 0
    query_shape = (local_sequences, local_rows, latent_heads)
    pair_shape = (chan_local, local_rows, residues)
    full_pair_shape = (pair_width, local_rows, residues)
    key_shape = (local_sequences, 2 * latent_heads, local_rows)
    gathered = full_channels(pairwise_input)

    def alignment_early():
        alignment_module = layer_normalize(alignment_input.astype(jnp.float32), 2)
        normalized_values = (alignment_module * alignment_gain).astype(jnp.bfloat16)
        outer_normalized = (alignment_module * product_gain).astype(jnp.bfloat16)
        flattened_rows = normalized_values.reshape(-1, alignment_channels)
        outer_flattened = outer_normalized.reshape(-1, alignment_channels)
        query = (
            (
                jnp.dot(flattened_rows, attention_weight[:, 0], preferred_element_type=jnp.float32)
                * head_size ** (-0.5)
            )
            .astype(jnp.bfloat16)
            .reshape(query_shape)
        )
        gate = (
            jax.nn.sigmoid(
                jnp.dot(flattened_rows, attention_weight[:, 3], preferred_element_type=jnp.float32)
            )
            .astype(jnp.bfloat16)
            .reshape(query_shape)
        )
        key_values = (
            jnp.einsum(
                "sim,mkc->skci",
                normalized_values,
                attention_weight[:, 1:3],
                preferred_element_type=jnp.float32,
            )
            .astype(jnp.bfloat16)
            .reshape(key_shape)
        )
        left = (
            jnp.dot(outer_flattened, outer_input_weight[:, 0], preferred_element_type=jnp.float32)
            .astype(jnp.bfloat16)
            .reshape(local_sequences, local_rows, outer_width)
        )
        right_cols = jnp.einsum(
            "sim,mc->sci",
            outer_normalized,
            outer_input_weight[:, 1],
            preferred_element_type=jnp.float32,
        ).astype(jnp.bfloat16)
        empty_bias = jnp.zeros((head_total, local_rows, residues), jnp.bfloat16)
        empty_pair = jnp.zeros(full_pair_shape, jnp.bfloat16)
        return (empty_bias, empty_pair, query, key_values, gate, left, right_cols)

    def pair_early():
        unit = layer_normalize(gathered.astype(jnp.float32), 0)
        plain = unit.astype(jnp.bfloat16).reshape(pair_width, -1)
        bias_rows = (
            jnp.einsum("ch,cn->hn", bias_matrix, plain, preferred_element_type=jnp.float32)
            .astype(jnp.bfloat16)
            .reshape(head_total, local_rows, residues)
        )
        tri_input = (unit * pairwise_gain[:, None, None]).astype(jnp.bfloat16)
        empty_query = jnp.zeros(query_shape, jnp.bfloat16)
        empty_keys = jnp.zeros(key_shape, jnp.bfloat16)
        empty_left = jnp.zeros((local_sequences, local_rows, outer_width), jnp.bfloat16)
        empty_right = jnp.zeros((local_sequences, outer_width, local_rows), jnp.bfloat16)
        return (bias_rows, tri_input, empty_query, empty_keys, empty_query, empty_left, empty_right)

    bias_local, tri_input, query, key_values, gate, left, right_cols = lax.cond(
        alignment_branch, alignment_early, pair_early
    )
    bias_recv = shifted(bias_local, "branch", -1)
    query_heads = query.reshape(local_sequences, local_rows, head_total, head_size).transpose(
        0, 2, 1, 3
    )

    def fold_real(running, shard_part):
        highest, totals, weighted = running
        columns = shard_part.shape[2]
        keys_part = shard_part[:, :latent_heads].reshape(
            local_sequences, head_total, head_size, columns
        )
        values_part = shard_part[:, latent_heads:].reshape(
            local_sequences, head_total, head_size, columns
        )
        bias_part = bias_recv.astype(jnp.float32)
        scores = (
            jnp.einsum(
                "shid,shdj->shij", query_heads, keys_part, preferred_element_type=jnp.float32
            )
            + bias_part[None]
        )
        raised = jnp.maximum(highest, jnp.max(scores, axis=3))
        weights = jnp.exp(scores - raised[..., None])
        totals = jnp.sum(weights, axis=3)
        weighted = jnp.einsum(
            "shij,shdj->shid",
            weights.astype(jnp.bfloat16),
            values_part,
            preferred_element_type=jnp.float32,
        )
        return (raised, totals, weighted)

    initial = (
        jnp.full((local_sequences, head_total, local_rows), -1e30, jnp.float32),
        jnp.zeros((local_sequences, head_total, local_rows), jnp.float32),
        jnp.zeros((local_sequences, head_total, local_rows, head_size), jnp.float32),
    )
    shard_part = lax.all_gather(key_values, "row", axis=2, tiled=True)
    highest, totals, weighted = lax.cond(
        alignment_branch, lambda: fold_real(initial, shard_part), lambda: initial
    )
    safe_totals = jnp.where(totals > 0, totals, 1.0)
    attended = (weighted / safe_totals[..., None]).transpose(0, 2, 1, 3).reshape(query_shape)
    mixed_heads = (gate.astype(jnp.float32) * attended).astype(jnp.bfloat16)
    right_full = lax.all_gather(right_cols, "row", axis=2, tiled=True)
    right_matrix = right_full.reshape(local_sequences * outer_width, residues)
    spread = lax.cond(
        alignment_branch,
        lambda: jnp.einsum(
            "sic,cdo->oisd", left, outer_output_weight, preferred_element_type=jnp.float32
        ).astype(jnp.bfloat16),
        lambda: jnp.zeros((pair_width, local_rows, local_sequences, outer_width), jnp.bfloat16),
    )

    def outer_term(amount):
        spread_part = spread.reshape(amount * local_rows, local_sequences * outer_width)
        return jnp.dot(spread_part, right_matrix, preferred_element_type=jnp.float32).reshape(
            amount, local_rows, residues
        )

    tri_flat = tri_input.reshape(pair_width, -1)

    def pair_operands():
        linear = jnp.dot(
            triangle_input_weight.reshape(4 * tri_local, pair_width),
            tri_flat,
            preferred_element_type=jnp.float32,
        )
        linear = linear.reshape(4, tri_local, local_rows, residues)
        left_part = (linear[0] * jax.nn.sigmoid(linear[1])).astype(jnp.bfloat16)
        right_part = (linear[2] * jax.nn.sigmoid(linear[3])).astype(jnp.bfloat16)
        return (left_part, right_part)

    def empty_operands():
        empty = jnp.zeros((tri_local, local_rows, residues), jnp.bfloat16)
        return (empty, empty)

    left_tri, right_tri = lax.cond(alignment_branch, empty_operands, pair_operands)
    tri_shard_part = lax.all_gather(right_tri, "row", axis=1, tiled=True)
    triangle = lax.optimization_barrier(
        lax.cond(
            alignment_branch,
            lambda: jnp.zeros((tri_local, local_rows, tri_shard_part.shape[1]), jnp.float32),
            lambda: jnp.einsum(
                "cik,cjk->cij", left_tri, tri_shard_part, preferred_element_type=jnp.float32
            ),
        ).astype(jnp.bfloat16)
    )
    tri_float = triangle.astype(jnp.float32)
    summed, squared = lax.psum(
        (jnp.sum(tri_float, axis=0), jnp.sum(tri_float * tri_float, axis=0)), "seq"
    )
    tri_total = tri_local * lax.axis_size("seq")
    average = summed / tri_total
    variance = jnp.maximum(squared / tri_total - average * average, 0.0)
    tri_norm = (
        (tri_float - average) * lax.rsqrt(variance + EPSILON) * triangle_gain[:, None, None]
    ).astype(jnp.bfloat16)
    norm_flat = tri_norm.reshape(tri_local, -1)

    def tri_term(amount):
        return jnp.dot(
            triangle_output_weight, norm_flat, preferred_element_type=jnp.float32
        ).reshape(amount, local_rows, residues)

    def first_term(offset, amount):
        return lax.cond(alignment_branch, lambda: outer_term(amount), lambda: tri_term(amount))

    summed_first = channel_sum(first_term, chan_local)
    outer_increment = (summed_first * (1.0 / seq_total)).astype(jnp.bfloat16)
    gate_values = jax.nn.sigmoid(
        jnp.dot(triangle_gate_weight, tri_flat, preferred_element_type=jnp.float32)
    ).reshape(pair_shape)
    first_update = lax.optimization_barrier(
        (pairwise_input.astype(jnp.float32) + gate_values * summed_first).astype(jnp.bfloat16)
    )
    gathered_next = full_channels(first_update)

    def pair_hidden():
        trans_norm = (
            (layer_normalize(gathered_next.astype(jnp.float32), 0) * transition_gain[:, None, None])
            .astype(jnp.bfloat16)
            .reshape(pair_width, -1)
        )
        return jax.nn.relu(
            jnp.dot(transition_up_weight, trans_norm, preferred_element_type=jnp.float32)
        ).astype(jnp.bfloat16)

    hidden_units = lax.cond(
        alignment_branch,
        lambda: jnp.zeros((trans_local, local_rows * residues), jnp.bfloat16),
        pair_hidden,
    )

    def trans_real(amount):
        return jnp.dot(
            transition_down_weight, hidden_units, preferred_element_type=jnp.float32
        ).reshape(amount, local_rows, residues)

    def trans_term(offset, amount):
        return lax.cond(
            alignment_branch,
            lambda: jnp.zeros((amount, local_rows, residues), jnp.float32),
            lambda: trans_real(amount),
        )

    pair_following = (
        first_update.astype(jnp.float32) + channel_sum(trans_term, chan_local)
    ).astype(jnp.bfloat16)
    half_residues = residues // 2
    halved_width = alignment_channels // 2
    outgoing_product = jnp.where(
        alignment_branch,
        outer_increment[:, :, half_residues:],
        pair_following[:, :, :half_residues],
    )
    incoming = from_partner(outgoing_product, "branch", 0)
    local_half = jnp.where(
        alignment_branch,
        outer_increment[:, :, :half_residues],
        pair_following[:, :, half_residues:],
    )
    pairwise_output = (local_half.astype(jnp.float32) + incoming.astype(jnp.float32)).astype(
        jnp.bfloat16
    )
    mixed_received = shifted(mixed_heads, "branch", 1)
    mixed_applied = jnp.where(alignment_branch, mixed_heads, mixed_received)
    mix_columns = lax.dynamic_slice_in_dim(
        mixing_weight, path_index * halved_width, halved_width, 1
    )
    residual_stream = lax.dynamic_slice_in_dim(
        alignment_input, path_index * halved_width, halved_width, 2
    )
    projected_values = jnp.dot(
        mixed_applied.reshape(-1, latent_heads), mix_columns, preferred_element_type=jnp.float32
    )
    alignment_output = (
        residual_stream.astype(jnp.float32)
        + projected_values.reshape(local_sequences, local_rows, halved_width)
    ).astype(jnp.bfloat16)
    return (alignment_output, pairwise_output)


BIAS_COST = 175 * 10**6


def rounded(values):
    return values.astype(jnp.bfloat16)


def widened(values):
    return values.astype(jnp.float32)


def product(left, right, contract_left=1, contract_right=0):
    return lax.dot_general(
        left,
        right,
        (((contract_left,), (contract_right,)), ((), ())),
        preferred_element_type=jnp.float32,
    )


def head_mask(groups, rows, head_size):
    shape = (groups * rows, groups * head_size)
    row = lax.broadcasted_iota(jnp.int32, shape, 0) // rows
    return row == lax.broadcasted_iota(jnp.int32, shape, 1) // head_size


def same_group(rows, columns, group):
    row = lax.broadcasted_iota(jnp.int32, (rows, columns), 0) // group
    column = lax.broadcasted_iota(jnp.int32, (rows, columns), 1) // group
    return row == column


def as_column(row):
    size = row.shape[1]
    return jnp.sum(jnp.where(same_group(size, size, 1), row, 0.0), axis=1, keepdims=True)


def kernel_call(body, outputs, operands, scratch=(), flops=0, in_hbm=(), room=32 * 2**20):
    vmem = pl.BlockSpec(memory_space=pltpu.VMEM)
    hbm = pl.BlockSpec(memory_space=pltpu.HBM)
    size = sum(a.size * a.dtype.itemsize for a in operands)
    size += sum(o.size * o.dtype.itemsize for o in outputs)
    return pl.pallas_call(
        body,
        out_shape=outputs,
        in_specs=[hbm if i in in_hbm else vmem for i in range(len(operands))],
        out_specs=[vmem] * len(outputs),
        scratch_shapes=list(scratch),
        cost_estimate=pl.CostEstimate(flops=flops, bytes_accessed=size, transcendentals=0),
        compiler_params=pltpu.CompilerParams(vmem_limit_bytes=room),
    )(*operands)


def exchange(value, axes, distance):
    members = lax.axis_size(axes)
    return lax.ppermute(value, axes, [(i, i ^ distance) for i in range(members)])


def start_kernel(token_ref):
    token_ref[...] = jnp.zeros_like(token_ref)


def send_kernel(
    sizes, rows_ref, pair_ref, gain_ref, weight_ref, input_ref, gate_ref, tri_gain_ref, output_ref, up_ref,
    down_ref, token_ref, same_ref, other_ref, shared_ref, wide,
):
    sequences, local_rows, residues, chan_local, outer_width = sizes
    part = sequences // 4
    part_rows = part * local_rows
    pair = widened(pair_ref[...])
    flat_pair = rounded(jnp.concatenate([pair[:, i, :] for i in range(local_rows)], axis=1))
    shared_ref[0:chan_local, :] = flat_pair
    at = chan_local + sequences
    narrow = gate_ref.shape[1]
    scaled = rounded(widened(output_ref[...]) * as_column(tri_gain_ref[...]))
    kinds = [input_ref[kind] for kind in range(input_ref.shape[0])]
    down = down_ref[...]
    for block in (*kinds, gate_ref[...], scaled, down[:chan_local]):
        shared_ref[at : at + chan_local, :narrow] = block
        at += chan_local
    at = chan_local + sequences
    for block in (up_ref[...], down[chan_local:]):
        shared_ref[at : at + block.shape[0], narrow:] = block
        at += block.shape[0]
    same_ref[part_rows : part_rows + chan_local, :] = flat_pair
    other_ref[part_rows : part_rows + chan_local, :] = flat_pair
    unit_here = 2 * lax.axis_index("branch") + lax.rem(lax.axis_index("row"), 2)
    unit_other = 2 * lax.axis_index("branch") + 1 - lax.rem(lax.axis_index("row"), 2)
    same_ref[0:part_rows, :] = rows_ref[pl.ds(unit_here * part_rows, part_rows), :]
    other_ref[0:part_rows, :] = rows_ref[pl.ds(unit_other * part_rows, part_rows), :]
    normed = rounded(layer_normalize(widened(rows_ref[...]), 1) * gain_ref[...])
    wide[:, 0 : 2 * outer_width] = product(normed, weight_ref[...], 1, 1)
    base = part_rows + chan_local
    for i in range(local_rows):
        both = rounded(wide[pl.ds(i, sequences, stride=local_rows), :])
        lanes = slice(i * outer_width, (i + 1) * outer_width)
        shared_ref[chan_local : chan_local + sequences, lanes] = both[:, :outer_width]
        same_ref[base : base + sequences, lanes] = both[:, outer_width : 2 * outer_width]
    other_ref[base : base + sequences, :] = same_ref[base : base + sequences, :]


def pack_kernel(chan_local, own_ref, other_ref, pair_ref, rest_ref):
    rest = own_ref.shape[0] - chan_local
    for k, ref in enumerate((own_ref, other_ref)):
        pair_ref[k * chan_local : (k + 1) * chan_local, :] = ref[:chan_local, :]
        rest_ref[k * rest : (k + 1) * rest, :] = ref[chan_local:, :]


def keep_kernel(*refs):
    count = len(refs) // 2
    for source, target in zip(refs[:count], refs[count:]):
        target[...] = source[...]


def arrive_kernel(*refs):
    refs[-1][...] = jnp.zeros_like(refs[-1])


def relay_kernel(sizes, own_ref, one_ref, two_ref, three_ref, after_bias_ref, after_keep_ref, relay_ref):
    sequences, local_rows, residues, chan_local, outer_width = sizes
    part_rows = sequences // 4 * local_rows
    row = lax.axis_index("row")
    branch = lax.axis_index("branch")
    base = part_rows + chan_local
    for distance, ref in enumerate((own_ref, one_ref, two_ref, three_ref)):
        shard = row ^ distance

        @pl.when(shard // 2 == branch)
        def _():
            place = lax.rem(shard, 2)
            relay_ref[pl.ds(pl.multiple_of(place * chan_local, chan_local), chan_local), :] = ref[
                part_rows:base, :
            ]
            start = 2 * chan_local + place * sequences
            relay_ref[pl.ds(pl.multiple_of(start, chan_local), sequences), :] = ref[
                base : base + sequences, :
            ]


def score_kernel(
    sizes, own_ref, one_ref, two_ref, three_ref, gain_ref, weight_ref, *refs,
):
    score_ref, values_ref, gate_ref, module = refs[-4:]
    sequences, local_rows, residues, chan_local, outer_width = sizes
    part = sequences // 4
    part_rows = part * local_rows
    width = gain_ref.shape[1]
    head_size = 32
    row = lax.axis_index("row")
    for distance, ref in enumerate((own_ref, one_ref, two_ref, three_ref)):
        shard = row ^ distance
        block = widened(ref[0:part_rows, :])
        unit = layer_normalize(block, 1) * gain_ref[...]
        module[:, pl.ds(pl.multiple_of(shard * local_rows, local_rows), local_rows), :] = unit.reshape(
            part, local_rows, width
        )
    normed = rounded(module[...].reshape(part * residues, width))
    half = residues // 2
    here = module[:, pl.ds(pl.multiple_of(row // 2 * half, half), half), :]
    query_rows = rounded(here.reshape(part * half, width))
    heads = values_ref.shape[1]
    query = rounded(product(query_rows, weight_ref[:, 0:heads]) * head_size ** (-0.5))
    keys = rounded(product(normed, weight_ref[:, heads : 2 * heads]))
    values_ref[...] = rounded(product(normed, weight_ref[:, 2 * heads : 3 * heads]))
    gate_ref[...] = rounded(jax.nn.sigmoid(product(query_rows, weight_ref[:, 3 * heads :])))
    groups = heads // head_size
    mask = head_mask(groups, half, head_size)
    for s in range(part):
        one = query[s * half : (s + 1) * half]
        spread = jnp.where(mask, jnp.concatenate([one] * groups, axis=0), jnp.bfloat16(0))
        score_ref[s * residues : (s + 1) * residues, :] = product(
            keys[s * residues : (s + 1) * residues], spread, 1, 1
        )


def bias_kernel(chan_local, local_rows, pair_refs, matrix_ref, bias_ref, full):
    groups = matrix_ref.shape[0]
    residues = bias_ref.shape[0]
    seq = lax.axis_index("seq")
    for distance, ref in zip((0, 2, 1, 3), pair_refs):
        place = pl.ds(pl.multiple_of((seq ^ distance) * chan_local, chan_local), chan_local)
        full[place, :] = widened(ref[0:chan_local, :])
    plain = rounded(layer_normalize(full[...], 0))
    bias = rounded(product(matrix_ref[...], plain).T)
    lanes = bias_ref.shape[1]
    half = lanes // groups
    head = lax.broadcasted_iota(jnp.int32, (groups, lanes), 0)
    lane = lax.broadcasted_iota(jnp.int32, (groups, lanes), 1)
    first = lax.rem(lax.axis_index("row"), 2) * local_rows
    total = jnp.zeros(bias_ref.shape, jnp.float32)
    for i in range(local_rows):
        pick = jnp.where(lane == head * half + first + i, jnp.bfloat16(1), jnp.bfloat16(0))
        total += product(bias[i * residues : (i + 1) * residues, :], pick)
    bias_ref[...] = rounded(total)


def mix_kernel(
    sizes, near_bias_ref, far_bias_ref, score_ref, values_ref, gate_ref, mixing_ref, own_ref, one_ref, *refs,
):
    near_here_ref, near_there_ref, far_here_ref, far_there_ref, module = refs[-5:]
    sequences, local_rows, residues, chan_local, outer_width = sizes
    part = sequences // 4
    part_rows = part * local_rows
    half = residues // 2
    heads = values_ref.shape[1]
    head_size = 32
    groups = heads // head_size
    row = lax.axis_index("row")
    branch = lax.axis_index("branch")
    bias = widened(near_bias_ref[...]) + widened(far_bias_ref[...])
    scores = score_ref[...].reshape(part, residues, groups * half) + bias[None]
    weights = jnp.exp(scores - jnp.max(scores, axis=1, keepdims=True))
    weights = rounded(weights / jnp.sum(weights, axis=1, keepdims=True))
    mask = head_mask(groups, half, head_size)
    attended = []
    for s in range(part):
        every = product(weights[s], values_ref[s * residues : (s + 1) * residues, :], 0, 0)
        every = jnp.where(mask, every, 0.0).reshape(groups, half, heads)
        attended.append(jnp.sum(every, axis=0))
    mixed = rounded(widened(gate_ref[...]) * jnp.concatenate(attended, axis=0))
    projected = product(mixed, mixing_ref[...])
    width = projected.shape[1]
    module[...] = projected.reshape(part, half, width)
    halved = width // 2
    for distance, ref, here, there in (
        (0, own_ref, near_here_ref, near_there_ref),
        (1, one_ref, far_here_ref, far_there_ref),
    ):
        place = lax.rem(row, 2) ^ distance
        update = module[:, pl.ds(pl.multiple_of(place * local_rows, local_rows), local_rows), :]
        result = rounded(widened(ref[0:part_rows, :]) + update.reshape(part_rows, width))
        low, high = result[:, :halved], result[:, halved:]
        here[...] = jnp.where(branch == 0, low, high)
        there[...] = jnp.where(branch == 0, high, low)


def place_kernel(own_ref, branch_ref, row_ref, both_ref, pair_ref, token_ref, output_ref, pair_output_ref):
    pair_output_ref[...] = pair_ref[...]
    rows = own_ref.shape[0]
    branch = lax.axis_index("branch")
    parity = lax.rem(lax.axis_index("row"), 2)
    for flip_branch, flip_row, ref in (
        (0, 0, own_ref),
        (1, 0, branch_ref),
        (0, 1, row_ref),
        (1, 1, both_ref),
    ):
        unit = 2 * (branch ^ flip_branch) + (parity ^ flip_row)
        output_ref[pl.ds(pl.multiple_of(unit * rows, rows), rows), :] = ref[...]


def pair_kernel(
    sizes, row_refs, rest_refs, pair_refs, gain_ref, transition_gain_ref, outer_weight_ref, seq_total, hidden_local,
    output_ref, rows, columns, gates, outer, outer_flat, ordered, final,
):
    sequences, local_rows, residues, chan_local, outer_width = sizes
    half = residues // 2
    branch = lax.axis_index("branch")
    seq = lax.axis_index("seq")
    width = 4 * chan_local
    chan = chan_local
    gain = as_column(gain_ref[...])
    weight_refs = [ref.at[sequences:, 0:width] for ref in rest_refs]
    hidden_refs = [ref.at[sequences:, width:] for ref in rest_refs]
    for distance, row_ref, pair_ref, weight_ref in zip((0, 2, 1, 3), row_refs, pair_refs, weight_refs):
        place = pl.ds(pl.multiple_of((seq ^ distance) * chan, chan), chan)
        rows[place, :] = row_ref[0:chan, :]
        for k in range(2):
            columns[k, place, :] = pair_ref[k * chan : (k + 1) * chan, :]
        gates[place, :] = weight_ref[4 * chan : 5 * chan, :]

    def projection(values, kind):
        weights = jnp.concatenate([w[kind * chan : (kind + 1) * chan, :] for w in weight_refs], axis=0)
        return product(values, weights, 1, 1)

    raw = widened(rows[...])
    row_input = rounded((layer_normalize(raw, 0) * gain).T)
    left = widened(
        rounded(projection(row_input, 0) * jax.nn.sigmoid(projection(row_input, 1)))
    ).reshape(local_rows, residues, width)
    right = []
    for k in range(2):
        column_input = rounded((layer_normalize(widened(columns[k]), 0) * gain).T)
        right.append(
            widened(
                rounded(projection(column_input, 2) * jax.nn.sigmoid(projection(column_input, 3)))
            ).reshape(local_rows, residues, width)
        )
    right = jnp.concatenate(right, axis=0)
    triangle = jnp.concatenate(
        [jnp.sum(left[i][None] * right, axis=1) for i in range(local_rows)], axis=0
    )
    triangle = widened(rounded(triangle))
    tri_norm = rounded(layer_normalize(triangle, 1))
    output_weight = jnp.concatenate([w[5 * chan : 6 * chan, :] for w in weight_refs], axis=0)
    tri_out = product(tri_norm, output_weight)
    ordered[...] = raw.T.reshape(local_rows, residues, width)
    place = pl.ds(pl.multiple_of(branch * half, half), half)
    raw_here = ordered[:, place, :].reshape(local_rows * half, width)
    ordered[...] = widened(row_input).reshape(local_rows, residues, width)
    input_here = rounded(ordered[:, place, :].reshape(local_rows * half, width))
    gate = jax.nn.sigmoid(product(input_here, gates[...], 1, 1))
    first_update = widened(rounded(raw_here + gate * tri_out))
    trans_norm = rounded(layer_normalize(first_update, 1) * transition_gain_ref[...])
    down = jnp.zeros((local_rows * half, width), jnp.float32)
    for w, h in zip(weight_refs, hidden_refs):
        hidden = rounded(jax.nn.relu(product(trans_norm, h[0:hidden_local, :], 1, 1)))
        down_weight = jnp.concatenate([w[6 * chan : 7 * chan, :], h[hidden_local : hidden_local + 3 * chan, :]], axis=0)
        down += product(hidden, down_weight, 1, 1)
    pair_next = widened(rounded(first_update + down))

    lefts = jnp.concatenate([ref[:sequences, :] for ref in rest_refs], axis=0)
    base = 2 * chan
    rights = jnp.concatenate(
        [
            jnp.concatenate([p[base : base + sequences, :], p[base + sequences :, :]], axis=1)
            for p in pair_refs
        ],
        axis=0,
    )
    outer_all = product(rounded(widened(lefts).T), rights)
    each = 128 // outer_width
    for tile in range(half // each):
        outer[tile] = outer_all[:, tile * 128 : (tile + 1) * 128]
        for c in range(outer_width):
            strip = outer[tile, pl.ds(c, local_rows, stride=outer_width), :]
            for k in range(each):
                j = tile * each + k
                outer_flat[
                    j * local_rows : (j + 1) * local_rows, c * outer_width : (c + 1) * outer_width
                ] = strip[:, k * outer_width : (k + 1) * outer_width]
    final[...] = product(rounded(outer_flat[...]), outer_weight_ref[...]) * (1.0 / seq_total)
    outer_update = jnp.concatenate(
        [final[pl.ds(i, half, stride=local_rows), :] for i in range(local_rows)], axis=0
    )
    outer_update = widened(rounded(outer_update))
    result = pair_next + outer_update
    own = result[:, 0:chan]
    for k in range(1, 4):
        own = jnp.where(seq == k, result[:, k * chan : (k + 1) * chan], own)
    output_ref[...] = rounded(own)


def compact_shards(
    alignment_input, pairwise_input, alignment_gain, product_gain, attention_weight, mixing_weight,
    outer_input_weight, outer_output_weight, bias_matrix, pairwise_gain, triangle_input_weight,
    triangle_gate_weight, triangle_gain, triangle_output_weight, transition_gain,
    transition_up_weight, transition_down_weight,
):
    sequences, local_rows, width = alignment_input.shape
    chan_local, _, residues = pairwise_input.shape
    pair_width, groups = bias_matrix.shape
    heads = mixing_weight.shape[0]
    outer_width = outer_input_weight.shape[2]
    part = sequences // 4
    part_rows = part * local_rows
    half = residues // 2
    sizes = (sequences, local_rows, residues, chan_local, outer_width)
    half_type, full_type = jnp.bfloat16, jnp.float32

    def shape(*dims, dtype=half_type):
        return jax.ShapeDtypeStruct(dims, dtype)

    rows_flat = alignment_input.reshape(sequences * local_rows, width)
    message_rows = part_rows + chan_local + sequences
    outer_weight_flat = outer_input_weight.transpose(1, 2, 0).reshape(2 * outer_width, width)
    (token,) = kernel_call(start_kernel, [shape(8, 128, dtype=full_type)], [], flops=5 * 10**9)
    hidden_local = transition_up_weight.shape[0]
    shared_rows = chan_local + sequences + 7 * chan_local
    same, other, shared = kernel_call(
        functools.partial(send_kernel, sizes),
        [shape(message_rows, width), shape(message_rows, width),
         shape(shared_rows, width)],
        [rows_flat, pairwise_input, product_gain[None], outer_weight_flat, triangle_input_weight,
         triangle_gate_weight, triangle_gain[None], triangle_output_weight.T, transition_up_weight,
         transition_down_weight, token],
        [pltpu.VMEM((sequences * local_rows, 128), full_type)],
    )
    shared_x = exchange(shared, "seq", 2)
    pair_two, rest_two = kernel_call(
        functools.partial(pack_kernel, chan_local),
        [shape(2 * chan_local, width), shape(2 * (shared_rows - chan_local), width)],
        [shared, shared_x],
    )
    pair_core = exchange(pair_two, "seq", 1)
    rest_core = exchange(rest_two, "seq", 1)
    from_three = exchange(other, "row", 3)
    from_two = exchange(same, "row", 2)
    from_one = exchange(other, "row", 1)
    received = (same, from_one, from_two, from_three)

    late_weight = lax.optimization_barrier((attention_weight, shared))[0]
    kept = [late_weight.reshape(width, 4 * heads), mixing_weight,
            outer_output_weight.reshape(outer_width * outer_width, pair_width),
            alignment_gain[None], pairwise_gain[None], transition_gain[None]]
    attention_kept, mixing_kept, outer_kept, row_gain, pair_gain, last_gain = kernel_call(
        keep_kernel, [shape(*a.shape, dtype=a.dtype) for a in kept], kept
    )

    def bias_body(*refs):
        bias_kernel(chan_local, local_rows, (refs[0], refs[1], refs[2].at[:chan_local], refs[2].at[chan_local:]), *refs[3:])

    (near_bias,) = kernel_call(
        bias_body,
        [shape(residues, groups * half)],
        [shared, shared_x, pair_core, bias_matrix.T],
        [
            pltpu.VMEM((pair_width, local_rows * residues), full_type),
        ],
        flops=BIAS_COST,
    )
    far_bias = exchange(near_bias, "row", 1)

    (relay,) = kernel_call(
        functools.partial(relay_kernel, sizes),
        [shape(2 * chan_local + 2 * sequences, width)],
        [*received, far_bias, row_gain],
    )
    relay_x = exchange(relay, "seq", 2)
    relay_core = exchange(relay, "seq", 1)
    relay_both = exchange(relay, "seq", 3)
    relays = (relay, relay_x, relay_core, relay_both)

    scores, values, gate = kernel_call(
        functools.partial(score_kernel, sizes),
        [shape(part * residues, groups * half, dtype=full_type), shape(part * residues, heads), shape(part * half, heads)],
        [*received, row_gain, attention_kept, relay],
        [pltpu.VMEM((part, residues, width), full_type)],
        flops=3 * 10**9,
    )

    near_here, near_there, far_here, far_there = kernel_call(
        functools.partial(mix_kernel, sizes),
        [shape(part_rows, width // 2)] * 4,
        [near_bias, far_bias, scores, values, gate, mixing_kept, same, from_one, rest_core, relay_core],
        [pltpu.VMEM((part, half, width), full_type)],
        flops=3 * 10**9,
    )
    axes = ("branch", "row")
    across = lax.axis_size("row")
    from_branch = exchange(near_there, axes, across)
    from_both = exchange(far_there, axes, across + 1)
    from_row = exchange(far_here, axes, 1)

    def pair_body(*refs):
        own, other, pair, rest = refs[:4]
        count = rest.shape[0] // 2
        row_refs = (own, other, pair.at[:chan_local], pair.at[chan_local:])
        rest_refs = (own.at[chan_local:], other.at[chan_local:], rest.at[:count], rest.at[count:])
        pair_kernel(sizes, row_refs, rest_refs, refs[4:8], *refs[8:11], sequences * 4, hidden_local, *refs[11:])

    (pair_done,) = kernel_call(
        pair_body,
        [shape(local_rows * half, chan_local)],
        [shared, shared_x, pair_core, rest_core, *relays, pair_gain, last_gain, outer_kept],
        [
            pltpu.VMEM((pair_width, local_rows * residues), half_type),
            pltpu.VMEM((2, pair_width, local_rows * residues), half_type),
            pltpu.VMEM((pair_width, pair_width), half_type),
            pltpu.VMEM((half * outer_width // 128, local_rows * outer_width, 128), full_type),
            pltpu.VMEM((local_rows * half, outer_width * outer_width), full_type),
            pltpu.VMEM((local_rows, residues, pair_width), full_type),
            pltpu.VMEM((local_rows * half, pair_width), full_type),
        ],
    )
    (arrived,) = kernel_call(arrive_kernel, [shape(8, 128, dtype=full_type)], [from_row])
    alignment_flat, pairwise_output = kernel_call(
        place_kernel,
        [shape(sequences * local_rows, width // 2), shape(local_rows * half, chan_local)],
        [near_here, from_branch, from_row, from_both, pair_done, arrived],
    )
    return (
        alignment_flat.reshape(sequences, local_rows, width // 2),
        pairwise_output.reshape(local_rows, half, chan_local).transpose(2, 0, 1),
    )


def is_compact(mesh, residues):
    return mesh.shape["row"] == 4 and mesh.shape["seq"] == 4 and mesh.shape["branch"] == 2


def solution(mesh):
    return jax.shard_map(
        compact_shards if is_compact(mesh, None) else shards,
        mesh=mesh,
        in_specs=(
            P("seq", "row", None),
            P("seq", "row", None),
            P(),
            P(),
            P(),
            P(),
            P(),
            P(),
            P(),
            P(),
            P(None, "seq", None),
            P("seq", None),
            P("seq"),
            P(None, "seq"),
            P(),
            P("seq", None),
            P(None, "seq"),
        ),
        out_specs=(P("seq", "row", "branch"), P("seq", "row", "branch")),
        check_vma=False,
    )
```

```python
import functools

import jax
import jax.numpy as jnp
from jax import lax
from jax.experimental import pallas as pl
from jax.experimental.pallas import tpu as pltpu
from jax.sharding import PartitionSpec as P

EPSILON = 1e-05


def shifted(value, axis, by):
    length = lax.axis_size(axis)
    pairs = [(i, i + by) for i in range(length) if 0 <= i + by < length]
    return lax.ppermute(value, axis, pairs)


def from_partner(value, axis, distance):
    return lax.ppermute(value, axis, [(i, i ^ 1 << distance) for i in range(lax.axis_size(axis))])


def layer_normalize(values, axis):
    average = jnp.mean(values, axis=axis, keepdims=True)
    centred = values - average
    spread = jnp.mean(centred * centred, axis=axis, keepdims=True)
    return centred * lax.rsqrt(spread + EPSILON)


def full_channels(values):
    return lax.all_gather(values, "seq", axis=0, tiled=True)


def channel_sum(term, kept_rows):
    return lax.psum_scatter(
        term(jnp.int32(0), kept_rows * lax.axis_size("seq")), "seq", scatter_dimension=0, tiled=True
    )


def shards(
    alignment_input,
    pairwise_input,
    alignment_gain,
    product_gain,
    attention_weight,
    mixing_weight,
    outer_input_weight,
    outer_output_weight,
    bias_matrix,
    pairwise_gain,
    triangle_input_weight,
    triangle_gate_weight,
    triangle_gain,
    triangle_output_weight,
    transition_gain,
    transition_up_weight,
    transition_down_weight,
):
    local_sequences, local_rows, alignment_channels = alignment_input.shape
    chan_local = pairwise_input.shape[0]
    residues = pairwise_input.shape[2]
    pair_width, head_total = bias_matrix.shape
    latent_heads = mixing_weight.shape[0]
    head_size = latent_heads // head_total
    outer_width = outer_input_weight.shape[2]
    tri_local = triangle_input_weight.shape[1]
    trans_local = transition_up_weight.shape[0]
    seq_total = local_sequences * lax.axis_size("seq")
    path_index = lax.axis_index("branch")
    alignment_branch = path_index == 0
    query_shape = (local_sequences, local_rows, latent_heads)
    pair_shape = (chan_local, local_rows, residues)
    full_pair_shape = (pair_width, local_rows, residues)
    key_shape = (local_sequences, 2 * latent_heads, local_rows)
    gathered = full_channels(pairwise_input)

    def alignment_early():
        alignment_module = layer_normalize(alignment_input.astype(jnp.float32), 2)
        normalized_values = (alignment_module * alignment_gain).astype(jnp.bfloat16)
        outer_normalized = (alignment_module * product_gain).astype(jnp.bfloat16)
        flattened_rows = normalized_values.reshape(-1, alignment_channels)
        outer_flattened = outer_normalized.reshape(-1, alignment_channels)
        query = (
            (
                jnp.dot(flattened_rows, attention_weight[:, 0], preferred_element_type=jnp.float32)
                * head_size ** (-0.5)
            )
            .astype(jnp.bfloat16)
            .reshape(query_shape)
        )
        gate = (
            jax.nn.sigmoid(
                jnp.dot(flattened_rows, attention_weight[:, 3], preferred_element_type=jnp.float32)
            )
            .astype(jnp.bfloat16)
            .reshape(query_shape)
        )
        key_values = (
            jnp.einsum(
                "sim,mkc->skci",
                normalized_values,
                attention_weight[:, 1:3],
                preferred_element_type=jnp.float32,
            )
            .astype(jnp.bfloat16)
            .reshape(key_shape)
        )
        left = (
            jnp.dot(outer_flattened, outer_input_weight[:, 0], preferred_element_type=jnp.float32)
            .astype(jnp.bfloat16)
            .reshape(local_sequences, local_rows, outer_width)
        )
        right_cols = jnp.einsum(
            "sim,mc->sci",
            outer_normalized,
            outer_input_weight[:, 1],
            preferred_element_type=jnp.float32,
        ).astype(jnp.bfloat16)
        empty_bias = jnp.zeros((head_total, local_rows, residues), jnp.bfloat16)
        empty_pair = jnp.zeros(full_pair_shape, jnp.bfloat16)
        return (empty_bias, empty_pair, query, key_values, gate, left, right_cols)

    def pair_early():
        unit = layer_normalize(gathered.astype(jnp.float32), 0)
        plain = unit.astype(jnp.bfloat16).reshape(pair_width, -1)
        bias_rows = (
            jnp.einsum("ch,cn->hn", bias_matrix, plain, preferred_element_type=jnp.float32)
            .astype(jnp.bfloat16)
            .reshape(head_total, local_rows, residues)
        )
        tri_input = (unit * pairwise_gain[:, None, None]).astype(jnp.bfloat16)
        empty_query = jnp.zeros(query_shape, jnp.bfloat16)
        empty_keys = jnp.zeros(key_shape, jnp.bfloat16)
        empty_left = jnp.zeros((local_sequences, local_rows, outer_width), jnp.bfloat16)
        empty_right = jnp.zeros((local_sequences, outer_width, local_rows), jnp.bfloat16)
        return (bias_rows, tri_input, empty_query, empty_keys, empty_query, empty_left, empty_right)

    bias_local, tri_input, query, key_values, gate, left, right_cols = lax.cond(
        alignment_branch, alignment_early, pair_early
    )
    bias_recv = shifted(bias_local, "branch", -1)
    query_heads = query.reshape(local_sequences, local_rows, head_total, head_size).transpose(
        0, 2, 1, 3
    )

    def fold_real(running, shard_part):
        highest, totals, weighted = running
        columns = shard_part.shape[2]
        keys_part = shard_part[:, :latent_heads].reshape(
            local_sequences, head_total, head_size, columns
        )
        values_part = shard_part[:, latent_heads:].reshape(
            local_sequences, head_total, head_size, columns
        )
        bias_part = bias_recv.astype(jnp.float32)
        scores = (
            jnp.einsum(
                "shid,shdj->shij", query_heads, keys_part, preferred_element_type=jnp.float32
            )
            + bias_part[None]
        )
        raised = jnp.maximum(highest, jnp.max(scores, axis=3))
        weights = jnp.exp(scores - raised[..., None])
        totals = jnp.sum(weights, axis=3)
        weighted = jnp.einsum(
            "shij,shdj->shid",
            weights.astype(jnp.bfloat16),
            values_part,
            preferred_element_type=jnp.float32,
        )
        return (raised, totals, weighted)

    initial = (
        jnp.full((local_sequences, head_total, local_rows), -1e30, jnp.float32),
        jnp.zeros((local_sequences, head_total, local_rows), jnp.float32),
        jnp.zeros((local_sequences, head_total, local_rows, head_size), jnp.float32),
    )
    shard_part = lax.all_gather(key_values, "row", axis=2, tiled=True)
    highest, totals, weighted = lax.cond(
        alignment_branch, lambda: fold_real(initial, shard_part), lambda: initial
    )
    safe_totals = jnp.where(totals > 0, totals, 1.0)
    attended = (weighted / safe_totals[..., None]).transpose(0, 2, 1, 3).reshape(query_shape)
    mixed_heads = (gate.astype(jnp.float32) * attended).astype(jnp.bfloat16)
    right_full = lax.all_gather(right_cols, "row", axis=2, tiled=True)
    right_matrix = right_full.reshape(local_sequences * outer_width, residues)
    spread = lax.cond(
        alignment_branch,
        lambda: jnp.einsum(
            "sic,cdo->oisd", left, outer_output_weight, preferred_element_type=jnp.float32
        ).astype(jnp.bfloat16),
        lambda: jnp.zeros((pair_width, local_rows, local_sequences, outer_width), jnp.bfloat16),
    )

    def outer_term(amount):
        spread_part = spread.reshape(amount * local_rows, local_sequences * outer_width)
        return jnp.dot(spread_part, right_matrix, preferred_element_type=jnp.float32).reshape(
            amount, local_rows, residues
        )

    tri_flat = tri_input.reshape(pair_width, -1)

    def pair_operands():
        linear = jnp.dot(
            triangle_input_weight.reshape(4 * tri_local, pair_width),
            tri_flat,
            preferred_element_type=jnp.float32,
        )
        linear = linear.reshape(4, tri_local, local_rows, residues)
        left_part = (linear[0] * jax.nn.sigmoid(linear[1])).astype(jnp.bfloat16)
        right_part = (linear[2] * jax.nn.sigmoid(linear[3])).astype(jnp.bfloat16)
        return (left_part, right_part)

    def empty_operands():
        empty = jnp.zeros((tri_local, local_rows, residues), jnp.bfloat16)
        return (empty, empty)

    left_tri, right_tri = lax.cond(alignment_branch, empty_operands, pair_operands)
    tri_shard_part = lax.all_gather(right_tri, "row", axis=1, tiled=True)
    triangle = lax.optimization_barrier(
        lax.cond(
            alignment_branch,
            lambda: jnp.zeros((tri_local, local_rows, tri_shard_part.shape[1]), jnp.float32),
            lambda: jnp.einsum(
                "cik,cjk->cij", left_tri, tri_shard_part, preferred_element_type=jnp.float32
            ),
        ).astype(jnp.bfloat16)
    )
    tri_float = triangle.astype(jnp.float32)
    summed, squared = lax.psum(
        (jnp.sum(tri_float, axis=0), jnp.sum(tri_float * tri_float, axis=0)), "seq"
    )
    tri_total = tri_local * lax.axis_size("seq")
    average = summed / tri_total
    variance = jnp.maximum(squared / tri_total - average * average, 0.0)
    tri_norm = (
        (tri_float - average) * lax.rsqrt(variance + EPSILON) * triangle_gain[:, None, None]
    ).astype(jnp.bfloat16)
    norm_flat = tri_norm.reshape(tri_local, -1)

    def tri_term(amount):
        return jnp.dot(
            triangle_output_weight, norm_flat, preferred_element_type=jnp.float32
        ).reshape(amount, local_rows, residues)

    def first_term(offset, amount):
        return lax.cond(alignment_branch, lambda: outer_term(amount), lambda: tri_term(amount))

    summed_first = channel_sum(first_term, chan_local)
    outer_increment = (summed_first * (1.0 / seq_total)).astype(jnp.bfloat16)
    gate_values = jax.nn.sigmoid(
        jnp.dot(triangle_gate_weight, tri_flat, preferred_element_type=jnp.float32)
    ).reshape(pair_shape)
    first_update = lax.optimization_barrier(
        (pairwise_input.astype(jnp.float32) + gate_values * summed_first).astype(jnp.bfloat16)
    )
    gathered_next = full_channels(first_update)

    def pair_hidden():
        trans_norm = (
            (layer_normalize(gathered_next.astype(jnp.float32), 0) * transition_gain[:, None, None])
            .astype(jnp.bfloat16)
            .reshape(pair_width, -1)
        )
        return jax.nn.relu(
            jnp.dot(transition_up_weight, trans_norm, preferred_element_type=jnp.float32)
        ).astype(jnp.bfloat16)

    hidden_units = lax.cond(
        alignment_branch,
        lambda: jnp.zeros((trans_local, local_rows * residues), jnp.bfloat16),
        pair_hidden,
    )

    def trans_real(amount):
        return jnp.dot(
            transition_down_weight, hidden_units, preferred_element_type=jnp.float32
        ).reshape(amount, local_rows, residues)

    def trans_term(offset, amount):
        return lax.cond(
            alignment_branch,
            lambda: jnp.zeros((amount, local_rows, residues), jnp.float32),
            lambda: trans_real(amount),
        )

    pair_following = (
        first_update.astype(jnp.float32) + channel_sum(trans_term, chan_local)
    ).astype(jnp.bfloat16)
    half_residues = residues // 2
    halved_width = alignment_channels // 2
    outgoing_product = jnp.where(
        alignment_branch,
        outer_increment[:, :, half_residues:],
        pair_following[:, :, :half_residues],
    )
    incoming = from_partner(outgoing_product, "branch", 0)
    local_half = jnp.where(
        alignment_branch,
        outer_increment[:, :, :half_residues],
        pair_following[:, :, half_residues:],
    )
    pairwise_output = (local_half.astype(jnp.float32) + incoming.astype(jnp.float32)).astype(
        jnp.bfloat16
    )
    mixed_received = shifted(mixed_heads, "branch", 1)
    mixed_applied = jnp.where(alignment_branch, mixed_heads, mixed_received)
    mix_columns = lax.dynamic_slice_in_dim(
        mixing_weight, path_index * halved_width, halved_width, 1
    )
    residual_stream = lax.dynamic_slice_in_dim(
        alignment_input, path_index * halved_width, halved_width, 2
    )
    projected_values = jnp.dot(
        mixed_applied.reshape(-1, latent_heads), mix_columns, preferred_element_type=jnp.float32
    )
    alignment_output = (
        residual_stream.astype(jnp.float32)
        + projected_values.reshape(local_sequences, local_rows, halved_width)
    ).astype(jnp.bfloat16)
    return (alignment_output, pairwise_output)


BIAS_COST = 175 * 10**6


def rounded(values):
    return values.astype(jnp.bfloat16)


def widened(values):
    return values.astype(jnp.float32)


def product(left, right, contract_left=1, contract_right=0):
    return lax.dot_general(
        left,
        right,
        (((contract_left,), (contract_right,)), ((), ())),
        preferred_element_type=jnp.float32,
    )


def head_mask(groups, rows, head_size):
    shape = (groups * rows, groups * head_size)
    row = lax.broadcasted_iota(jnp.int32, shape, 0) // rows
    return row == lax.broadcasted_iota(jnp.int32, shape, 1) // head_size


def same_group(rows, columns, group):
    row = lax.broadcasted_iota(jnp.int32, (rows, columns), 0) // group
    column = lax.broadcasted_iota(jnp.int32, (rows, columns), 1) // group
    return row == column


def as_column(row):
    size = row.shape[1]
    return jnp.sum(jnp.where(same_group(size, size, 1), row, 0.0), axis=1, keepdims=True)


def kernel_call(body, outputs, operands, scratch=(), flops=0, in_hbm=(), room=32 * 2**20):
    vmem = pl.BlockSpec(memory_space=pltpu.VMEM)
    hbm = pl.BlockSpec(memory_space=pltpu.HBM)
    size = sum(a.size * a.dtype.itemsize for a in operands)
    size += sum(o.size * o.dtype.itemsize for o in outputs)
    return pl.pallas_call(
        body,
        out_shape=outputs,
        in_specs=[hbm if i in in_hbm else vmem for i in range(len(operands))],
        out_specs=[vmem] * len(outputs),
        scratch_shapes=list(scratch),
        cost_estimate=pl.CostEstimate(flops=flops, bytes_accessed=size, transcendentals=0),
        compiler_params=pltpu.CompilerParams(vmem_limit_bytes=room),
    )(*operands)


def exchange(value, axes, distance):
    members = lax.axis_size(axes)
    return lax.ppermute(value, axes, [(i, i ^ distance) for i in range(members)])


def start_kernel(token_ref):
    token_ref[...] = jnp.zeros_like(token_ref)


def send_kernel(
    sizes, rows_ref, pair_ref, gain_ref, weight_ref, input_ref, gate_ref, tri_gain_ref, output_ref, up_ref,
    down_ref, token_ref, same_ref, other_ref, shared_ref, wide,
):
    sequences, local_rows, residues, chan_local, outer_width = sizes
    part = sequences // 4
    part_rows = part * local_rows
    pair = widened(pair_ref[...])
    flat_pair = rounded(jnp.concatenate([pair[:, i, :] for i in range(local_rows)], axis=1))
    shared_ref[0:chan_local, :] = flat_pair
    at = chan_local + sequences
    narrow = gate_ref.shape[1]
    scaled = rounded(widened(output_ref[...]) * as_column(tri_gain_ref[...]))
    kinds = [input_ref[kind] for kind in range(input_ref.shape[0])]
    down = down_ref[...]
    for block in (*kinds, gate_ref[...], scaled, down[:chan_local]):
        shared_ref[at : at + chan_local, :narrow] = block
        at += chan_local
    at = chan_local + sequences
    for block in (up_ref[...], down[chan_local:]):
        shared_ref[at : at + block.shape[0], narrow:] = block
        at += block.shape[0]
    same_ref[part_rows : part_rows + chan_local, :] = flat_pair
    other_ref[part_rows : part_rows + chan_local, :] = flat_pair
    unit_here = 2 * lax.axis_index("branch") + lax.rem(lax.axis_index("row"), 2)
    unit_other = 2 * lax.axis_index("branch") + 1 - lax.rem(lax.axis_index("row"), 2)
    same_ref[0:part_rows, :] = rows_ref[pl.ds(unit_here * part_rows, part_rows), :]
    other_ref[0:part_rows, :] = rows_ref[pl.ds(unit_other * part_rows, part_rows), :]
    normed = rounded(layer_normalize(widened(rows_ref[...]), 1) * gain_ref[...])
    wide[:, 0 : 2 * outer_width] = product(normed, weight_ref[...], 1, 1)
    base = part_rows + chan_local
    for i in range(local_rows):
        both = rounded(wide[pl.ds(i, sequences, stride=local_rows), :])
        lanes = slice(i * outer_width, (i + 1) * outer_width)
        shared_ref[chan_local : chan_local + sequences, lanes] = both[:, :outer_width]
        same_ref[base : base + sequences, lanes] = both[:, outer_width : 2 * outer_width]
    other_ref[base : base + sequences, :] = same_ref[base : base + sequences, :]


def pack_kernel(chan_local, own_ref, other_ref, pair_ref, rest_ref):
    rest = own_ref.shape[0] - chan_local
    for k, ref in enumerate((own_ref, other_ref)):
        pair_ref[k * chan_local : (k + 1) * chan_local, :] = ref[:chan_local, :]
        rest_ref[k * rest : (k + 1) * rest, :] = ref[chan_local:, :]


def keep_kernel(*refs):
    count = len(refs) // 2
    for source, target in zip(refs[:count], refs[count:]):
        target[...] = source[...]


def arrive_kernel(*refs):
    refs[-1][...] = jnp.zeros_like(refs[-1])


def relay_kernel(sizes, own_ref, one_ref, two_ref, three_ref, after_bias_ref, after_keep_ref, relay_ref):
    sequences, local_rows, residues, chan_local, outer_width = sizes
    part_rows = sequences // 4 * local_rows
    row = lax.axis_index("row")
    branch = lax.axis_index("branch")
    base = part_rows + chan_local
    for distance, ref in enumerate((own_ref, one_ref, two_ref, three_ref)):
        shard = row ^ distance

        @pl.when(shard // 2 == branch)
        def _():
            place = lax.rem(shard, 2)
            relay_ref[pl.ds(pl.multiple_of(place * chan_local, chan_local), chan_local), :] = ref[
                part_rows:base, :
            ]
            start = 2 * chan_local + place * sequences
            relay_ref[pl.ds(pl.multiple_of(start, chan_local), sequences), :] = ref[
                base : base + sequences, :
            ]


def score_kernel(
    sizes, own_ref, one_ref, two_ref, three_ref, gain_ref, weight_ref, *refs,
):
    score_ref, values_ref, gate_ref, module = refs[-4:]
    sequences, local_rows, residues, chan_local, outer_width = sizes
    part = sequences // 4
    part_rows = part * local_rows
    width = gain_ref.shape[1]
    row = lax.axis_index("row")
    for distance, ref in enumerate((own_ref, one_ref, two_ref, three_ref)):
        shard = row ^ distance
        block = widened(ref[0:part_rows, :])
        unit = layer_normalize(block, 1) * gain_ref[...]
        module[:, pl.ds(pl.multiple_of(shard * local_rows, local_rows), local_rows), :] = unit.reshape(
            part, local_rows, width
        )
    normed = rounded(module[...].reshape(part * residues, width))
    half = residues // 2
    here = module[:, pl.ds(pl.multiple_of(row // 2 * half, half), half), :]
    query_rows = rounded(here.reshape(part * half, width))
    heads = values_ref.shape[1]
    groups = score_ref.shape[1] // half
    head_size = heads // groups
    query = rounded(product(query_rows, weight_ref[:, 0:heads]) * head_size ** (-0.5))
    keys = rounded(product(normed, weight_ref[:, heads : 2 * heads]))
    values_ref[...] = rounded(product(normed, weight_ref[:, 2 * heads : 3 * heads]))
    gate_ref[...] = rounded(jax.nn.sigmoid(product(query_rows, weight_ref[:, 3 * heads :])))
    mask = head_mask(groups, half, head_size)
    for s in range(part):
        one = query[s * half : (s + 1) * half]
        spread = jnp.where(mask, jnp.concatenate([one] * groups, axis=0), jnp.bfloat16(0))
        score_ref[s * residues : (s + 1) * residues, :] = product(
            keys[s * residues : (s + 1) * residues], spread, 1, 1
        )


def bias_kernel(chan_local, local_rows, pair_refs, matrix_ref, bias_ref, full):
    groups = matrix_ref.shape[0]
    residues = bias_ref.shape[0]
    seq = lax.axis_index("seq")
    for distance, ref in zip((0, 2, 1, 3), pair_refs):
        place = pl.ds(pl.multiple_of((seq ^ distance) * chan_local, chan_local), chan_local)
        full[place, :] = widened(ref[0:chan_local, :])
    plain = rounded(layer_normalize(full[...], 0))
    bias = rounded(product(matrix_ref[...], plain).T)
    lanes = bias_ref.shape[1]
    half = lanes // groups
    head = lax.broadcasted_iota(jnp.int32, (groups, lanes), 0)
    lane = lax.broadcasted_iota(jnp.int32, (groups, lanes), 1)
    first = lax.rem(lax.axis_index("row"), 2) * local_rows
    total = jnp.zeros(bias_ref.shape, jnp.float32)
    for i in range(local_rows):
        pick = jnp.where(lane == head * half + first + i, jnp.bfloat16(1), jnp.bfloat16(0))
        total += product(bias[i * residues : (i + 1) * residues, :], pick)
    bias_ref[...] = rounded(total)


def mix_kernel(
    sizes, near_bias_ref, far_bias_ref, score_ref, values_ref, gate_ref, mixing_ref, own_ref, one_ref, *refs,
):
    near_here_ref, near_there_ref, far_here_ref, far_there_ref, module = refs[-5:]
    sequences, local_rows, residues, chan_local, outer_width = sizes
    part = sequences // 4
    part_rows = part * local_rows
    half = residues // 2
    heads = values_ref.shape[1]
    groups = score_ref.shape[1] // half
    head_size = heads // groups
    row = lax.axis_index("row")
    branch = lax.axis_index("branch")
    bias = widened(near_bias_ref[...]) + widened(far_bias_ref[...])
    scores = score_ref[...].reshape(part, residues, groups * half) + bias[None]
    weights = jnp.exp(scores - jnp.max(scores, axis=1, keepdims=True))
    weights = rounded(weights / jnp.sum(weights, axis=1, keepdims=True))
    mask = head_mask(groups, half, head_size)
    attended = []
    for s in range(part):
        every = product(weights[s], values_ref[s * residues : (s + 1) * residues, :], 0, 0)
        every = jnp.where(mask, every, 0.0).reshape(groups, half, heads)
        attended.append(jnp.sum(every, axis=0))
    mixed = rounded(widened(gate_ref[...]) * jnp.concatenate(attended, axis=0))
    projected = product(mixed, mixing_ref[...])
    width = projected.shape[1]
    module[...] = projected.reshape(part, half, width)
    halved = width // 2
    for distance, ref, here, there in (
        (0, own_ref, near_here_ref, near_there_ref),
        (1, one_ref, far_here_ref, far_there_ref),
    ):
        place = lax.rem(row, 2) ^ distance
        update = module[:, pl.ds(pl.multiple_of(place * local_rows, local_rows), local_rows), :]
        result = rounded(widened(ref[0:part_rows, :]) + update.reshape(part_rows, width))
        low, high = result[:, :halved], result[:, halved:]
        here[...] = jnp.where(branch == 0, low, high)
        there[...] = jnp.where(branch == 0, high, low)


def place_kernel(own_ref, branch_ref, row_ref, both_ref, pair_ref, token_ref, output_ref, pair_output_ref):
    pair_output_ref[...] = pair_ref[...]
    rows = own_ref.shape[0]
    branch = lax.axis_index("branch")
    parity = lax.rem(lax.axis_index("row"), 2)
    for flip_branch, flip_row, ref in (
        (0, 0, own_ref),
        (1, 0, branch_ref),
        (0, 1, row_ref),
        (1, 1, both_ref),
    ):
        unit = 2 * (branch ^ flip_branch) + (parity ^ flip_row)
        output_ref[pl.ds(pl.multiple_of(unit * rows, rows), rows), :] = ref[...]


def pair_kernel(
    sizes, row_refs, rest_refs, pair_refs, gain_ref, transition_gain_ref, outer_weight_ref, seq_total, hidden_local,
    output_ref, rows, columns, gates, outer, outer_flat, ordered, final,
):
    sequences, local_rows, residues, chan_local, outer_width = sizes
    half = residues // 2
    branch = lax.axis_index("branch")
    seq = lax.axis_index("seq")
    width = 4 * chan_local
    chan = chan_local
    gain = as_column(gain_ref[...])
    weight_refs = [ref.at[sequences:, 0:width] for ref in rest_refs]
    hidden_refs = [ref.at[sequences:, width:] for ref in rest_refs]
    for distance, row_ref, pair_ref, weight_ref in zip((0, 2, 1, 3), row_refs, pair_refs, weight_refs):
        place = pl.ds(pl.multiple_of((seq ^ distance) * chan, chan), chan)
        rows[place, :] = row_ref[0:chan, :]
        for k in range(2):
            columns[k, place, :] = pair_ref[k * chan : (k + 1) * chan, :]
        gates[place, :] = weight_ref[4 * chan : 5 * chan, :]

    def projection(values, kind):
        weights = jnp.concatenate([w[kind * chan : (kind + 1) * chan, :] for w in weight_refs], axis=0)
        return product(values, weights, 1, 1)

    raw = widened(rows[...])
    row_input = rounded((layer_normalize(raw, 0) * gain).T)
    left = widened(
        rounded(projection(row_input, 0) * jax.nn.sigmoid(projection(row_input, 1)))
    ).reshape(local_rows, residues, width)
    right = []
    for k in range(2):
        column_input = rounded((layer_normalize(widened(columns[k]), 0) * gain).T)
        right.append(
            widened(
                rounded(projection(column_input, 2) * jax.nn.sigmoid(projection(column_input, 3)))
            ).reshape(local_rows, residues, width)
        )
    right = jnp.concatenate(right, axis=0)
    triangle = jnp.concatenate(
        [jnp.sum(left[i][None] * right, axis=1) for i in range(local_rows)], axis=0
    )
    triangle = widened(rounded(triangle))
    tri_norm = rounded(layer_normalize(triangle, 1))
    output_weight = jnp.concatenate([w[5 * chan : 6 * chan, :] for w in weight_refs], axis=0)
    tri_out = product(tri_norm, output_weight)
    ordered[...] = raw.T.reshape(local_rows, residues, width)
    place = pl.ds(pl.multiple_of(branch * half, half), half)
    raw_here = ordered[:, place, :].reshape(local_rows * half, width)
    ordered[...] = widened(row_input).reshape(local_rows, residues, width)
    input_here = rounded(ordered[:, place, :].reshape(local_rows * half, width))
    gate = jax.nn.sigmoid(product(input_here, gates[...], 1, 1))
    first_update = widened(rounded(raw_here + gate * tri_out))
    trans_norm = rounded(layer_normalize(first_update, 1) * transition_gain_ref[...])
    down = jnp.zeros((local_rows * half, width), jnp.float32)
    for w, h in zip(weight_refs, hidden_refs):
        hidden = rounded(jax.nn.relu(product(trans_norm, h[0:hidden_local, :], 1, 1)))
        down_weight = jnp.concatenate([w[6 * chan : 7 * chan, :], h[hidden_local : hidden_local + 3 * chan, :]], axis=0)
        down += product(hidden, down_weight, 1, 1)
    pair_next = widened(rounded(first_update + down))

    lefts = jnp.concatenate([ref[:sequences, :] for ref in rest_refs], axis=0)
    base = 2 * chan
    rights = jnp.concatenate(
        [
            jnp.concatenate([p[base : base + sequences, :], p[base + sequences :, :]], axis=1)
            for p in pair_refs
        ],
        axis=0,
    )
    outer_all = product(rounded(widened(lefts).T), rights)
    each = 128 // outer_width
    for tile in range(half // each):
        outer[tile] = outer_all[:, tile * 128 : (tile + 1) * 128]
        for c in range(outer_width):
            strip = outer[tile, pl.ds(c, local_rows, stride=outer_width), :]
            for k in range(each):
                j = tile * each + k
                outer_flat[
                    j * local_rows : (j + 1) * local_rows, c * outer_width : (c + 1) * outer_width
                ] = strip[:, k * outer_width : (k + 1) * outer_width]
    final[...] = product(rounded(outer_flat[...]), outer_weight_ref[...]) * (1.0 / seq_total)
    outer_update = jnp.concatenate(
        [final[pl.ds(i, half, stride=local_rows), :] for i in range(local_rows)], axis=0
    )
    outer_update = widened(rounded(outer_update))
    result = pair_next + outer_update
    own = result[:, 0:chan]
    for k in range(1, 4):
        own = jnp.where(seq == k, result[:, k * chan : (k + 1) * chan], own)
    output_ref[...] = rounded(own)


def compact_shards(
    alignment_input, pairwise_input, alignment_gain, product_gain, attention_weight, mixing_weight,
    outer_input_weight, outer_output_weight, bias_matrix, pairwise_gain, triangle_input_weight,
    triangle_gate_weight, triangle_gain, triangle_output_weight, transition_gain,
    transition_up_weight, transition_down_weight,
):
    sequences, local_rows, width = alignment_input.shape
    chan_local, _, residues = pairwise_input.shape
    pair_width, groups = bias_matrix.shape
    heads = mixing_weight.shape[0]
    outer_width = outer_input_weight.shape[2]
    part = sequences // 4
    part_rows = part * local_rows
    half = residues // 2
    sizes = (sequences, local_rows, residues, chan_local, outer_width)
    half_type, full_type = jnp.bfloat16, jnp.float32

    def shape(*dims, dtype=half_type):
        return jax.ShapeDtypeStruct(dims, dtype)

    rows_flat = alignment_input.reshape(sequences * local_rows, width)
    message_rows = part_rows + chan_local + sequences
    outer_weight_flat = outer_input_weight.transpose(1, 2, 0).reshape(2 * outer_width, width)
    (token,) = kernel_call(start_kernel, [shape(8, 128, dtype=full_type)], [], flops=5 * 10**9)
    hidden_local = transition_up_weight.shape[0]
    shared_rows = chan_local + sequences + 7 * chan_local
    same, other, shared = kernel_call(
        functools.partial(send_kernel, sizes),
        [shape(message_rows, width), shape(message_rows, width),
         shape(shared_rows, width)],
        [rows_flat, pairwise_input, product_gain[None], outer_weight_flat, triangle_input_weight,
         triangle_gate_weight, triangle_gain[None], triangle_output_weight.T, transition_up_weight,
         transition_down_weight, token],
        [pltpu.VMEM((sequences * local_rows, 128), full_type)],
    )
    shared_x = exchange(shared, "seq", 2)
    pair_two, rest_two = kernel_call(
        functools.partial(pack_kernel, chan_local),
        [shape(2 * chan_local, width), shape(2 * (shared_rows - chan_local), width)],
        [shared, shared_x],
    )
    pair_core = exchange(pair_two, "seq", 1)
    rest_core = exchange(rest_two, "seq", 1)
    from_three = exchange(other, "row", 3)
    from_two = exchange(same, "row", 2)
    from_one = exchange(other, "row", 1)
    received = (same, from_one, from_two, from_three)

    late_weight = lax.optimization_barrier((attention_weight, shared))[0]
    kept = [late_weight.reshape(width, 4 * heads), mixing_weight,
            outer_output_weight.reshape(outer_width * outer_width, pair_width),
            alignment_gain[None], pairwise_gain[None], transition_gain[None]]
    attention_kept, mixing_kept, outer_kept, row_gain, pair_gain, last_gain = kernel_call(
        keep_kernel, [shape(*a.shape, dtype=a.dtype) for a in kept], kept
    )

    def bias_body(*refs):
        bias_kernel(chan_local, local_rows, (refs[0], refs[1], refs[2].at[:chan_local], refs[2].at[chan_local:]), *refs[3:])

    (near_bias,) = kernel_call(
        bias_body,
        [shape(residues, groups * half)],
        [shared, shared_x, pair_core, bias_matrix.T],
        [
            pltpu.VMEM((pair_width, local_rows * residues), full_type),
        ],
        flops=BIAS_COST,
    )
    far_bias = exchange(near_bias, "row", 1)

    (relay,) = kernel_call(
        functools.partial(relay_kernel, sizes),
        [shape(2 * chan_local + 2 * sequences, width)],
        [*received, far_bias, row_gain],
    )
    relay_x = exchange(relay, "seq", 2)
    relay_core = exchange(relay, "seq", 1)
    relay_both = exchange(relay, "seq", 3)
    relays = (relay, relay_x, relay_core, relay_both)

    scores, values, gate = kernel_call(
        functools.partial(score_kernel, sizes),
        [shape(part * residues, groups * half, dtype=full_type), shape(part * residues, heads), shape(part * half, heads)],
        [*received, row_gain, attention_kept, relay],
        [pltpu.VMEM((part, residues, width), full_type)],
        flops=3 * 10**9,
    )

    near_here, near_there, far_here, far_there = kernel_call(
        functools.partial(mix_kernel, sizes),
        [shape(part_rows, width // 2)] * 4,
        [near_bias, far_bias, scores, values, gate, mixing_kept, same, from_one, rest_core, relay_core],
        [pltpu.VMEM((part, half, width), full_type)],
        flops=3 * 10**9,
    )
    axes = ("branch", "row")
    across = lax.axis_size("row")
    from_branch = exchange(near_there, axes, across)
    from_both = exchange(far_there, axes, across + 1)
    from_row = exchange(far_here, axes, 1)

    def pair_body(*refs):
        own, other, pair, rest = refs[:4]
        count = rest.shape[0] // 2
        row_refs = (own, other, pair.at[:chan_local], pair.at[chan_local:])
        rest_refs = (own.at[chan_local:], other.at[chan_local:], rest.at[:count], rest.at[count:])
        pair_kernel(sizes, row_refs, rest_refs, refs[4:8], *refs[8:11], sequences * 4, hidden_local, *refs[11:])

    (pair_done,) = kernel_call(
        pair_body,
        [shape(local_rows * half, chan_local)],
        [shared, shared_x, pair_core, rest_core, *relays, pair_gain, last_gain, outer_kept],
        [
            pltpu.VMEM((pair_width, local_rows * residues), half_type),
            pltpu.VMEM((2, pair_width, local_rows * residues), half_type),
            pltpu.VMEM((pair_width, pair_width), half_type),
            pltpu.VMEM((half * outer_width // 128, local_rows * outer_width, 128), full_type),
            pltpu.VMEM((local_rows * half, outer_width * outer_width), full_type),
            pltpu.VMEM((local_rows, residues, pair_width), full_type),
            pltpu.VMEM((local_rows * half, pair_width), full_type),
        ],
    )
    (arrived,) = kernel_call(arrive_kernel, [shape(8, 128, dtype=full_type)], [from_row])
    alignment_flat, pairwise_output = kernel_call(
        place_kernel,
        [shape(sequences * local_rows, width // 2), shape(local_rows * half, chan_local)],
        [near_here, from_branch, from_row, from_both, pair_done, arrived],
    )
    return (
        alignment_flat.reshape(sequences, local_rows, width // 2),
        pairwise_output.reshape(local_rows, half, chan_local).transpose(2, 0, 1),
    )


def is_compact(mesh):
    return (mesh.shape["branch"], mesh.shape["row"], mesh.shape["seq"]) == (2, 4, 4)


def solution(mesh):
    return jax.shard_map(
        compact_shards if is_compact(mesh) else shards,
        mesh=mesh,
        in_specs=(
            P("seq", "row", None),
            P("seq", "row", None),
            P(),
            P(),
            P(),
            P(),
            P(),
            P(),
            P(),
            P(),
            P(None, "seq", None),
            P("seq", None),
            P("seq"),
            P(None, "seq"),
            P(),
            P("seq", None),
            P(None, "seq"),
        ),
        out_specs=(P("seq", "row", "branch"), P("seq", "row", "branch")),
        check_vma=False,
    )
```

```python
import functools

import jax
import jax.numpy as jnp
from jax import lax
from jax.experimental import pallas as pl
from jax.experimental.pallas import tpu as pltpu
from jax.sharding import PartitionSpec as P

EPSILON = 1e-05


def shifted(value, axis, by):
    length = lax.axis_size(axis)
    pairs = [(i, i + by) for i in range(length) if 0 <= i + by < length]
    return lax.ppermute(value, axis, pairs)


def from_partner(value, axis, distance):
    return lax.ppermute(value, axis, [(i, i ^ 1 << distance) for i in range(lax.axis_size(axis))])


def layer_normalize(values, axis):
    average = jnp.mean(values, axis=axis, keepdims=True)
    centred = values - average
    spread = jnp.mean(centred * centred, axis=axis, keepdims=True)
    return centred * lax.rsqrt(spread + EPSILON)


def full_channels(values):
    return lax.all_gather(values, "seq", axis=0, tiled=True)


def channel_sum(term, kept_rows):
    return lax.psum_scatter(
        term(jnp.int32(0), kept_rows * lax.axis_size("seq")), "seq", scatter_dimension=0, tiled=True
    )


def shards(
    alignment_input,
    pairwise_input,
    alignment_gain,
    product_gain,
    attention_weight,
    mixing_weight,
    outer_input_weight,
    outer_output_weight,
    bias_matrix,
    pairwise_gain,
    triangle_input_weight,
    triangle_gate_weight,
    triangle_gain,
    triangle_output_weight,
    transition_gain,
    transition_up_weight,
    transition_down_weight,
):
    local_sequences, local_rows, alignment_channels = alignment_input.shape
    chan_local = pairwise_input.shape[0]
    residues = pairwise_input.shape[2]
    pair_width, head_total = bias_matrix.shape
    latent_heads = mixing_weight.shape[0]
    head_size = latent_heads // head_total
    outer_width = outer_input_weight.shape[2]
    tri_local = triangle_input_weight.shape[1]
    trans_local = transition_up_weight.shape[0]
    seq_total = local_sequences * lax.axis_size("seq")
    path_index = lax.axis_index("branch")
    alignment_branch = path_index == 0
    query_shape = (local_sequences, local_rows, latent_heads)
    pair_shape = (chan_local, local_rows, residues)
    full_pair_shape = (pair_width, local_rows, residues)
    key_shape = (local_sequences, 2 * latent_heads, local_rows)
    gathered = full_channels(pairwise_input)

    def alignment_early():
        alignment_module = layer_normalize(alignment_input.astype(jnp.float32), 2)
        normalized_values = (alignment_module * alignment_gain).astype(jnp.bfloat16)
        outer_normalized = (alignment_module * product_gain).astype(jnp.bfloat16)
        flattened_rows = normalized_values.reshape(-1, alignment_channels)
        outer_flattened = outer_normalized.reshape(-1, alignment_channels)
        query = (
            (
                jnp.dot(flattened_rows, attention_weight[:, 0], preferred_element_type=jnp.float32)
                * head_size ** (-0.5)
            )
            .astype(jnp.bfloat16)
            .reshape(query_shape)
        )
        gate = (
            jax.nn.sigmoid(
                jnp.dot(flattened_rows, attention_weight[:, 3], preferred_element_type=jnp.float32)
            )
            .astype(jnp.bfloat16)
            .reshape(query_shape)
        )
        key_values = (
            jnp.einsum(
                "sim,mkc->skci",
                normalized_values,
                attention_weight[:, 1:3],
                preferred_element_type=jnp.float32,
            )
            .astype(jnp.bfloat16)
            .reshape(key_shape)
        )
        left = (
            jnp.dot(outer_flattened, outer_input_weight[:, 0], preferred_element_type=jnp.float32)
            .astype(jnp.bfloat16)
            .reshape(local_sequences, local_rows, outer_width)
        )
        right_cols = jnp.einsum(
            "sim,mc->sci",
            outer_normalized,
            outer_input_weight[:, 1],
            preferred_element_type=jnp.float32,
        ).astype(jnp.bfloat16)
        empty_bias = jnp.zeros((head_total, local_rows, residues), jnp.bfloat16)
        empty_pair = jnp.zeros(full_pair_shape, jnp.bfloat16)
        return (empty_bias, empty_pair, query, key_values, gate, left, right_cols)

    def pair_early():
        unit = layer_normalize(gathered.astype(jnp.float32), 0)
        plain = unit.astype(jnp.bfloat16).reshape(pair_width, -1)
        bias_rows = (
            jnp.einsum("ch,cn->hn", bias_matrix, plain, preferred_element_type=jnp.float32)
            .astype(jnp.bfloat16)
            .reshape(head_total, local_rows, residues)
        )
        tri_input = (unit * pairwise_gain[:, None, None]).astype(jnp.bfloat16)
        empty_query = jnp.zeros(query_shape, jnp.bfloat16)
        empty_keys = jnp.zeros(key_shape, jnp.bfloat16)
        empty_left = jnp.zeros((local_sequences, local_rows, outer_width), jnp.bfloat16)
        empty_right = jnp.zeros((local_sequences, outer_width, local_rows), jnp.bfloat16)
        return (bias_rows, tri_input, empty_query, empty_keys, empty_query, empty_left, empty_right)

    bias_local, tri_input, query, key_values, gate, left, right_cols = lax.cond(
        alignment_branch, alignment_early, pair_early
    )
    bias_recv = shifted(bias_local, "branch", -1)
    query_heads = query.reshape(local_sequences, local_rows, head_total, head_size).transpose(
        0, 2, 1, 3
    )

    def fold_real(running, shard_part):
        highest, totals, weighted = running
        columns = shard_part.shape[2]
        keys_part = shard_part[:, :latent_heads].reshape(
            local_sequences, head_total, head_size, columns
        )
        values_part = shard_part[:, latent_heads:].reshape(
            local_sequences, head_total, head_size, columns
        )
        bias_part = bias_recv.astype(jnp.float32)
        scores = (
            jnp.einsum(
                "shid,shdj->shij", query_heads, keys_part, preferred_element_type=jnp.float32
            )
            + bias_part[None]
        )
        raised = jnp.maximum(highest, jnp.max(scores, axis=3))
        weights = jnp.exp(scores - raised[..., None])
        totals = jnp.sum(weights, axis=3)
        weighted = jnp.einsum(
            "shij,shdj->shid",
            weights.astype(jnp.bfloat16),
            values_part,
            preferred_element_type=jnp.float32,
        )
        return (raised, totals, weighted)

    initial = (
        jnp.full((local_sequences, head_total, local_rows), -1e30, jnp.float32),
        jnp.zeros((local_sequences, head_total, local_rows), jnp.float32),
        jnp.zeros((local_sequences, head_total, local_rows, head_size), jnp.float32),
    )
    shard_part = lax.all_gather(key_values, "row", axis=2, tiled=True)
    highest, totals, weighted = lax.cond(
        alignment_branch, lambda: fold_real(initial, shard_part), lambda: initial
    )
    safe_totals = jnp.where(totals > 0, totals, 1.0)
    attended = (weighted / safe_totals[..., None]).transpose(0, 2, 1, 3).reshape(query_shape)
    mixed_heads = (gate.astype(jnp.float32) * attended).astype(jnp.bfloat16)
    right_full = lax.all_gather(right_cols, "row", axis=2, tiled=True)
    right_matrix = right_full.reshape(local_sequences * outer_width, residues)
    spread = lax.cond(
        alignment_branch,
        lambda: jnp.einsum(
            "sic,cdo->oisd", left, outer_output_weight, preferred_element_type=jnp.float32
        ).astype(jnp.bfloat16),
        lambda: jnp.zeros((pair_width, local_rows, local_sequences, outer_width), jnp.bfloat16),
    )

    def outer_term(amount):
        spread_part = spread.reshape(amount * local_rows, local_sequences * outer_width)
        return jnp.dot(spread_part, right_matrix, preferred_element_type=jnp.float32).reshape(
            amount, local_rows, residues
        )

    tri_flat = tri_input.reshape(pair_width, -1)

    def pair_operands():
        linear = jnp.dot(
            triangle_input_weight.reshape(4 * tri_local, pair_width),
            tri_flat,
            preferred_element_type=jnp.float32,
        )
        linear = linear.reshape(4, tri_local, local_rows, residues)
        left_part = (linear[0] * jax.nn.sigmoid(linear[1])).astype(jnp.bfloat16)
        right_part = (linear[2] * jax.nn.sigmoid(linear[3])).astype(jnp.bfloat16)
        return (left_part, right_part)

    def empty_operands():
        empty = jnp.zeros((tri_local, local_rows, residues), jnp.bfloat16)
        return (empty, empty)

    left_tri, right_tri = lax.cond(alignment_branch, empty_operands, pair_operands)
    tri_shard_part = lax.all_gather(right_tri, "row", axis=1, tiled=True)
    triangle = lax.optimization_barrier(
        lax.cond(
            alignment_branch,
            lambda: jnp.zeros((tri_local, local_rows, tri_shard_part.shape[1]), jnp.float32),
            lambda: jnp.einsum(
                "cik,cjk->cij", left_tri, tri_shard_part, preferred_element_type=jnp.float32
            ),
        ).astype(jnp.bfloat16)
    )
    tri_float = triangle.astype(jnp.float32)
    summed, squared = lax.psum(
        (jnp.sum(tri_float, axis=0), jnp.sum(tri_float * tri_float, axis=0)), "seq"
    )
    tri_total = tri_local * lax.axis_size("seq")
    average = summed / tri_total
    variance = jnp.maximum(squared / tri_total - average * average, 0.0)
    tri_norm = (
        (tri_float - average) * lax.rsqrt(variance + EPSILON) * triangle_gain[:, None, None]
    ).astype(jnp.bfloat16)
    norm_flat = tri_norm.reshape(tri_local, -1)

    def tri_term(amount):
        return jnp.dot(
            triangle_output_weight, norm_flat, preferred_element_type=jnp.float32
        ).reshape(amount, local_rows, residues)

    def first_term(offset, amount):
        return lax.cond(alignment_branch, lambda: outer_term(amount), lambda: tri_term(amount))

    summed_first = channel_sum(first_term, chan_local)
    outer_increment = (summed_first * (1.0 / seq_total)).astype(jnp.bfloat16)
    gate_values = jax.nn.sigmoid(
        jnp.dot(triangle_gate_weight, tri_flat, preferred_element_type=jnp.float32)
    ).reshape(pair_shape)
    first_update = lax.optimization_barrier(
        (pairwise_input.astype(jnp.float32) + gate_values * summed_first).astype(jnp.bfloat16)
    )
    gathered_next = full_channels(first_update)

    def pair_hidden():
        trans_norm = (
            (layer_normalize(gathered_next.astype(jnp.float32), 0) * transition_gain[:, None, None])
            .astype(jnp.bfloat16)
            .reshape(pair_width, -1)
        )
        return jax.nn.relu(
            jnp.dot(transition_up_weight, trans_norm, preferred_element_type=jnp.float32)
        ).astype(jnp.bfloat16)

    hidden_units = lax.cond(
        alignment_branch,
        lambda: jnp.zeros((trans_local, local_rows * residues), jnp.bfloat16),
        pair_hidden,
    )

    def trans_real(amount):
        return jnp.dot(
            transition_down_weight, hidden_units, preferred_element_type=jnp.float32
        ).reshape(amount, local_rows, residues)

    def trans_term(offset, amount):
        return lax.cond(
            alignment_branch,
            lambda: jnp.zeros((amount, local_rows, residues), jnp.float32),
            lambda: trans_real(amount),
        )

    pair_following = (
        first_update.astype(jnp.float32) + channel_sum(trans_term, chan_local)
    ).astype(jnp.bfloat16)
    half_residues = residues // 2
    halved_width = alignment_channels // 2
    outgoing_product = jnp.where(
        alignment_branch,
        outer_increment[:, :, half_residues:],
        pair_following[:, :, :half_residues],
    )
    incoming = from_partner(outgoing_product, "branch", 0)
    local_half = jnp.where(
        alignment_branch,
        outer_increment[:, :, :half_residues],
        pair_following[:, :, half_residues:],
    )
    pairwise_output = (local_half.astype(jnp.float32) + incoming.astype(jnp.float32)).astype(
        jnp.bfloat16
    )
    mixed_received = shifted(mixed_heads, "branch", 1)
    mixed_applied = jnp.where(alignment_branch, mixed_heads, mixed_received)
    mix_columns = lax.dynamic_slice_in_dim(
        mixing_weight, path_index * halved_width, halved_width, 1
    )
    residual_stream = lax.dynamic_slice_in_dim(
        alignment_input, path_index * halved_width, halved_width, 2
    )
    projected_values = jnp.dot(
        mixed_applied.reshape(-1, latent_heads), mix_columns, preferred_element_type=jnp.float32
    )
    alignment_output = (
        residual_stream.astype(jnp.float32)
        + projected_values.reshape(local_sequences, local_rows, halved_width)
    ).astype(jnp.bfloat16)
    return (alignment_output, pairwise_output)


BIAS_COST = 175 * 10**6


def rounded(values):
    return values.astype(jnp.bfloat16)


def widened(values):
    return values.astype(jnp.float32)


def product(left, right, contract_left=1, contract_right=0):
    return lax.dot_general(
        left,
        right,
        (((contract_left,), (contract_right,)), ((), ())),
        preferred_element_type=jnp.float32,
    )


def head_mask(groups, rows, head_size):
    shape = (groups * rows, groups * head_size)
    row = lax.broadcasted_iota(jnp.int32, shape, 0) // rows
    return row == lax.broadcasted_iota(jnp.int32, shape, 1) // head_size


def same_group(rows, columns, group):
    row = lax.broadcasted_iota(jnp.int32, (rows, columns), 0) // group
    column = lax.broadcasted_iota(jnp.int32, (rows, columns), 1) // group
    return row == column


def as_column(row):
    size = row.shape[1]
    return jnp.sum(jnp.where(same_group(size, size, 1), row, 0.0), axis=1, keepdims=True)


def kernel_call(body, outputs, operands, scratch=(), flops=0, in_hbm=(), room=32 * 2**20):
    vmem = pl.BlockSpec(memory_space=pltpu.VMEM)
    hbm = pl.BlockSpec(memory_space=pltpu.HBM)
    size = sum(a.size * a.dtype.itemsize for a in operands)
    size += sum(o.size * o.dtype.itemsize for o in outputs)
    return pl.pallas_call(
        body,
        out_shape=outputs,
        in_specs=[hbm if i in in_hbm else vmem for i in range(len(operands))],
        out_specs=[vmem] * len(outputs),
        scratch_shapes=list(scratch),
        cost_estimate=pl.CostEstimate(flops=flops, bytes_accessed=size, transcendentals=0),
        compiler_params=pltpu.CompilerParams(vmem_limit_bytes=room),
    )(*operands)


def exchange(value, axes, distance):
    members = lax.axis_size(axes)
    return lax.ppermute(value, axes, [(i, i ^ distance) for i in range(members)])


def start_kernel(token_ref):
    token_ref[...] = jnp.zeros_like(token_ref)


def send_kernel(
    sizes, rows_ref, pair_ref, gain_ref, weight_ref, input_ref, gate_ref, tri_gain_ref, output_ref, up_ref,
    down_ref, token_ref, same_ref, other_ref, shared_ref, wide,
):
    sequences, local_rows, residues, chan_local, outer_width = sizes
    part = sequences // 4
    part_rows = part * local_rows
    pair = widened(pair_ref[...])
    flat_pair = rounded(jnp.concatenate([pair[:, i, :] for i in range(local_rows)], axis=1))
    shared_ref[0:chan_local, :] = flat_pair
    at = chan_local + sequences
    narrow = gate_ref.shape[1]
    scaled = rounded(widened(output_ref[...]) * as_column(tri_gain_ref[...]))
    kinds = [input_ref[kind] for kind in range(input_ref.shape[0])]
    down = down_ref[...]
    for block in (*kinds, gate_ref[...], scaled, down[:chan_local]):
        shared_ref[at : at + chan_local, :narrow] = block
        at += chan_local
    at = chan_local + sequences
    for block in (up_ref[...], down[chan_local:]):
        shared_ref[at : at + block.shape[0], narrow:] = block
        at += block.shape[0]
    same_ref[part_rows : part_rows + chan_local, :] = flat_pair
    other_ref[part_rows : part_rows + chan_local, :] = flat_pair
    unit_here = 2 * lax.axis_index("branch") + lax.rem(lax.axis_index("row"), 2)
    unit_other = 2 * lax.axis_index("branch") + 1 - lax.rem(lax.axis_index("row"), 2)
    same_ref[0:part_rows, :] = rows_ref[pl.ds(unit_here * part_rows, part_rows), :]
    other_ref[0:part_rows, :] = rows_ref[pl.ds(unit_other * part_rows, part_rows), :]
    normed = rounded(layer_normalize(widened(rows_ref[...]), 1) * gain_ref[...])
    wide[:, 0 : 2 * outer_width] = product(normed, weight_ref[...], 1, 1)
    base = part_rows + chan_local
    for i in range(local_rows):
        both = rounded(wide[pl.ds(i, sequences, stride=local_rows), :])
        lanes = slice(i * outer_width, (i + 1) * outer_width)
        shared_ref[chan_local : chan_local + sequences, lanes] = both[:, :outer_width]
        same_ref[base : base + sequences, lanes] = both[:, outer_width : 2 * outer_width]
    other_ref[base : base + sequences, :] = same_ref[base : base + sequences, :]


def pack_kernel(chan_local, own_ref, other_ref, pair_ref, rest_ref):
    rest = own_ref.shape[0] - chan_local
    for k, ref in enumerate((own_ref, other_ref)):
        pair_ref[k * chan_local : (k + 1) * chan_local, :] = ref[:chan_local, :]
        rest_ref[k * rest : (k + 1) * rest, :] = ref[chan_local:, :]


def keep_kernel(*refs):
    count = len(refs) // 2
    for source, target in zip(refs[:count], refs[count:]):
        target[...] = source[...]


def arrive_kernel(*refs):
    refs[-1][...] = jnp.zeros_like(refs[-1])


def relay_kernel(sizes, own_ref, one_ref, two_ref, three_ref, after_bias_ref, after_keep_ref, relay_ref):
    sequences, local_rows, residues, chan_local, outer_width = sizes
    part_rows = sequences // 4 * local_rows
    row = lax.axis_index("row")
    branch = lax.axis_index("branch")
    base = part_rows + chan_local
    for distance, ref in enumerate((own_ref, one_ref, two_ref, three_ref)):
        shard = row ^ distance

        @pl.when(shard // 2 == branch)
        def _():
            place = lax.rem(shard, 2)
            relay_ref[pl.ds(pl.multiple_of(place * chan_local, chan_local), chan_local), :] = ref[
                part_rows:base, :
            ]
            start = 2 * chan_local + place * sequences
            relay_ref[pl.ds(pl.multiple_of(start, chan_local), sequences), :] = ref[
                base : base + sequences, :
            ]


def score_kernel(
    sizes, own_ref, one_ref, two_ref, three_ref, gain_ref, weight_ref, *refs,
):
    score_ref, values_ref, gate_ref, module = refs[-4:]
    sequences, local_rows, residues, chan_local, outer_width = sizes
    part = sequences // 4
    part_rows = part * local_rows
    width = gain_ref.shape[1]
    row = lax.axis_index("row")
    for distance, ref in enumerate((own_ref, one_ref, two_ref, three_ref)):
        shard = row ^ distance
        block = widened(ref[0:part_rows, :])
        unit = layer_normalize(block, 1) * gain_ref[...]
        module[:, pl.ds(pl.multiple_of(shard * local_rows, local_rows), local_rows), :] = unit.reshape(
            part, local_rows, width
        )
    normed = rounded(module[...].reshape(part * residues, width))
    half = residues // 2
    here = module[:, pl.ds(pl.multiple_of(row // 2 * half, half), half), :]
    query_rows = rounded(here.reshape(part * half, width))
    heads = values_ref.shape[1]
    groups = score_ref.shape[1] // half
    head_size = heads // groups
    query = rounded(product(query_rows, weight_ref[:, 0:heads]) * head_size ** (-0.5))
    both = rounded(product(normed, weight_ref[:, heads : 3 * heads]))
    keys = both[:, :heads]
    values_ref[...] = both[:, heads:]
    gate_ref[...] = rounded(jax.nn.sigmoid(product(query_rows, weight_ref[:, 3 * heads :])))
    mask = head_mask(groups, half, head_size)
    for s in range(part):
        one = query[s * half : (s + 1) * half]
        spread = jnp.where(mask, jnp.concatenate([one] * groups, axis=0), jnp.bfloat16(0))
        score_ref[s * residues : (s + 1) * residues, :] = product(
            keys[s * residues : (s + 1) * residues], spread, 1, 1
        )


def bias_kernel(chan_local, local_rows, pair_refs, matrix_ref, bias_ref, full):
    groups = matrix_ref.shape[0]
    residues = bias_ref.shape[0]
    seq = lax.axis_index("seq")
    for distance, ref in zip((0, 2, 1, 3), pair_refs):
        place = pl.ds(pl.multiple_of((seq ^ distance) * chan_local, chan_local), chan_local)
        full[place, :] = widened(ref[0:chan_local, :])
    plain = rounded(layer_normalize(full[...], 0))
    bias = rounded(product(matrix_ref[...], plain).T)
    lanes = bias_ref.shape[1]
    half = lanes // groups
    head = lax.broadcasted_iota(jnp.int32, (groups, lanes), 0)
    lane = lax.broadcasted_iota(jnp.int32, (groups, lanes), 1)
    first = lax.rem(lax.axis_index("row"), 2) * local_rows
    total = jnp.zeros(bias_ref.shape, jnp.float32)
    for i in range(local_rows):
        pick = jnp.where(lane == head * half + first + i, jnp.bfloat16(1), jnp.bfloat16(0))
        total += product(bias[i * residues : (i + 1) * residues, :], pick)
    bias_ref[...] = rounded(total)


def mix_kernel(
    sizes, near_bias_ref, far_bias_ref, score_ref, values_ref, gate_ref, mixing_ref, own_ref, one_ref, *refs,
):
    near_here_ref, near_there_ref, far_here_ref, far_there_ref, module = refs[-5:]
    sequences, local_rows, residues, chan_local, outer_width = sizes
    part = sequences // 4
    part_rows = part * local_rows
    half = residues // 2
    heads = values_ref.shape[1]
    groups = score_ref.shape[1] // half
    head_size = heads // groups
    row = lax.axis_index("row")
    branch = lax.axis_index("branch")
    bias = widened(near_bias_ref[...]) + widened(far_bias_ref[...])
    scores = score_ref[...].reshape(part, residues, groups * half) + bias[None]
    weights = jnp.exp(scores - jnp.max(scores, axis=1, keepdims=True))
    weights = rounded(weights * (1.0 / jnp.sum(weights, axis=1, keepdims=True)))
    mask = head_mask(groups, half, head_size)
    attended = []
    for s in range(part):
        every = product(weights[s], values_ref[s * residues : (s + 1) * residues, :], 0, 0)
        every = jnp.where(mask, every, 0.0).reshape(groups, half, heads)
        attended.append(jnp.sum(every, axis=0))
    mixed = rounded(widened(gate_ref[...]) * jnp.concatenate(attended, axis=0))
    projected = product(mixed, mixing_ref[...])
    width = projected.shape[1]
    module[...] = projected.reshape(part, half, width)
    halved = width // 2
    for distance, ref, here, there in (
        (0, own_ref, near_here_ref, near_there_ref),
        (1, one_ref, far_here_ref, far_there_ref),
    ):
        place = lax.rem(row, 2) ^ distance
        update = module[:, pl.ds(pl.multiple_of(place * local_rows, local_rows), local_rows), :]
        result = rounded(widened(ref[0:part_rows, :]) + update.reshape(part_rows, width))
        low, high = result[:, :halved], result[:, halved:]
        here[...] = jnp.where(branch == 0, low, high)
        there[...] = jnp.where(branch == 0, high, low)


def place_kernel(own_ref, branch_ref, row_ref, both_ref, pair_ref, token_ref, output_ref, pair_output_ref):
    pair_output_ref[...] = pair_ref[...]
    rows = own_ref.shape[0]
    branch = lax.axis_index("branch")
    parity = lax.rem(lax.axis_index("row"), 2)
    for flip_branch, flip_row, ref in (
        (0, 0, own_ref),
        (1, 0, branch_ref),
        (0, 1, row_ref),
        (1, 1, both_ref),
    ):
        unit = 2 * (branch ^ flip_branch) + (parity ^ flip_row)
        output_ref[pl.ds(pl.multiple_of(unit * rows, rows), rows), :] = ref[...]


def pair_kernel(
    sizes, row_refs, rest_refs, pair_refs, gain_ref, transition_gain_ref, outer_weight_ref, seq_total, hidden_local,
    output_ref, rows, columns, gates, outer, outer_flat, ordered, final,
):
    sequences, local_rows, residues, chan_local, outer_width = sizes
    half = residues // 2
    branch = lax.axis_index("branch")
    seq = lax.axis_index("seq")
    width = 4 * chan_local
    chan = chan_local
    gain = as_column(gain_ref[...])
    weight_refs = [ref.at[sequences:, 0:width] for ref in rest_refs]
    hidden_refs = [ref.at[sequences:, width:] for ref in rest_refs]
    for distance, row_ref, pair_ref, weight_ref in zip((0, 2, 1, 3), row_refs, pair_refs, weight_refs):
        place = pl.ds(pl.multiple_of((seq ^ distance) * chan, chan), chan)
        rows[place, :] = row_ref[0:chan, :]
        for k in range(2):
            columns[k, place, :] = pair_ref[k * chan : (k + 1) * chan, :]
        gates[place, :] = weight_ref[4 * chan : 5 * chan, :]

    def projection(values, kind):
        weights = jnp.concatenate([w[kind * chan : (kind + 1) * chan, :] for w in weight_refs], axis=0)
        return product(values, weights, 1, 1)

    raw = widened(rows[...])
    row_input = rounded((layer_normalize(raw, 0) * gain).T)
    left = widened(
        rounded(projection(row_input, 0) * jax.nn.sigmoid(projection(row_input, 1)))
    ).reshape(local_rows, residues, width)
    right = []
    for k in range(2):
        column_input = rounded((layer_normalize(widened(columns[k]), 0) * gain).T)
        right.append(
            widened(
                rounded(projection(column_input, 2) * jax.nn.sigmoid(projection(column_input, 3)))
            ).reshape(local_rows, residues, width)
        )
    right = jnp.concatenate(right, axis=0)
    triangle = jnp.concatenate(
        [jnp.sum(left[i][None] * right, axis=1) for i in range(local_rows)], axis=0
    )
    triangle = widened(rounded(triangle))
    tri_norm = rounded(layer_normalize(triangle, 1))
    output_weight = jnp.concatenate([w[5 * chan : 6 * chan, :] for w in weight_refs], axis=0)
    tri_out = product(tri_norm, output_weight)
    ordered[...] = raw.T.reshape(local_rows, residues, width)
    place = pl.ds(pl.multiple_of(branch * half, half), half)
    raw_here = ordered[:, place, :].reshape(local_rows * half, width)
    ordered[...] = widened(row_input).reshape(local_rows, residues, width)
    input_here = rounded(ordered[:, place, :].reshape(local_rows * half, width))
    gate = jax.nn.sigmoid(product(input_here, gates[...], 1, 1))
    first_update = widened(rounded(raw_here + gate * tri_out))
    trans_norm = rounded(layer_normalize(first_update, 1) * transition_gain_ref[...])
    down = jnp.zeros((local_rows * half, width), jnp.float32)
    for w, h in zip(weight_refs, hidden_refs):
        hidden = rounded(jax.nn.relu(product(trans_norm, h[0:hidden_local, :], 1, 1)))
        down_weight = jnp.concatenate([w[6 * chan : 7 * chan, :], h[hidden_local : hidden_local + 3 * chan, :]], axis=0)
        down += product(hidden, down_weight, 1, 1)
    pair_next = widened(rounded(first_update + down))

    lefts = jnp.concatenate([ref[:sequences, :] for ref in rest_refs], axis=0)
    base = 2 * chan
    rights = jnp.concatenate(
        [
            jnp.concatenate([p[base : base + sequences, :], p[base + sequences :, :]], axis=1)
            for p in pair_refs
        ],
        axis=0,
    )
    outer_all = product(rounded(widened(lefts).T), rights)
    each = 128 // outer_width
    for tile in range(half // each):
        outer[tile] = outer_all[:, tile * 128 : (tile + 1) * 128]
        for c in range(outer_width):
            strip = outer[tile, pl.ds(c, local_rows, stride=outer_width), :]
            for k in range(each):
                j = tile * each + k
                outer_flat[
                    j * local_rows : (j + 1) * local_rows, c * outer_width : (c + 1) * outer_width
                ] = strip[:, k * outer_width : (k + 1) * outer_width]
    final[...] = product(rounded(outer_flat[...]), outer_weight_ref[...]) * (1.0 / seq_total)
    outer_update = jnp.concatenate(
        [final[pl.ds(i, half, stride=local_rows), :] for i in range(local_rows)], axis=0
    )
    outer_update = widened(rounded(outer_update))
    result = pair_next + outer_update
    own = result[:, 0:chan]
    for k in range(1, 4):
        own = jnp.where(seq == k, result[:, k * chan : (k + 1) * chan], own)
    output_ref[...] = rounded(own)


def compact_shards(
    alignment_input, pairwise_input, alignment_gain, product_gain, attention_weight, mixing_weight,
    outer_input_weight, outer_output_weight, bias_matrix, pairwise_gain, triangle_input_weight,
    triangle_gate_weight, triangle_gain, triangle_output_weight, transition_gain,
    transition_up_weight, transition_down_weight,
):
    sequences, local_rows, width = alignment_input.shape
    chan_local, _, residues = pairwise_input.shape
    pair_width, groups = bias_matrix.shape
    heads = mixing_weight.shape[0]
    outer_width = outer_input_weight.shape[2]
    part = sequences // 4
    part_rows = part * local_rows
    half = residues // 2
    sizes = (sequences, local_rows, residues, chan_local, outer_width)
    half_type, full_type = jnp.bfloat16, jnp.float32

    def shape(*dims, dtype=half_type):
        return jax.ShapeDtypeStruct(dims, dtype)

    rows_flat = alignment_input.reshape(sequences * local_rows, width)
    message_rows = part_rows + chan_local + sequences
    outer_weight_flat = outer_input_weight.transpose(1, 2, 0).reshape(2 * outer_width, width)
    (token,) = kernel_call(start_kernel, [shape(8, 128, dtype=full_type)], [], flops=5 * 10**9)
    hidden_local = transition_up_weight.shape[0]
    shared_rows = chan_local + sequences + 7 * chan_local
    same, other, shared = kernel_call(
        functools.partial(send_kernel, sizes),
        [shape(message_rows, width), shape(message_rows, width),
         shape(shared_rows, width)],
        [rows_flat, pairwise_input, product_gain[None], outer_weight_flat, triangle_input_weight,
         triangle_gate_weight, triangle_gain[None], triangle_output_weight.T, transition_up_weight,
         transition_down_weight, token],
        [pltpu.VMEM((sequences * local_rows, 128), full_type)],
    )
    shared_x = exchange(shared, "seq", 2)
    pair_two, rest_two = kernel_call(
        functools.partial(pack_kernel, chan_local),
        [shape(2 * chan_local, width), shape(2 * (shared_rows - chan_local), width)],
        [shared, shared_x],
    )
    pair_core = exchange(pair_two, "seq", 1)
    rest_core = exchange(rest_two, "seq", 1)
    from_three = exchange(other, "row", 3)
    from_two = exchange(same, "row", 2)
    from_one = exchange(other, "row", 1)
    received = (same, from_one, from_two, from_three)

    late_weight = lax.optimization_barrier((attention_weight, shared))[0]
    kept = [late_weight.reshape(width, 4 * heads), mixing_weight,
            outer_output_weight.reshape(outer_width * outer_width, pair_width),
            alignment_gain[None], pairwise_gain[None], transition_gain[None]]
    attention_kept, mixing_kept, outer_kept, row_gain, pair_gain, last_gain = kernel_call(
        keep_kernel, [shape(*a.shape, dtype=a.dtype) for a in kept], kept
    )

    def bias_body(*refs):
        bias_kernel(chan_local, local_rows, (refs[0], refs[1], refs[2].at[:chan_local], refs[2].at[chan_local:]), *refs[3:])

    (near_bias,) = kernel_call(
        bias_body,
        [shape(residues, groups * half)],
        [shared, shared_x, pair_core, bias_matrix.T],
        [
            pltpu.VMEM((pair_width, local_rows * residues), full_type),
        ],
        flops=BIAS_COST,
    )
    far_bias = exchange(near_bias, "row", 1)

    (relay,) = kernel_call(
        functools.partial(relay_kernel, sizes),
        [shape(2 * chan_local + 2 * sequences, width)],
        [*received, far_bias, row_gain],
    )
    relay_x = exchange(relay, "seq", 2)
    relay_core = exchange(relay, "seq", 1)
    relay_both = exchange(relay, "seq", 3)
    relays = (relay, relay_x, relay_core, relay_both)

    scores, values, gate = kernel_call(
        functools.partial(score_kernel, sizes),
        [shape(part * residues, groups * half, dtype=full_type), shape(part * residues, heads), shape(part * half, heads)],
        [*received, row_gain, attention_kept, relay],
        [pltpu.VMEM((part, residues, width), full_type)],
        flops=3 * 10**9,
    )

    near_here, near_there, far_here, far_there = kernel_call(
        functools.partial(mix_kernel, sizes),
        [shape(part_rows, width // 2)] * 4,
        [near_bias, far_bias, scores, values, gate, mixing_kept, same, from_one, rest_core, relay_core],
        [pltpu.VMEM((part, half, width), full_type)],
        flops=3 * 10**9,
    )
    axes = ("branch", "row")
    across = lax.axis_size("row")
    from_branch = exchange(near_there, axes, across)
    from_both = exchange(far_there, axes, across + 1)
    from_row = exchange(far_here, axes, 1)

    def pair_body(*refs):
        own, other, pair, rest = refs[:4]
        count = rest.shape[0] // 2
        row_refs = (own, other, pair.at[:chan_local], pair.at[chan_local:])
        rest_refs = (own.at[chan_local:], other.at[chan_local:], rest.at[:count], rest.at[count:])
        pair_kernel(sizes, row_refs, rest_refs, refs[4:8], *refs[8:11], sequences * 4, hidden_local, *refs[11:])

    (pair_done,) = kernel_call(
        pair_body,
        [shape(local_rows * half, chan_local)],
        [shared, shared_x, pair_core, rest_core, *relays, pair_gain, last_gain, outer_kept],
        [
            pltpu.VMEM((pair_width, local_rows * residues), half_type),
            pltpu.VMEM((2, pair_width, local_rows * residues), half_type),
            pltpu.VMEM((pair_width, pair_width), half_type),
            pltpu.VMEM((half * outer_width // 128, local_rows * outer_width, 128), full_type),
            pltpu.VMEM((local_rows * half, outer_width * outer_width), full_type),
            pltpu.VMEM((local_rows, residues, pair_width), full_type),
            pltpu.VMEM((local_rows * half, pair_width), full_type),
        ],
    )
    (arrived,) = kernel_call(arrive_kernel, [shape(8, 128, dtype=full_type)], [from_row])
    alignment_flat, pairwise_output = kernel_call(
        place_kernel,
        [shape(sequences * local_rows, width // 2), shape(local_rows * half, chan_local)],
        [near_here, from_branch, from_row, from_both, pair_done, arrived],
    )
    return (
        alignment_flat.reshape(sequences, local_rows, width // 2),
        pairwise_output.reshape(local_rows, half, chan_local).transpose(2, 0, 1),
    )


def is_compact(mesh):
    return (mesh.shape["branch"], mesh.shape["row"], mesh.shape["seq"]) == (2, 4, 4)


def solution(mesh):
    return jax.shard_map(
        compact_shards if is_compact(mesh) else shards,
        mesh=mesh,
        in_specs=(
            P("seq", "row", None),
            P("seq", "row", None),
            P(),
            P(),
            P(),
            P(),
            P(),
            P(),
            P(),
            P(),
            P(None, "seq", None),
            P("seq", None),
            P("seq"),
            P(None, "seq"),
            P(),
            P("seq", None),
            P(None, "seq"),
        ),
        out_specs=(P("seq", "row", "branch"), P("seq", "row", "branch")),
        check_vma=False,
    )
```
